32 devices in a mesh: inst: 16 (over z, y, core), tp: 2 (over x).
Axes of the slice: x: 2, y: 2, z: 4, core: 2. Of those that a mesh axis runs over, the one named last changes fastest.
Arguments:
- tokens_in: bfloat16 [4096, 8192], P('inst', 'tp'), may hold values from -32 to 32
- w_query: bfloat16 [8192, 4096], P('inst', 'tp'), may hold values from -1 to 1
- w_key: bfloat16 [8192, 1024], P('inst', 'tp'), may hold values from -1 to 1
- w_value: bfloat16 [8192, 1024], P('inst', 'tp'), may hold values from -0.0625 to 0.0625
- stored_key_cache: bfloat16 [28672, 1024], P('inst', 'tp'), may hold values from -6 to 6
- stored_value_cache: bfloat16 [28672, 1024], P('inst', 'tp'), may hold values from -6 to 6
- prompt_len: int32 [16], P('inst'), may hold values from 64 to 256
Outputs:
- attended: bfloat16 [4096, 4096], P('inst', 'tp')
- handoff: bfloat16 [16, 4096], P(None, 'tp')
The draws below stay inside these ranges and needn't reach their ends.
All inputs are finite; a program needn't handle non-finite values.
Results may differ from the reference program's by a relative error of at most 0.011.
Values may be sent and summed in bfloat16 or wider, within the bound.
No kernel may reach another device: no remote copies, remote signals or barrier semaphores. Data moves between devices by JAX's collectives and lax.ppermute only.
A program may use at most 128 MiB of HBM per device.

```python
import jax
import jax.numpy as jnp
from jax import lax

MODEL_WIDTH = 8192
KEY_VALUE_HEADS = 8
HEAD_SIZE = 128
QUERY_PER_GROUP = 4
TOKEN_COUNT = 256
PREFIX_LENGTH = 1792
ROWS = 4096
CACHED = 28672
QCOLS = 4096
KEY_COLUMNS = 1024
N_INST = 16


def shared_query(key):
    return jnp.clip(jax.random.normal(key, (MODEL_WIDTH, QCOLS), jnp.float32), -6.0, 6.0)


def draw_tokens_in(key, part):
    key = jax.random.fold_in(key, 11)
    noise_key = jax.random.fold_in(key, 0)
    result = jnp.clip(jax.random.normal(noise_key, (ROWS, MODEL_WIDTH), jnp.float32), -6.0, 6.0)
    return result.astype(jnp.bfloat16)


def draw_w_query(key, part):
    base_offset = shared_query(key)
    return (base_offset * MODEL_WIDTH ** (-0.5)).astype(jnp.bfloat16)


def draw_w_key(key, part):
    key = jax.random.fold_in(key, 13)
    result = jnp.clip(jax.random.normal(key, (MODEL_WIDTH, KEY_COLUMNS), jnp.float32), -6.0, 6.0)
    return (result * MODEL_WIDTH ** (-0.5)).astype(jnp.bfloat16)


def set_ends(values, key, least, largest):
    dims = values.shape
    place = [jax.random.randint(jax.random.fold_in(key, axis), (), 0, dims[axis]) for axis in range(len(dims))]
    values = values.at[tuple(place)].set(least)
    longest = dims.index(max(dims))
    place[longest] = (place[longest] + 1) % dims[longest]
    return values.at[tuple(place)].set(largest)


def steps_of(rng, extent, pieces, smallest, high):
    gain, own = 1.0, jax.random.fold_in(rng, 6)
    for position, blocks in pieces:
        draws = jnp.exp(jax.random.uniform(jax.random.fold_in(own, position), (blocks,), jnp.float32, smallest / len(pieces), high / len(pieces)))
        gain = gain * jnp.repeat(draws, extent[position] // blocks).reshape([-1 if axis == position else 1 for axis in range(len(extent))])
    return gain


def normal_values(own_key, shape, spread, reach, cuts=(), kind=jnp.bfloat16):
    level = steps_of(own_key, shape, cuts, -0.22, 0.18) if cuts else 1.0
    array = jax.random.normal(own_key, shape, jnp.float32) * spread * level
    return jnp.minimum(jnp.maximum(array, -reach), reach).astype(kind)


def setup_inputs(seed: int = 0) -> dict:
    key_of = jax.random.split(jax.random.key(seed), 8)
    tokens_in = draw_tokens_in(jax.random.fold_in(key_of[7], 71), 0)
    w_query = draw_w_query(jax.random.fold_in(key_of[7], 71), 0)
    w_key = draw_w_key(jax.random.fold_in(key_of[7], 71), 0)
    w_value = normal_values(key_of[3], (MODEL_WIDTH, KEY_COLUMNS), MODEL_WIDTH ** -0.5, 0.0625, ((0, 16), (1, 2)))
    stored_key_cache = normal_values(key_of[4], (CACHED, KEY_COLUMNS), 1.0, 6.0, ((0, 16), (1, 2)))
    stored_value_cache = normal_values(key_of[5], (CACHED, KEY_COLUMNS), 1.0, 6.0, ((0, 16), (1, 2)))
    prompt_len = set_ends(jax.random.randint(key_of[6], (N_INST,), TOKEN_COUNT // 4, TOKEN_COUNT + 1), jax.random.fold_in(key_of[6], 1), TOKEN_COUNT // 4, TOKEN_COUNT).astype(jnp.int32)
    return dict(tokens_in=tokens_in, w_query=w_query, w_key=w_key, w_value=w_value, stored_key_cache=stored_key_cache, stored_value_cache=stored_value_cache, prompt_len=prompt_len)


def reference(tokens_in, w_query, w_key, w_value, stored_key_cache, stored_value_cache, prompt_len):
    query_matrix = jnp.dot(tokens_in, w_query, preferred_element_type=jnp.float32).astype(jnp.bfloat16)
    key_matrix = jnp.dot(tokens_in, w_key, preferred_element_type=jnp.float32).astype(jnp.bfloat16)
    value_matrix = jnp.dot(tokens_in, w_value, preferred_element_type=jnp.float32).astype(jnp.bfloat16)
    query_matrix = query_matrix.reshape(N_INST, TOKEN_COUNT, KEY_VALUE_HEADS, QUERY_PER_GROUP, HEAD_SIZE)
    key_matrix = key_matrix.reshape(N_INST, TOKEN_COUNT, KEY_VALUE_HEADS, HEAD_SIZE)
    value_matrix = value_matrix.reshape(N_INST, TOKEN_COUNT, KEY_VALUE_HEADS, HEAD_SIZE)
    cached_key_rows = stored_key_cache.reshape(N_INST, PREFIX_LENGTH, KEY_VALUE_HEADS, HEAD_SIZE)
    cached_value_rows = stored_value_cache.reshape(N_INST, PREFIX_LENGTH, KEY_VALUE_HEADS, HEAD_SIZE)
    positions = jnp.arange(TOKEN_COUNT, dtype=jnp.int32)
    key_pos = jnp.arange(PREFIX_LENGTH + TOKEN_COUNT, dtype=jnp.int32) - PREFIX_LENGTH

    def one(item):
        qpart, kpart, vpart, ckpart, cvpart, length = item
        key_all = jnp.concatenate([ckpart, kpart], axis=0)
        value_all = jnp.concatenate([cvpart, vpart], axis=0)
        scores = jnp.einsum('tgjd,sgd->gjts', qpart.astype(jnp.float32), key_all.astype(jnp.float32)) / jnp.sqrt(jnp.float32(HEAD_SIZE))
        allowed = (key_pos[None, :] <= positions[:, None]) & (key_pos[None, :] < length)
        scores = jnp.where(allowed[None, None], scores, -jnp.inf)
        probs = jax.nn.softmax(scores, axis=-1).astype(jnp.bfloat16)
        attention_output = jnp.einsum('gjts,sgd->tgjd', probs.astype(jnp.float32), value_all.astype(jnp.float32))
        return attention_output.astype(jnp.bfloat16).reshape(TOKEN_COUNT, KEY_VALUE_HEADS * QUERY_PER_GROUP * HEAD_SIZE)
    attended = lax.map(one, (query_matrix, key_matrix, value_matrix, cached_key_rows, cached_value_rows, prompt_len))
    handoff = attended[jnp.arange(N_INST), prompt_len - 1]
    return (attended.reshape(N_INST * TOKEN_COUNT, KEY_VALUE_HEADS * QUERY_PER_GROUP * HEAD_SIZE), handoff)
```

```python
import functools

import jax
import jax.numpy as jnp
from jax import lax
from jax.experimental import pallas as pl
from jax.experimental.pallas import tpu as pltpu
from jax.sharding import PartitionSpec as P

HEAD_SIZE = 128
QUERY_PER_GROUP = 4
INNER = 4


def dot(a, b):
    return jnp.dot(a, b, preferred_element_type=jnp.float32)


def attention_kernel(len_ref, q_ref, kc_ref, vc_ref, kb_ref, vb_ref, prev_ref, o_ref):
    del prev_ref
    length = len_ref[0]
    rows = q_ref.shape[0]
    block = kb_ref.shape[0]
    factor = 1.4426950408889634 / HEAD_SIZE**0.5
    row = lax.broadcasted_iota(jnp.int32, (rows, block), 0)
    col = lax.broadcasted_iota(jnp.int32, (rows, block), 1)
    allowed = (col <= row) & (col < length)
    contract = (((1,), (1,)), ((), ()))
    for member in range(QUERY_PER_GROUP):
        cols = slice(member * HEAD_SIZE, (member + 1) * HEAD_SIZE)
        q = q_ref[:, cols]
        s1 = lax.dot_general(q, kc_ref[...], contract, preferred_element_type=jnp.float32)
        s2 = lax.dot_general(q, kb_ref[...], contract, preferred_element_type=jnp.float32)
        s2 = jnp.where(allowed, s2, -jnp.inf)
        top = jnp.maximum(
            jnp.max(s1, axis=1, keepdims=True), jnp.max(s2, axis=1, keepdims=True)
        )
        p1 = jnp.exp2((s1 - top) * factor)
        p2 = jnp.exp2((s2 - top) * factor)
        total = jnp.sum(p1, axis=1, keepdims=True) + jnp.sum(p2, axis=1, keepdims=True)
        out = dot(p1.astype(jnp.bfloat16), vc_ref[...]) + dot(p2.astype(jnp.bfloat16), vb_ref[...])
        o_ref[:, cols] = (out / total).astype(o_ref.dtype)


def attend(length, q, k_cache, v_cache, k_block, v_block, group, buffer):
    rows = q.shape[0]
    wide = QUERY_PER_GROUP * HEAD_SIZE
    cached = k_cache.shape[0]
    column = lambda i: (0, group)
    return pl.pallas_call(
        attention_kernel,
        grid=(1,),
        out_shape=jax.ShapeDtypeStruct(buffer.shape, buffer.dtype),
        in_specs=[
            pl.BlockSpec(memory_space=pltpu.SMEM),
            pl.BlockSpec((rows, wide), lambda i: (0, 0)),
            pl.BlockSpec((cached, HEAD_SIZE), column),
            pl.BlockSpec((cached, HEAD_SIZE), column),
            pl.BlockSpec((rows, HEAD_SIZE), column),
            pl.BlockSpec((rows, HEAD_SIZE), column),
            pl.BlockSpec(memory_space=pl.ANY),
        ],
        out_specs=pl.BlockSpec((rows, wide), column),
        input_output_aliases={6: 0},
        compiler_params=pltpu.CompilerParams(vmem_limit_bytes=40 * 1024 * 1024),
        cost_estimate=pl.CostEstimate(
            flops=4 * rows * wide * (cached + rows),
            bytes_accessed=4 * (cached + rows) * HEAD_SIZE + 4 * rows * wide,
            transcendentals=rows * QUERY_PER_GROUP * (cached + rows),
        ),
        name="attention",
    )(length, q, k_cache, v_cache, k_block, v_block, buffer)


def shards(tokens_in, w_query, w_key, w_value, stored_key_cache, stored_value_cache, prompt_len):
    n_inst, n_tp = lax.axis_size("inst"), lax.axis_size("tp")
    outer = n_inst // INNER
    me = lax.axis_index("inst")
    z, w = me // INNER, me % INNER
    x = lax.axis_index("tp")
    rows, local = tokens_in.shape
    part = local // outer
    groups = [list(range(o * INNER, (o + 1) * INNER)) for o in range(outer)]

    def over_outer(value, bits):
        return lax.ppermute(value, "inst", [(i, i ^ (bits * INNER)) for i in range(n_inst)])

    w_kv = jnp.concatenate([w_key, w_value], axis=1)
    kv_all = lax.all_gather(w_kv, "inst", axis=0, tiled=True, axis_index_groups=groups)
    q_all = lax.all_gather(w_query, "inst", axis=0, tiled=True, axis_index_groups=groups)

    own = tokens_in.reshape(rows, outer // n_tp, n_tp, part)
    if n_tp == 2:
        mine = lax.dynamic_index_in_dim(own, x, 2, keepdims=False)
        swap = lax.ppermute(
            lax.dynamic_index_in_dim(own, 1 - x, 2, keepdims=False), "tp", [(0, 1), (1, 0)]
        )
        parts = jnp.where(
            x == 0,
            jnp.concatenate([mine, swap], axis=1),
            jnp.concatenate([swap, mine], axis=1),
        )
    else:
        parts = lax.all_to_all(own, "tp", 2, 1, tiled=True).reshape(rows, outer, part)
    got = {}
    order = [b for b in range(outer) if b % 2] + [b for b in range(outer) if b % 2 == 0]
    for bits in order:
        mine = lax.dynamic_index_in_dim(parts, z ^ bits, 1, keepdims=False)
        got[bits] = over_outer(mine, bits) if bits else mine
    odd = [b for b in range(outer) if b % 2]
    even = [b for b in range(outer) if b % 2 == 0]

    def whole(list_of_bits):
        stack = jnp.concatenate([got[b] for b in list_of_bits], axis=0)
        if n_tp == 2:
            other = lax.ppermute(stack, "tp", [(0, 1), (1, 0)])
            first = jnp.where(x == 0, stack, other)
            second = jnp.where(x == 0, other, stack)
            return jnp.concatenate([first, second], axis=1)
        return lax.all_gather(stack, "tp", axis=1, tiled=True)

    t_odd = whole(odd)
    t_even = whole(even)

    def reduced(weight):
        cols = weight.shape[1]
        send = dot(t_odd, weight).astype(jnp.bfloat16)
        keep = dot(t_even, weight)
        keep = keep + over_outer(send, 1).astype(jnp.float32)
        bits, count = 2, outer // 2
        while count > 1:
            pairs = keep.reshape(count // 2, 2, rows, cols)
            send = pairs[:, 1].astype(jnp.bfloat16)
            keep = pairs[:, 0] + over_outer(send, bits).astype(jnp.float32)
            bits, count = bits * 2, count // 2
        return keep.reshape(rows, cols).astype(jnp.bfloat16)

    kv = reduced(kv_all)
    half = w_key.shape[1]
    k_block, v_block = kv[:, :half], kv[:, half:]
    heads = half // HEAD_SIZE
    wide = QUERY_PER_GROUP * HEAD_SIZE
    attended = jnp.zeros((rows, heads * wide), jnp.bfloat16)
    for group in range(heads):
        q = reduced(q_all[:, group * wide : (group + 1) * wide])
        attended = attend(
            prompt_len, q, stored_key_cache, stored_value_cache, k_block, v_block, group, attended
        )
    last_row = lax.dynamic_slice_in_dim(attended, prompt_len[0] - 1, 1, 0)
    handoff = lax.all_gather(last_row, "inst", axis=0, tiled=True)
    return (attended, handoff)


def solution(mesh):
    return jax.shard_map(
        shards,
        mesh=mesh,
        in_specs=(
            P("inst", "tp"),
            P("inst", "tp"),
            P("inst", "tp"),
            P("inst", "tp"),
            P("inst", "tp"),
            P("inst", "tp"),
            P("inst"),
        ),
        out_specs=(P("inst", "tp"), P(None, "tp")),
        check_vma=False,
    )
```

```python
import functools

import jax
import jax.numpy as jnp
from jax import lax
from jax.experimental import pallas as pl
from jax.experimental.pallas import tpu as pltpu
from jax.sharding import PartitionSpec as P

HEAD_SIZE = 128
QUERY_PER_GROUP = 4
COST = 1 << 20
INNER = 4


def dot(a, b):
    return jnp.dot(a, b, preferred_element_type=jnp.float32)


def product(place_ref, t_refs, w_ref, t_whole):
    if len(t_refs) == 1:
        return dot(t_refs[0][...], w_ref[...])
    x = place_ref[0]
    part = t_refs[0].shape[1]
    n = len(t_refs) // 2

    @pl.when(pl.program_id(0) == 0)
    def _():
        for refs, where in ((t_refs[:n], x), (t_refs[n:], 1 - x)):
            cols = pl.ds(pl.multiple_of(where * part, part), part)
            row = 0
            for ref in refs:
                t_whole[row : row + ref.shape[0], cols] = ref[...]
                row += ref.shape[0]

    return dot(t_whole[...], w_ref[...])


def first_kernel(n_t, place_ref, *refs):
    out = product(place_ref, refs[:n_t], refs[n_t], refs[-1])
    row = 0
    for ref in refs[n_t + 1 : -1]:
        ref[...] = out[row : row + ref.shape[0]].astype(ref.dtype)
        row += ref.shape[0]


def later_kernel(n_t, place_ref, *refs):
    send_ref, keep_ref, t_whole = refs[-3:]
    out = product(place_ref, refs[:n_t], refs[n_t], t_whole)
    came = jnp.concatenate([ref[...] for ref in refs[n_t + 1 : -3]], axis=0)
    out = out + came.astype(jnp.float32)
    n = keep_ref.shape[0]
    keep_ref[...] = out[:n]
    send_ref[...] = out[n:].astype(send_ref.dtype)


def multiply(kernel, place, tokens, weight, came, outs, tile=512):
    columns = weight.shape[1]
    tile = min(tile, columns)
    column = lambda i, place: (0, i)
    some = lambda which: lambda i, place: (which, 0)
    held = len(tokens) // 2
    t_rows = sum(n for _, n, _ in tokens[: max(held, 1)])
    t_cols = tokens[0][0].shape[1] * (2 if held else 1)
    return pl.pallas_call(
        functools.partial(kernel, len(tokens)),
        grid_spec=pltpu.PrefetchScalarGridSpec(
            num_scalar_prefetch=1,
            grid=(columns // tile,),
            in_specs=[pl.BlockSpec((n, t.shape[1]), some(which)) for t, n, which in tokens]
            + [pl.BlockSpec((v.shape[0], tile), column) for v in (weight, *came)],
            out_specs=[pl.BlockSpec((n, tile), column) for n, _ in outs],
            scratch_shapes=[pltpu.VMEM((t_rows, t_cols), jnp.bfloat16)],
        ),
        out_shape=[jax.ShapeDtypeStruct((n, columns), dtype) for n, dtype in outs],
        compiler_params=pltpu.CompilerParams(vmem_limit_bytes=40 * 1024 * 1024),
        cost_estimate=pl.CostEstimate(flops=0, bytes_accessed=COST, transcendentals=0),
        name="product",
    )(place, *[t for t, _, _ in tokens], weight, *came)


def attention_kernel(
    place_ref, qm_ref, qc_ref, kc_ref, vc_ref, km_ref, kt_ref, vm_ref, vt_ref, *rest
):
    o_ref, last_ref = rest[-2:]
    length, here, first = place_ref[0], place_ref[1], place_ref[2]
    rows, block = qm_ref.shape[0], km_ref.shape[0]
    half = block // 2
    total = lambda mine, came: (mine + came.astype(jnp.float32)).astype(jnp.bfloat16)
    factor = 1.4426950408889634 / HEAD_SIZE**0.5
    row = lax.broadcasted_iota(jnp.int32, (rows, 1), 0)
    row = jnp.where(row < half, row + here * half, row - here * half)
    col = lax.broadcasted_iota(jnp.int32, (rows, block), 1)
    col = jnp.where(col < half, col + first * half, col - first * half)
    allowed = (col <= row) & (col < length)
    contract = (((1,), (1,)), ((), ()))
    at = row == length - 1
    keys = total(km_ref[...], kt_ref[...])
    values = total(vm_ref[...], vt_ref[...])
    for member in range(QUERY_PER_GROUP):
        cols = slice(member * HEAD_SIZE, (member + 1) * HEAD_SIZE)
        q = total(qm_ref[:, cols], qc_ref[:, cols])
        s1 = lax.dot_general(q, kc_ref[...], contract, preferred_element_type=jnp.float32)
        s2 = lax.dot_general(q, keys, contract, preferred_element_type=jnp.float32)
        s2 = jnp.where(allowed, s2, -jnp.inf)
        top = jnp.maximum(jnp.max(s1, axis=1, keepdims=True), jnp.max(s2, axis=1, keepdims=True))
        p1 = jnp.exp2((s1 - top) * factor)
        p2 = jnp.exp2((s2 - top) * factor)
        norm = jnp.sum(p1, axis=1, keepdims=True) + jnp.sum(p2, axis=1, keepdims=True)
        out = dot(p1.astype(jnp.bfloat16), vc_ref[...]) + dot(p2.astype(jnp.bfloat16), values)
        out = out / norm
        if rows == half:
            o_ref[:, cols] = out.astype(o_ref.dtype)
        else:
            for h, where in ((0, first), (1, 1 - first)):
                to = pl.ds(pl.multiple_of(where * half, half), half)
                o_ref[to, cols] = out[h * half : (h + 1) * half].astype(o_ref.dtype)
        last_ref[:, cols] = jnp.sum(jnp.where(at, out, 0.0), axis=0, keepdims=True).astype(
            last_ref.dtype
        )


def attend(place, q, k_cache, v_cache, kv, start, shape, buffer):
    rows, cols = q[0].shape
    wide = QUERY_PER_GROUP * HEAD_SIZE
    cached, block = k_cache.shape[0], kv[0].shape[0]
    heads = k_cache.shape[1] // HEAD_SIZE
    groups = cols // wide
    begin = start // wide
    column = lambda i, place: (0, begin + i)
    after = lambda i, place: (0, heads + begin + i)
    mine = lambda i, place: (0, i)
    out = column if rows == shape[0] else lambda i, place: (place[1], begin + i)
    buffers = [] if buffer is None else [buffer]
    return pl.pallas_call(
        attention_kernel,
        grid_spec=pltpu.PrefetchScalarGridSpec(
            num_scalar_prefetch=1,
            grid=(groups,),
            in_specs=[
                pl.BlockSpec((rows, wide), mine),
                pl.BlockSpec((rows, wide), mine),
                pl.BlockSpec((cached, HEAD_SIZE), column),
                pl.BlockSpec((cached, HEAD_SIZE), column),
                pl.BlockSpec((block, HEAD_SIZE), column),
                pl.BlockSpec((block, HEAD_SIZE), column),
                pl.BlockSpec((block, HEAD_SIZE), after),
                pl.BlockSpec((block, HEAD_SIZE), after),
            ]
            + [pl.BlockSpec(memory_space=pl.ANY)] * len(buffers),
            out_specs=[
                pl.BlockSpec((rows, wide), out),
                pl.BlockSpec((1, wide), mine),
            ],
        ),
        out_shape=[
            jax.ShapeDtypeStruct(shape, jnp.bfloat16),
            jax.ShapeDtypeStruct((1, cols), jnp.bfloat16),
        ],
        input_output_aliases={9: 0} if buffers else {},
        compiler_params=pltpu.CompilerParams(vmem_limit_bytes=40 * 1024 * 1024),
        cost_estimate=pl.CostEstimate(flops=0, bytes_accessed=COST, transcendentals=0),
        name="attention",
    )(place, *q, k_cache, v_cache, *kv, *kv, *buffers)


def shards(tokens_in, w_query, w_key, w_value, stored_key_cache, stored_value_cache, prompt_len):
    n_inst, n_tp = lax.axis_size("inst"), lax.axis_size("tp")
    outer = n_inst // INNER
    me = lax.axis_index("inst")
    z, w = me // INNER, me % INNER
    x = lax.axis_index("tp")
    rows, local = tokens_in.shape
    half = rows // 2
    part = local // outer
    groups = [list(range(o * INNER, (o + 1) * INNER)) for o in range(outer)]
    halves = (0, 1)
    count = outer // 2

    first = (prompt_len[0] - 1) // half

    def over_inst(value, bits):
        return lax.ppermute(value, "inst", [(i, i ^ bits) for i in range(n_inst)])

    def over_outer(value, bits):
        return over_inst(value, bits * INNER)

    def over_tp(value):
        return lax.ppermute(value, "tp", [(0, 1), (1, 0)])

    def swapped_if(flag, a, b, axis):
        return jnp.where(
            flag, jnp.concatenate([b, a], axis=axis), jnp.concatenate([a, b], axis=axis)
        )

    last_step = [None]

    def step(*values):
        if last_step[0] is not None:
            *values, _ = lax.optimization_barrier((*values, last_step[0]))
        last_step[0] = values[0]
        return values[0] if len(values) == 1 else values

    heads = w_key.shape[1] // HEAD_SIZE
    wide = QUERY_PER_GROUP * HEAD_SIZE
    pieces = 2 if heads % 2 == 0 else 1
    chunk = heads * wide // pieces
    fast = outer == 4 and n_tp == 2

    def group_gather(value):
        return lax.all_gather(value, "inst", axis=0, tiled=True, axis_index_groups=groups)

    weights = {}

    def gather_weights():
        w_kv = jnp.concatenate([w_key, w_value], axis=1)
        cut = [w_query[:, piece * chunk : (piece + 1) * chunk] for piece in range(pieces)]
        for name, value in ((0, cut[0]), ("kv", w_kv), (1, cut[-1])):
            if name != 1 or pieces == 2:
                weights[name] = group_gather(step(value))

    tokens = [{}, {}]
    spot = jnp.stack([x, w]).astype(jnp.int32)
    every = (None, 0, 1)
    if fast:

        def cut(j, p):
            column = (((z % 2) ^ j) * n_tp + p) * part
            return jnp.concatenate(
                [
                    lax.dynamic_slice(tokens_in, (h * half, column), (half, part))
                    for h in (first, 1 - first)
                ],
                axis=0,
            )

        swap = {j: over_tp(step(cut(j, 1 - x))) for j in (1, 0)}
        gather_weights()
        mine = z // 2 == x
        held, came = {}, {}
        own = {j: cut(j, x) for j in (1, 0)}
        swap[1] = step(swap[1])
        send = {b: jnp.where(mine == (b < 2), own[1], swap[1]) for b in (1, 3)}
        send[1], send[3] = step(send[1], send[3])
        got = {b: over_outer(send[b], b) for b in (1, 3)}
        swap[0] = step(swap[0])
        send = {b: jnp.where(mine == (b < 2), own[0], swap[0]) for b in (2, 0)}
        send[2] = step(send[2])
        got[2], got[0] = over_outer(send[2], 2), send[0]
        for b in (1, 3, 0, 2):
            held[b] = step(got[b])
            came[b] = over_tp(held[b])

        def arrived(j):
            bits = (j, j + 2)
            came[j], came[j + 2] = step(came[j], came[j + 2])
            arrays = [which[b] for which in (held, came) for b in bits]
            for h in every:
                tokens[j][h] = [(a, rows, 0) if h is None else (a, half, h) for a in arrays]

    else:
        gather_weights()
        swapped = jnp.where(first == 1, jnp.roll(tokens_in, half, axis=0), tokens_in)
        own = swapped.reshape(rows, outer // n_tp, n_tp, part)
        parts = lax.all_to_all(own, "tp", 2, 1, tiled=True).reshape(rows, outer, part)
        for j in (1, 0):
            come = jnp.stack(
                [
                    over_outer(lax.dynamic_index_in_dim(parts, z ^ b, 1, keepdims=False), b)
                    for b in range(j, outer, 2)
                ]
            )
            both = lax.all_gather(come.reshape(-1, part), "tp", axis=1, tiled=True)
            both = both.reshape(count, 2, half, -1)
            for h in every:
                array = (both if h is None else both[:, h]).reshape(-1, both.shape[-1])
                tokens[j][h] = [(array, array.shape[0], 0)]

        def arrived(j):
            pass

    def first_send(h, name):
        weight = step(weights[name])
        n = rows if h is None else half
        outs = [(n, jnp.bfloat16)] * count if h is None else [(count * n, jnp.bfloat16)]
        sends = multiply(first_kernel, spot, tokens[1][h], weight, (), outs)
        sends = step(*sends) if len(sends) > 1 else [step(*sends)]
        return [over_outer(send, 1) for send in sends]

    def later_sends(h, name, came):
        weight = weights[name]
        n, cols = rows if h is None else half, weight.shape[1]
        came = step(*came) if len(came) > 1 else [step(*came)]
        if count == 2:
            outs = [(n, jnp.bfloat16), (n, jnp.float32)]
            send, keep = multiply(later_kernel, spot, tokens[0][h], weight, came, outs)
            return keep, over_outer(step(send), 2)
        keep = dot(tokens[0][h][0][0], weight) + jnp.concatenate(came, axis=0).astype(jnp.float32)
        bits, left = 2, count
        while True:
            pairs = keep.reshape(left // 2, 2, n, cols)
            came = over_outer(step(pairs[:, 1].astype(jnp.bfloat16)), bits)
            bits, left = bits * 2, left // 2
            if left == 1:
                return pairs[:, 0].reshape(n, cols), came.reshape(n, cols)
            keep = pairs[:, 0] + came.astype(jnp.float32)

    if pieces == 2:
        jobs = [(None, 0), (None, "kv"), (0, 1), (1, 1)]
    else:
        jobs = [(None, "kv"), (0, 0), (1, 0)]
    opened, parts_of, lasts = {}, {}, []
    kv_job = jobs.index((None, "kv"))
    attended = [None]

    def start(n):
        opened[n] = first_send(*jobs[n])

    def advance(n):
        parts_of[n] = later_sends(*jobs[n], opened[n])

    def arrive(n):
        parts_of[n] = (parts_of[n][0], step(parts_of[n][1]))

    def attention(n):
        h, piece = jobs[n]
        here = first if h is None else h ^ first
        place = jnp.stack([prompt_len[0], here, first]).astype(jnp.int32)
        kv = parts_of[kv_job]
        shape = (rows, heads * wide)
        attended[0], last = attend(
            place, parts_of[n], stored_key_cache, stored_value_cache, kv, piece * chunk, shape, attended[0]
        )
        lasts.append(step(last))

    def from_xor_order(values, index):
        out = jnp.stack(values)
        shape = out.shape
        bits = len(values).bit_length() - 1
        for bit in range(bits):
            out = out.reshape(len(values) >> (bit + 1), 2, 1 << bit, *shape[1:])
            out = jnp.where((index >> bit) % 2 == 1, out[:, ::-1], out)
        return out.reshape(shape)

    last_a, last_b = len(jobs) - 2, len(jobs) - 1
    arrived(1)
    start(0)
    start(1)
    arrived(0)
    advance(0)
    if pieces == 2:
        advance(1)
        start(2)
        start(3)
        arrive(0)
        arrive(1)
        advance(2)
        attention(0)
        advance(3)
    else:
        start(2)
        advance(1)
        arrive(0)
        advance(2)
    arrive(last_a)
    attention(last_a)
    in_group = [jnp.concatenate(lasts, axis=1)]
    in_group += [over_inst(in_group[0], m) for m in range(1, INNER)]
    arrive(last_b)
    in_group[1] = step(in_group[1])
    in_group = from_xor_order(in_group, w)
    over_all = [in_group] + [over_outer(in_group, b) for b in range(1, outer)]
    attention(last_b)
    over_all[1] = step(over_all[1])
    handoff = from_xor_order(over_all, z).reshape(n_inst, heads * wide)
    return (attended[0], handoff)


def solution(mesh):
    return jax.shard_map(
        shards,
        mesh=mesh,
        in_specs=(
            P("inst", "tp"),
            P("inst", "tp"),
            P("inst", "tp"),
            P("inst", "tp"),
            P("inst", "tp"),
            P("inst", "tp"),
            P("inst"),
        ),
        out_specs=(P("inst", "tp"), P(None, "tp")),
        check_vma=False,
    )
```

```python
import jax
import jax.numpy as jnp
from jax import lax
from jax.experimental import pallas as pl
from jax.experimental.pallas import tpu as pltpu
from jax.sharding import PartitionSpec as P

HEAD_SIZE = 128
QUERY_PER_GROUP = 4
VMEM_LIMIT = 32 * 1024 * 1024
COST = 1 << 20
INNER = 4


def dot(a, b):
    return jnp.dot(a, b, preferred_element_type=jnp.float32)


def attention_kernel(
    place_ref, qm_ref, qc_ref, kc_ref, vc_ref, km_ref, kt_ref, vm_ref, vt_ref, *rest
):
    o_ref, last_ref = rest[-2:]
    length, here, first = place_ref[0], place_ref[1], place_ref[2]
    rows, block = qm_ref.shape[0], km_ref.shape[0]
    half = block // 2
    total = lambda mine, came: (mine + came.astype(jnp.float32)).astype(jnp.bfloat16)
    factor = 1.4426950408889634 / HEAD_SIZE**0.5
    row = lax.broadcasted_iota(jnp.int32, (rows, 1), 0) + here * half
    col = lax.broadcasted_iota(jnp.int32, (rows, block), 1)
    col = jnp.where(col < half, col + first * half, col - first * half)
    allowed = (col <= row) & (col < length)
    contract = (((1,), (1,)), ((), ()))
    at = row == length - 1
    keys = total(km_ref[...], kt_ref[...])
    values = total(vm_ref[...], vt_ref[...])
    stack = 2
    allowed = jnp.concatenate([allowed] * stack, axis=0)
    for member in range(0, QUERY_PER_GROUP, stack):
        each = [
            slice((member + i) * HEAD_SIZE, (member + i + 1) * HEAD_SIZE) for i in range(stack)
        ]
        q = jnp.concatenate([total(qm_ref[:, cols], qc_ref[:, cols]) for cols in each], axis=0)
        s1 = lax.dot_general(q, kc_ref[...], contract, preferred_element_type=jnp.float32)
        s2 = lax.dot_general(q, keys, contract, preferred_element_type=jnp.float32)
        s2 = jnp.where(allowed, s2, -jnp.inf)
        top = jnp.maximum(jnp.max(s1, axis=1, keepdims=True), jnp.max(s2, axis=1, keepdims=True))
        p1 = jnp.exp2((s1 - top) * factor)
        p2 = jnp.exp2((s2 - top) * factor)
        norm = jnp.sum(p1, axis=1, keepdims=True) + jnp.sum(p2, axis=1, keepdims=True)
        both = dot(p1.astype(jnp.bfloat16), vc_ref[...]) + dot(p2.astype(jnp.bfloat16), values)
        both = both / norm
        for i, cols in enumerate(each):
            out = both[i * rows : (i + 1) * rows]
            o_ref[:, cols] = out.astype(o_ref.dtype)
            last_ref[:, cols] = jnp.sum(jnp.where(at, out, 0.0), axis=0, keepdims=True).astype(
                last_ref.dtype
            )


def attend(place, q, which, k_cache, v_cache, kv, start, shape, buffer):
    cols = q[0].shape[1]
    wide = QUERY_PER_GROUP * HEAD_SIZE
    cached, block = k_cache.shape[0], kv[0].shape[0]
    rows = block // 2
    heads = k_cache.shape[1] // HEAD_SIZE
    groups = cols // wide
    begin = start // wide
    column = lambda i, place: (0, begin + i)
    after = lambda i, place: (0, heads + begin + i)
    mine = lambda i, place: (which, i)
    buffers = [] if buffer is None else [buffer]
    return pl.pallas_call(
        attention_kernel,
        grid_spec=pltpu.PrefetchScalarGridSpec(
            num_scalar_prefetch=1,
            grid=(groups,),
            in_specs=[
                pl.BlockSpec((rows, wide), mine),
                pl.BlockSpec((rows, wide), mine),
                pl.BlockSpec((cached, HEAD_SIZE), column),
                pl.BlockSpec((cached, HEAD_SIZE), column),
                pl.BlockSpec((block, HEAD_SIZE), column),
                pl.BlockSpec((block, HEAD_SIZE), column),
                pl.BlockSpec((block, HEAD_SIZE), after),
                pl.BlockSpec((block, HEAD_SIZE), after),
            ]
            + [pl.BlockSpec(memory_space=pl.ANY)] * len(buffers),
            out_specs=[
                pl.BlockSpec((rows, wide), lambda i, place: (place[1], begin + i)),
                pl.BlockSpec((1, wide), lambda i, place: (0, i)),
            ],
        ),
        out_shape=[
            jax.ShapeDtypeStruct(shape, jnp.bfloat16),
            jax.ShapeDtypeStruct((1, cols), jnp.bfloat16),
        ],
        input_output_aliases={9: 0} if buffers else {},
        compiler_params=pltpu.CompilerParams(vmem_limit_bytes=VMEM_LIMIT),
        cost_estimate=pl.CostEstimate(flops=0, bytes_accessed=COST, transcendentals=0),
        name="attention",
    )(place, *q, k_cache, v_cache, *kv, *kv, *buffers)


def shards(tokens_in, w_query, w_key, w_value, stored_key_cache, stored_value_cache, prompt_len):
    n_inst, n_tp = lax.axis_size("inst"), lax.axis_size("tp")
    outer = n_inst // INNER
    me = lax.axis_index("inst")
    z, w = me // INNER, me % INNER
    x = lax.axis_index("tp")
    rows, local = tokens_in.shape
    half = rows // 2
    part = local // outer
    groups = [list(range(o * INNER, (o + 1) * INNER)) for o in range(outer)]

    first = (prompt_len[0] - 1) // half

    def over_inst(value, bits):
        return lax.ppermute(value, "inst", [(i, i ^ bits) for i in range(n_inst)])

    def over_outer(value, bits):
        return over_inst(value, bits * INNER)

    def over_tp(value):
        return lax.ppermute(value, "tp", [(0, 1), (1, 0)])

    def swapped_if(flag, a, b, axis):
        return jnp.where(
            flag, jnp.concatenate([b, a], axis=axis), jnp.concatenate([a, b], axis=axis)
        )

    last_step = [None]

    def step(*values):
        if last_step[0] is not None:
            *values, _ = lax.optimization_barrier((*values, last_step[0]))
        last_step[0] = values[0]
        return values[0] if len(values) == 1 else values

    heads = w_key.shape[1] // HEAD_SIZE
    wide = QUERY_PER_GROUP * HEAD_SIZE
    pieces = 2 if heads % 2 == 0 else 1
    chunk = heads * wide // pieces
    fast = outer == 4 and n_tp == 2

    def group_gather(value):
        return lax.all_gather(value, "inst", axis=0, tiled=True, axis_index_groups=groups)

    weights = {}

    def gather_queries(piece):
        weights[piece] = group_gather(step(w_query[:, piece * chunk : (piece + 1) * chunk]))

    def gather_others():
        weights["kv"] = group_gather(step(jnp.concatenate([w_key, w_value], axis=1)))
        if pieces == 2:
            gather_queries(1)

    tokens = {}
    if fast:

        def cut(j, p):
            column = (((z % 2) ^ j) * n_tp + p) * part
            return jnp.concatenate(
                [
                    lax.dynamic_slice(tokens_in, (h * half, column), (half, part))
                    for h in (first, 1 - first)
                ],
                axis=0,
            )

        swap = {1: over_tp(step(cut(1, 1 - x)))}
        gather_queries(0)
        swap[0] = over_tp(step(cut(0, 1 - x)))
        gather_others()
        mine = z // 2 == x
        held, came = {}, {}
        own = {j: cut(j, x) for j in (1, 0)}
        swap[1] = step(swap[1])
        send = {b: jnp.where(mine == (b < 2), own[1], swap[1]) for b in (1, 3)}
        send[1], send[3] = step(send[1], send[3])
        got = {b: over_outer(send[b], b) for b in (1, 3)}

        def tp_exchange(b):
            held[b] = step(got[b])
            came[b] = over_tp(held[b])

        tp_exchange(1)
        tp_exchange(3)
        swap[0] = step(swap[0])
        send = {b: jnp.where(mine == (b < 2), own[0], swap[0]) for b in (2, 0)}
        send[2] = step(send[2])
        got[2], got[0] = over_outer(send[2], 2), send[0]
        tp_exchange(0)

        def arrived(b):
            if b not in tokens:
                tokens[b] = swapped_if(x == 1, held[b], step(came[b]), 1)

    else:
        gather_queries(0)
        gather_others()
        swapped = jnp.where(first == 1, jnp.roll(tokens_in, half, axis=0), tokens_in)
        own = swapped.reshape(rows, outer // n_tp, n_tp, part)
        parts = lax.all_to_all(own, "tp", 2, 1, tiled=True).reshape(rows, outer, part)
        come = jnp.stack(
            [
                over_outer(lax.dynamic_index_in_dim(parts, z ^ b, 1, keepdims=False), b)
                for b in range(outer)
            ]
        )
        both = lax.all_gather(come.reshape(-1, part), "tp", axis=1, tiled=True)
        both = both.reshape(outer, rows, -1)
        tokens.update({b: both[b] for b in range(outer)})

        def arrived(b):
            pass

    def rows_of(value, h):
        return value if h is None else value[h * half : (h + 1) * half]

    def first_send(h, name):
        weight = step(weights[name])
        bits = range(1, outer, 2)
        if h is None:
            come = {}
            for b in bits:
                arrived(b)
                come[b] = over_outer(step(dot(tokens[b], weight).astype(jnp.bfloat16)), 1)
            return come
        joined = jnp.concatenate([rows_of(tokens[b], h) for b in bits], axis=0)
        come = over_outer(step(dot(joined, weight).astype(jnp.bfloat16)), 1)
        return {b: (come, i) for i, b in enumerate(bits)}

    def later_sends(h, name, come):
        weight = weights[name]
        sums = {}
        if h is not None:
            whole = step(next(iter(come.values()))[0])
            come = {b: whole[i * half : (i + 1) * half] for b, (_, i) in come.items()}
        for b in reversed(range(0, outer, 2)):
            if h is None:
                come[b + 1] = step(come[b + 1])
            arrived(b)
            sums[b] = dot(rows_of(tokens[b], h), weight) + come[b + 1].astype(jnp.float32)
        bit = 2
        while True:
            for b in sorted(sums):
                if b & bit:
                    moved = over_outer(step(sums.pop(b).astype(jnp.bfloat16)), bit)
                    if 2 * bit == outer:
                        return sums[0], moved
                    sums[b ^ bit] = sums[b ^ bit] + moved.astype(jnp.float32)
            bit *= 2

    if pieces == 2:
        jobs = [(None, 0), (None, "kv"), (0, 1), (1, 1)]
    else:
        jobs = [(None, "kv"), (0, 0), (1, 0)]
    opened, parts_of, lasts = {}, {}, []
    attended = [None]

    def start(n):
        opened[n] = first_send(*jobs[n])

    def advance(n):
        parts_of[n] = later_sends(*jobs[n], opened[n])

    def arrive(n):
        parts_of[n] = (parts_of[n][0], step(parts_of[n][1]))

    def attention(n, h):
        own_half, piece = jobs[n]
        place = jnp.stack([prompt_len[0], h ^ first, first]).astype(jnp.int32)
        which = h if own_half is None else 0
        kv = parts_of[jobs.index((None, "kv"))]
        caches = (stored_key_cache, stored_value_cache)
        shape = (rows, heads * wide)
        attended[0], last = attend(
            place, parts_of[n], which, *caches, kv, piece * chunk, shape, attended[0]
        )
        lasts.append(step(last))

    def from_xor_order(values, index):
        out = jnp.stack(values)
        shape = out.shape
        bits = len(values).bit_length() - 1
        for bit in range(bits):
            out = out.reshape(len(values) >> (bit + 1), 2, 1 << bit, *shape[1:])
            out = jnp.where((index >> bit) % 2 == 1, out[:, ::-1], out)
        return out.reshape(shape)

    start(0)
    if fast:
        tp_exchange(2)
    start(1)
    advance(0)
    if pieces == 2:
        advance(1)
        start(2)
        arrive(0)
        start(3)
        advance(2)
        arrive(1)
        advance(3)
        attention(0, 0)
        arrive(2)
        attention(2, 0)
    else:
        start(2)
        advance(1)
        arrive(0)
        advance(2)
        arrive(1)
        attention(1, 0)
    arrive(len(jobs) - 1)
    row = jnp.concatenate(lasts, axis=1)
    in_group = [row] + [over_inst(row, m) for m in range(1, INNER)]
    if pieces == 2:
        attention(0, 1)
    in_group[1] = step(in_group[1])
    in_group = from_xor_order(in_group, w)
    over_all = [in_group] + [over_outer(in_group, b) for b in range(1, outer)]
    attention(len(jobs) - 1, 1)
    over_all[1] = step(over_all[1])
    handoff = from_xor_order(over_all, z).reshape(n_inst, heads * wide)
    return (attended[0], handoff)


def solution(mesh):
    return jax.shard_map(
        shards,
        mesh=mesh,
        in_specs=(
            P("inst", "tp"),
            P("inst", "tp"),
            P("inst", "tp"),
            P("inst", "tp"),
            P("inst", "tp"),
            P("inst", "tp"),
            P("inst"),
        ),
        out_specs=(P("inst", "tp"), P(None, "tp")),
        check_vma=False,
    )
```

```python
import jax
import jax.numpy as jnp
from jax import lax
from jax.experimental import pallas as pl
from jax.experimental.pallas import tpu as pltpu
from jax.sharding import PartitionSpec as P

HEAD_SIZE = 128
QUERY_PER_GROUP = 4
VMEM_LIMIT = 32 * 1024 * 1024
COST = 1 << 20
INNER = 4


def dot(a, b):
    return jnp.dot(a, b, preferred_element_type=jnp.float32)


def attention_kernel(
    place_ref, qm_ref, qc_ref, kc_ref, vc_ref, km_ref, kt_ref, vm_ref, vt_ref, *rest
):
    o_ref, last_ref = rest[-2:]
    length, here, first = place_ref[0], place_ref[1], place_ref[2]
    rows, block = qm_ref.shape[0], km_ref.shape[0]
    half = block // 2
    total = lambda mine, came: (mine + came.astype(jnp.float32)).astype(jnp.bfloat16)
    factor = 1.4426950408889634 / HEAD_SIZE**0.5
    row = lax.broadcasted_iota(jnp.int32, (rows, 1), 0) + here * half
    col = lax.broadcasted_iota(jnp.int32, (rows, block), 1)
    col = jnp.where(col < half, col + first * half, col - first * half)
    allowed = (col <= row) & (col < length)
    contract = (((1,), (1,)), ((), ()))
    at = row == length - 1
    keys = total(km_ref[...], kt_ref[...])
    values = total(vm_ref[...], vt_ref[...])
    stack = 2
    allowed = jnp.concatenate([allowed] * stack, axis=0)
    for member in range(0, QUERY_PER_GROUP, stack):
        each = [
            slice((member + i) * HEAD_SIZE, (member + i + 1) * HEAD_SIZE) for i in range(stack)
        ]
        q = jnp.concatenate([total(qm_ref[:, cols], qc_ref[:, cols]) for cols in each], axis=0)
        s1 = lax.dot_general(q, kc_ref[...], contract, preferred_element_type=jnp.float32)
        s2 = lax.dot_general(q, keys, contract, preferred_element_type=jnp.float32)
        s2 = jnp.where(allowed, s2, -jnp.inf)
        top = jnp.maximum(jnp.max(s1, axis=1, keepdims=True), jnp.max(s2, axis=1, keepdims=True))
        p1 = jnp.exp2((s1 - top) * factor)
        p2 = jnp.exp2((s2 - top) * factor)
        norm = jnp.sum(p1, axis=1, keepdims=True) + jnp.sum(p2, axis=1, keepdims=True)
        both = dot(p1.astype(jnp.bfloat16), vc_ref[...]) + dot(p2.astype(jnp.bfloat16), values)
        both = both / norm
        for i, cols in enumerate(each):
            out = both[i * rows : (i + 1) * rows]
            o_ref[:, cols] = out.astype(o_ref.dtype)
            last_ref[:, cols] = jnp.sum(jnp.where(at, out, 0.0), axis=0, keepdims=True).astype(
                last_ref.dtype
            )


def attend(place, q, which, k_cache, v_cache, kv, start, shape, buffer):
    cols = q[0].shape[1]
    wide = QUERY_PER_GROUP * HEAD_SIZE
    cached, block = k_cache.shape[0], kv[0].shape[0]
    rows = block // 2
    heads = k_cache.shape[1] // HEAD_SIZE
    groups = cols // wide
    begin = start // wide
    column = lambda i, place: (0, begin + i)
    after = lambda i, place: (0, heads + begin + i)
    mine = lambda i, place: (which, i)
    buffers = [] if buffer is None else [buffer]
    return pl.pallas_call(
        attention_kernel,
        grid_spec=pltpu.PrefetchScalarGridSpec(
            num_scalar_prefetch=1,
            grid=(groups,),
            in_specs=[
                pl.BlockSpec((rows, wide), mine),
                pl.BlockSpec((rows, wide), mine),
                pl.BlockSpec((cached, HEAD_SIZE), column),
                pl.BlockSpec((cached, HEAD_SIZE), column),
                pl.BlockSpec((block, HEAD_SIZE), column),
                pl.BlockSpec((block, HEAD_SIZE), column),
                pl.BlockSpec((block, HEAD_SIZE), after),
                pl.BlockSpec((block, HEAD_SIZE), after),
            ]
            + [pl.BlockSpec(memory_space=pl.ANY)] * len(buffers),
            out_specs=[
                pl.BlockSpec((rows, wide), lambda i, place: (place[1], begin + i)),
                pl.BlockSpec((1, wide), lambda i, place: (0, i)),
            ],
        ),
        out_shape=[
            jax.ShapeDtypeStruct(shape, jnp.bfloat16),
            jax.ShapeDtypeStruct((1, cols), jnp.bfloat16),
        ],
        input_output_aliases={9: 0} if buffers else {},
        compiler_params=pltpu.CompilerParams(vmem_limit_bytes=VMEM_LIMIT),
        cost_estimate=pl.CostEstimate(flops=0, bytes_accessed=COST, transcendentals=0),
        name="attention",
    )(place, *q, k_cache, v_cache, *kv, *kv, *buffers)


def shards(tokens_in, w_query, w_key, w_value, stored_key_cache, stored_value_cache, prompt_len):
    n_inst, n_tp = lax.axis_size("inst"), lax.axis_size("tp")
    outer = n_inst // INNER
    me = lax.axis_index("inst")
    z, w = me // INNER, me % INNER
    x = lax.axis_index("tp")
    rows, local = tokens_in.shape
    half = rows // 2
    part = local // outer

    first = (prompt_len[0] - 1) // half

    def over_inst(value, bits):
        return lax.ppermute(value, "inst", [(i, i ^ bits) for i in range(n_inst)])

    def over_outer(value, bits):
        return over_inst(value, bits * INNER)

    def over_tp(value):
        return lax.ppermute(value, "tp", [(0, 1), (1, 0)])

    def swapped_if(flag, a, b, axis):
        return jnp.where(
            flag, jnp.concatenate([b, a], axis=axis), jnp.concatenate([a, b], axis=axis)
        )

    last_step = [None]

    def step(*values):
        if last_step[0] is not None:
            *values, _ = lax.optimization_barrier((*values, last_step[0]))
        last_step[0] = values[0]
        return values[0] if len(values) == 1 else values

    heads = w_key.shape[1] // HEAD_SIZE
    wide = QUERY_PER_GROUP * HEAD_SIZE
    pieces = 2 if heads % 2 == 0 else 1
    chunk = heads * wide // pieces
    fast = outer == 4 and n_tp == 2

    groups = [list(range(o * INNER, (o + 1) * INNER)) for o in range(outer)]

    def group_gather(value):
        return lax.all_gather(value, "inst", axis=0, tiled=True, axis_index_groups=groups)

    weights = {}

    def gather_queries(piece, source):
        weights[piece] = group_gather(source[:, piece * chunk : (piece + 1) * chunk])

    def gather_others():
        key, value, query = step(w_key, w_value, w_query)
        weights["kv"] = group_gather(jnp.concatenate([key, value], axis=1))
        if pieces == 2:
            gather_queries(1, query)

    tokens = {}
    if fast:

        def cut(source, j, p):
            column = (((z % 2) ^ j) * n_tp + p) * part
            return jnp.concatenate(
                [
                    lax.dynamic_slice(source, (h * half, column), (half, part))
                    for h in (first, 1 - first)
                ],
                axis=0,
            )

        gather_queries(0, w_query)
        swap = {1: over_tp(step(cut(tokens_in, 1, 1 - x)))}
        source = step(tokens_in)
        swap[0] = over_tp(step(cut(source, 0, 1 - x)))
        mine = z // 2 == x
        held, came = {}, {}
        swap[1] = step(swap[1])
        own = cut(source, 1, x)
        send = {b: jnp.where(mine == (b < 2), own, swap[1]) for b in (1, 3)}
        send[1], send[3] = step(send[1], send[3])
        got = {b: over_outer(send[b], b) for b in (1, 3)}
        gather_others()

        def tp_exchange(b):
            held[b] = step(got[b])
            came[b] = over_tp(held[b])

        tp_exchange(1)
        tp_exchange(3)
        swap[0] = step(swap[0])
        own = cut(source, 0, x)
        send = {b: jnp.where(mine == (b < 2), own, swap[0]) for b in (2, 0)}
        send[2] = step(send[2])
        got[2], got[0] = over_outer(send[2], 2), send[0]
        tp_exchange(0)

        def arrived(b):
            if b not in tokens:
                tokens[b] = (swapped_if(x == 1, held[b], step(came[b]), 1),)

    else:
        gather_queries(0, w_query)
        gather_others()
        swapped = jnp.where(first == 1, jnp.roll(tokens_in, half, axis=0), tokens_in)
        own = swapped.reshape(rows, outer // n_tp, n_tp, part)
        parts = lax.all_to_all(own, "tp", 2, 1, tiled=True).reshape(rows, outer, part)
        come = jnp.stack(
            [
                over_outer(lax.dynamic_index_in_dim(parts, z ^ b, 1, keepdims=False), b)
                for b in range(outer)
            ]
        )
        both = lax.all_gather(come.reshape(-1, part), "tp", axis=1, tiled=True)
        both = both.reshape(outer, rows, -1)
        tokens.update({b: (both[b],) for b in range(outer)})

        def arrived(b):
            pass

    def rows_of(values, h):
        if h is None:
            return values
        return tuple(value[h * half : (h + 1) * half] for value in values)

    def times(values, weight):
        total, row = None, 0
        for value in values:
            one = dot(value, weight[row : row + value.shape[1]])
            total = one if total is None else total + one
            row += value.shape[1]
        return total

    def first_send(h, name):
        weight = weights[name] = step(weights[name])
        bits = range(1, outer, 2)
        if h is None:
            come = {}
            for b in bits:
                arrived(b)
                come[b] = over_outer(step(times(tokens[b], weight).astype(jnp.bfloat16)), 1)
            return come
        joined = [jnp.concatenate(same) for same in zip(*[rows_of(tokens[b], h) for b in bits])]
        come = over_outer(step(times(joined, weight).astype(jnp.bfloat16)), 1)
        return {b: (come, i) for i, b in enumerate(bits)}

    def later_sends(h, name, come):
        weight = weights[name]
        sums = {}
        if h is not None:
            whole = step(next(iter(come.values()))[0])
            come = {b: whole[i * half : (i + 1) * half] for b, (_, i) in come.items()}
        for b in range(0, outer, 2):
            if h is None:
                come[b + 1] = step(come[b + 1])
            arrived(b)
        for b in range(0, outer, 2):
            sums[b] = times(rows_of(tokens[b], h), weight) + come[b + 1].astype(jnp.float32)
        bit = 2
        while True:
            for b in sorted(sums):
                if b & bit:
                    moved = over_outer(step(sums.pop(b).astype(jnp.bfloat16)), bit)
                    if 2 * bit == outer:
                        return sums[0], moved
                    sums[b ^ bit] = sums[b ^ bit] + moved.astype(jnp.float32)
            bit *= 2

    if pieces == 2:
        jobs = [(None, 0), (None, "kv"), (0, 1), (1, 1)]
    else:
        jobs = [(None, "kv"), (0, 0), (1, 0)]
    opened, parts_of, lasts = {}, {}, []
    attended = [None]

    def start(n):
        opened[n] = first_send(*jobs[n])

    def advance(n):
        parts_of[n] = later_sends(*jobs[n], opened[n])

    def arrive(n):
        came_in, mine = step(parts_of[n][1], parts_of[n][0])
        parts_of[n] = (mine, came_in)

    def attention(n, h):
        own_half, piece = jobs[n]
        place = jnp.stack([prompt_len[0], h ^ first, first]).astype(jnp.int32)
        which = h if own_half is None else 0
        kv = parts_of[jobs.index((None, "kv"))]
        caches = (stored_key_cache, stored_value_cache)
        shape = (rows, heads * wide)
        attended[0], last = attend(
            place, parts_of[n], which, *caches, kv, piece * chunk, shape, attended[0]
        )
        lasts.append(step(last))

    def from_xor_order(values, index):
        out = jnp.stack(values)
        shape = out.shape
        bits = len(values).bit_length() - 1
        for bit in range(bits):
            out = out.reshape(len(values) >> (bit + 1), 2, 1 << bit, *shape[1:])
            out = jnp.where((index >> bit) % 2 == 1, out[:, ::-1], out)
        return out.reshape(shape)

    start(0)
    if fast:
        tp_exchange(2)
    start(1)
    advance(0)
    if pieces == 2:
        start(2)
        advance(1)
        arrive(0)
        start(3)
        advance(2)
        arrive(1)
        advance(3)
        attention(0, 0)
        arrive(2)
        attention(2, 0)
    else:
        start(2)
        advance(1)
        arrive(0)
        advance(2)
        arrive(1)
        attention(1, 0)
    arrive(len(jobs) - 1)
    row = step(jnp.concatenate(lasts, axis=1))
    in_group = [row] + [over_inst(row, m) for m in range(1, INNER)]
    if pieces == 2:
        attention(0, 1)
    in_group[1] = step(in_group[1])
    in_group = from_xor_order(in_group, w)
    over_all = [in_group] + [over_outer(in_group, b) for b in range(1, outer)]
    attention(len(jobs) - 1, 1)
    over_all[1] = step(over_all[1])
    handoff = from_xor_order(over_all, z).reshape(n_inst, heads * wide)
    return (attended[0], handoff)


def solution(mesh):
    return jax.shard_map(
        shards,
        mesh=mesh,
        in_specs=(
            P("inst", "tp"),
            P("inst", "tp"),
            P("inst", "tp"),
            P("inst", "tp"),
            P("inst", "tp"),
            P("inst", "tp"),
            P("inst"),
        ),
        out_specs=(P("inst", "tp"), P(None, "tp")),
        check_vma=False,
    )
```

```python
import jax
import jax.numpy as jnp
from jax import lax
from jax.experimental import pallas as pl
from jax.experimental.pallas import tpu as pltpu
from jax.sharding import PartitionSpec as P

HEAD_SIZE = 128
QUERY_PER_GROUP = 4
VMEM_LIMIT = 32 * 1024 * 1024
COST = 1 << 10
INNER = 4


def dot(a, b):
    return jnp.dot(a, b, preferred_element_type=jnp.float32)


def attention_kernel(
    place_ref, qm_ref, qc_ref, kc_ref, vc_ref, km_ref, kt_ref, vm_ref, vt_ref, *rest
):
    o_ref, last_ref = rest[-2:]
    length, here, first = place_ref[0], place_ref[1], place_ref[2]
    rows, block = qm_ref.shape[0], km_ref.shape[0]
    half = block // 2
    total = lambda mine, came: (mine + came.astype(jnp.float32)).astype(jnp.bfloat16)
    factor = 1.4426950408889634 / HEAD_SIZE**0.5
    row = lax.broadcasted_iota(jnp.int32, (rows, 1), 0) + here * half
    col = lax.broadcasted_iota(jnp.int32, (rows, block), 1)
    col = jnp.where(col < half, col + first * half, col - first * half)
    allowed = (col <= row) & (col < length)
    contract = (((1,), (1,)), ((), ()))
    at = row == length - 1
    keys = total(km_ref[...], kt_ref[...])
    values = total(vm_ref[...], vt_ref[...])
    stack = 2
    allowed = jnp.concatenate([allowed] * stack, axis=0)
    for member in range(0, QUERY_PER_GROUP, stack):
        each = [
            slice((member + i) * HEAD_SIZE, (member + i + 1) * HEAD_SIZE) for i in range(stack)
        ]
        q = jnp.concatenate([total(qm_ref[:, cols], qc_ref[:, cols]) for cols in each], axis=0)
        s1 = lax.dot_general(q, kc_ref[...], contract, preferred_element_type=jnp.float32)
        s2 = lax.dot_general(q, keys, contract, preferred_element_type=jnp.float32)
        s2 = jnp.where(allowed, s2, -jnp.inf)
        top = jnp.maximum(jnp.max(s1, axis=1, keepdims=True), jnp.max(s2, axis=1, keepdims=True))
        p1 = jnp.exp2((s1 - top) * factor)
        p2 = jnp.exp2((s2 - top) * factor)
        norm = jnp.sum(p1, axis=1, keepdims=True) + jnp.sum(p2, axis=1, keepdims=True)
        both = dot(p1.astype(jnp.bfloat16), vc_ref[...]) + dot(p2.astype(jnp.bfloat16), values)
        both = both / norm
        for i, cols in enumerate(each):
            out = both[i * rows : (i + 1) * rows]
            o_ref[:, cols] = out.astype(o_ref.dtype)
            last_ref[:, cols] = jnp.sum(jnp.where(at, out, 0.0), axis=0, keepdims=True).astype(
                last_ref.dtype
            )


def attend(place, q, k_cache, v_cache, kv, start, shape, buffer):
    cols = q[0].shape[1]
    wide = QUERY_PER_GROUP * HEAD_SIZE
    cached, block = k_cache.shape[0], kv[0].shape[0]
    rows = block // 2
    heads = k_cache.shape[1] // HEAD_SIZE
    groups = cols // wide
    begin = start // wide
    column = lambda i, place: (0, begin + i)
    after = lambda i, place: (0, heads + begin + i)
    mine = lambda i, place: (0, i)
    buffers = [] if buffer is None else [buffer]
    return pl.pallas_call(
        attention_kernel,
        grid_spec=pltpu.PrefetchScalarGridSpec(
            num_scalar_prefetch=1,
            grid=(groups,),
            in_specs=[
                pl.BlockSpec((rows, wide), mine),
                pl.BlockSpec((rows, wide), mine),
                pl.BlockSpec((cached, HEAD_SIZE), column),
                pl.BlockSpec((cached, HEAD_SIZE), column),
                pl.BlockSpec((block, HEAD_SIZE), column),
                pl.BlockSpec((block, HEAD_SIZE), column),
                pl.BlockSpec((block, HEAD_SIZE), after),
                pl.BlockSpec((block, HEAD_SIZE), after),
            ]
            + [pl.BlockSpec(memory_space=pl.ANY)] * len(buffers),
            out_specs=[
                pl.BlockSpec((rows, wide), lambda i, place: (place[1], begin + i)),
                pl.BlockSpec((1, wide), mine),
            ],
        ),
        out_shape=[
            jax.ShapeDtypeStruct(shape, jnp.bfloat16),
            jax.ShapeDtypeStruct((1, cols), jnp.bfloat16),
        ],
        input_output_aliases={9: 0} if buffers else {},
        compiler_params=pltpu.CompilerParams(vmem_limit_bytes=VMEM_LIMIT),
        cost_estimate=pl.CostEstimate(flops=0, bytes_accessed=COST, transcendentals=0),
        name="attention",
    )(place, *q, k_cache, v_cache, *kv, *kv, *buffers)


def shards(tokens_in, w_query, w_key, w_value, stored_key_cache, stored_value_cache, prompt_len):
    n_inst, n_tp = lax.axis_size("inst"), lax.axis_size("tp")
    outer = n_inst // INNER
    me = lax.axis_index("inst")
    z, w = me // INNER, me % INNER
    x = lax.axis_index("tp")
    rows, local = tokens_in.shape
    half = rows // 2
    part = local // outer

    first = (prompt_len[0] - 1) // half

    def over_inst(value, bits):
        return lax.ppermute(value, "inst", [(i, i ^ bits) for i in range(n_inst)])

    def over_outer(value, bits):
        return over_inst(value, bits * INNER)

    def over_tp(value):
        return lax.ppermute(value, "tp", [(0, 1), (1, 0)])

    def swapped_if(flag, a, b, axis):
        return jnp.where(
            flag, jnp.concatenate([b, a], axis=axis), jnp.concatenate([a, b], axis=axis)
        )

    last_step = [None]

    def step(*values):
        if last_step[0] is not None:
            *values, _ = lax.optimization_barrier((*values, last_step[0]))
        last_step[0] = values[0]
        return values[0] if len(values) == 1 else values

    heads = w_key.shape[1] // HEAD_SIZE
    wide = QUERY_PER_GROUP * HEAD_SIZE
    pieces = 2 if heads % 2 == 0 else 1
    chunk = heads * wide // pieces
    fast = outer == 4 and n_tp == 2

    groups = [list(range(o * INNER, (o + 1) * INNER)) for o in range(outer)]

    def group_gather(value):
        return lax.all_gather(value, "inst", axis=0, tiled=True, axis_index_groups=groups)

    weights = {}

    weights["kv"] = group_gather(jnp.concatenate([w_key, w_value], axis=1))

    def gather_queries():
        source = step(w_query) if fast else w_query
        for piece in range(pieces):
            part_of = source[:, piece * chunk : (piece + 1) * chunk]
            weights[piece] = group_gather(part_of)

    tokens = {}
    if fast:

        def cut(source, j, p):
            column = (((z % 2) ^ j) * n_tp + p) * part
            return jnp.concatenate(
                [
                    lax.dynamic_slice(source, (h * half, column), (half, part))
                    for h in (first, 1 - first)
                ],
                axis=0,
            )

        swap = {1: over_tp(step(cut(tokens_in, 1, 1 - x)))}
        source = step(tokens_in)
        swap[0] = over_tp(step(cut(source, 0, 1 - x)))
        mine = z // 2 == x
        held, came = {}, {}
        swap[1] = step(swap[1])
        own = cut(source, 1, x)
        send = {b: jnp.where(mine == (b < 2), own, swap[1]) for b in (1, 3)}
        send[1], send[3] = step(send[1], send[3])
        got = {b: over_outer(send[b], b) for b in (1, 3)}
        gather_queries()

        def tp_exchange(b):
            held[b] = step(got[b])
            came[b] = over_tp(held[b])

        tp_exchange(1)
        weights["kv"] = step(weights["kv"])
        tp_exchange(3)
        swap[0] = step(swap[0])
        own = cut(source, 0, x)
        send = {b: jnp.where(mine == (b < 2), own, swap[0]) for b in (2, 0)}
        send[2] = step(send[2])
        got[2], got[0] = over_outer(send[2], 2), send[0]
        tp_exchange(0)

        def arrived(b):
            if b not in tokens:
                tokens[b] = (swapped_if(x == 1, held[b], step(came[b]), 1),)

    else:
        gather_queries()
        swapped = jnp.where(first == 1, jnp.roll(tokens_in, half, axis=0), tokens_in)
        own = swapped.reshape(rows, outer // n_tp, n_tp, part)
        parts = lax.all_to_all(own, "tp", 2, 1, tiled=True).reshape(rows, outer, part)
        come = jnp.stack(
            [
                over_outer(lax.dynamic_index_in_dim(parts, z ^ b, 1, keepdims=False), b)
                for b in range(outer)
            ]
        )
        both = lax.all_gather(come.reshape(-1, part), "tp", axis=1, tiled=True)
        both = both.reshape(outer, rows, -1)
        tokens.update({b: (both[b],) for b in range(outer)})

        def arrived(b):
            pass

    def rows_of(values, h):
        if h is None:
            return values
        return tuple(value[h * half : (h + 1) * half] for value in values)

    def times(values, weight):
        total, row = None, 0
        for value in values:
            one = dot(value, weight[row : row + value.shape[1]])
            total = one if total is None else total + one
            row += value.shape[1]
        return total

    def first_send(h, name):
        weight = weights[name] = step(weights[name])
        bits = range(1, outer, 2)
        if h is None:
            come = {}
            for b in bits:
                arrived(b)
                come[b] = over_outer(step(times(tokens[b], weight).astype(jnp.bfloat16)), 1)
            return come
        joined = [jnp.concatenate(same) for same in zip(*[rows_of(tokens[b], h) for b in bits])]
        come = over_outer(step(times(joined, weight).astype(jnp.bfloat16)), 1)
        return {b: (come, i) for i, b in enumerate(bits)}

    def later_sends(h, name, come):
        weight = weights[name]
        for b in range(0, outer, 2):
            arrived(b)
        if h is None:
            bits = list(come)
            come = dict(zip(bits, step(*[come[b] for b in bits])))
        else:
            whole = step(next(iter(come.values()))[0])
            come = {b: whole[i * half : (i + 1) * half] for b, (_, i) in come.items()}

        def total(b, arrival):
            return times(rows_of(tokens[b], h), weight) + arrival.astype(jnp.float32)

        if outer == 4 and h is not None:
            send, keep = step(total(2, come[3]).astype(jnp.bfloat16), total(0, come[1]))
            return keep, over_outer(send, 2)
        if outer == 4:
            moved = over_outer(step(total(2, come[3]).astype(jnp.bfloat16)), 2)
            return total(0, step(come[1])), moved
        sums = {b: total(b, come[b + 1]) for b in range(0, outer, 2)}
        bit = 2
        while True:
            for b in sorted(sums):
                if b & bit:
                    moved = over_outer(step(sums.pop(b).astype(jnp.bfloat16)), bit)
                    if 2 * bit == outer:
                        return sums[0], moved
                    sums[b ^ bit] = sums[b ^ bit] + moved.astype(jnp.float32)
            bit *= 2

    jobs = [(None, "kv")] + [(h, piece) for piece in range(pieces) for h in (0, 1)]
    opened, parts_of, lasts = {}, {}, []
    attended = [None]

    def start(n):
        opened[n] = first_send(*jobs[n])

    def advance(n):
        parts_of[n] = later_sends(*jobs[n], opened[n])

    def arrive(n):
        came_in, mine = step(parts_of[n][1], parts_of[n][0])
        parts_of[n] = (mine, came_in)

    def attention(n):
        h, piece = jobs[n]
        place = jnp.stack([prompt_len[0], h ^ first, first]).astype(jnp.int32)
        caches = (stored_key_cache, stored_value_cache)
        shape = (rows, heads * wide)
        attended[0], last = attend(
            place, parts_of[n], *caches, parts_of[0], piece * chunk, shape, attended[0]
        )
        lasts.append(step(last))

    def from_xor_order(values, index):
        out = jnp.stack(values)
        shape = out.shape
        bits = len(values).bit_length() - 1
        for bit in range(bits):
            out = out.reshape(len(values) >> (bit + 1), 2, 1 << bit, *shape[1:])
            out = jnp.where((index >> bit) % 2 == 1, out[:, ::-1], out)
        return out.reshape(shape)

    start(0)
    if fast:
        tp_exchange(2)
    start(1)
    start(2)
    advance(0)
    advance(1)
    if pieces == 2:
        start(3)
        advance(2)
        start(4)
        arrive(0)
        arrive(1)
        advance(3)
        attention(1)
        arrive(2)
        advance(4)
        attention(2)
        arrive(3)
        attention(3)
        arrive(4)
        row = jnp.concatenate([lasts[0], lasts[2]], axis=1)
    else:
        advance(2)
        arrive(0)
        arrive(1)
        attention(1)
        arrive(2)
        row = lasts[0]
    row = step(row)
    in_group = [row] + [over_inst(row, m) for m in range(1, INNER)]
    attention(len(jobs) - 1)
    in_group[1] = step(in_group[1])
    in_group = from_xor_order(in_group, w)
    over_all = [in_group] + [over_outer(in_group, b) for b in range(1, outer)]
    handoff = from_xor_order(over_all, z).reshape(n_inst, heads * wide)
    return (attended[0], handoff)


def solution(mesh):
    return jax.shard_map(
        shards,
        mesh=mesh,
        in_specs=(
            P("inst", "tp"),
            P("inst", "tp"),
            P("inst", "tp"),
            P("inst", "tp"),
            P("inst", "tp"),
            P("inst", "tp"),
            P("inst"),
        ),
        out_specs=(P("inst", "tp"), P(None, "tp")),
        check_vma=False,
    )
```

```python
import jax
import jax.numpy as jnp
from jax import lax
from jax.experimental import pallas as pl
from jax.experimental.pallas import tpu as pltpu
from jax.sharding import PartitionSpec as P

HEAD_SIZE = 128
QUERY_PER_GROUP = 4
VMEM_LIMIT = 32 * 1024 * 1024
COST = 1 << 10
INNER = 4


def dot(a, b):
    return jnp.dot(a, b, preferred_element_type=jnp.float32)


def first_kernel(low_ref, high_ref, w_ref, send_ref):
    t = jnp.concatenate([low_ref[...], high_ref[...]], axis=0)
    send_ref[...] = dot(t, w_ref[...]).astype(send_ref.dtype)


def later_kernel(low_ref, high_ref, w_ref, came_ref, send_ref, keep_ref):
    t = jnp.concatenate([low_ref[...], high_ref[...]], axis=0)
    out = dot(t, w_ref[...]) + came_ref[...].astype(jnp.float32)
    n = keep_ref.shape[0]
    keep_ref[...] = out[:n]
    send_ref[...] = out[n:].astype(send_ref.dtype)


def half_product(low, high, h, weight, came=None, tile=512):
    half, features, columns = low.shape[0] // 2, low.shape[1], weight.shape[1]
    tile = min(tile, columns)
    column = lambda i: (0, i)
    rows = pl.BlockSpec((half, features), lambda i: (h, 0))
    both = pl.BlockSpec((2 * half, tile), column)
    one = pl.BlockSpec((half, tile), column)
    shape = lambda n, dtype: jax.ShapeDtypeStruct((n, columns), dtype)
    first = came is None
    cost = 2 * features * columns * 2 if first else COST
    return pl.pallas_call(
        first_kernel if first else later_kernel,
        grid=(columns // tile,),
        in_specs=[rows, rows, pl.BlockSpec((features, tile), column)] + ([] if first else [both]),
        out_specs=both if first else [one, one],
        out_shape=shape(2 * half, jnp.bfloat16)
        if first
        else [shape(half, jnp.bfloat16), shape(half, jnp.float32)],
        compiler_params=pltpu.CompilerParams(vmem_limit_bytes=VMEM_LIMIT),
        cost_estimate=pl.CostEstimate(flops=0, bytes_accessed=cost, transcendentals=0),
        name="half_product",
    )(low, high, weight, *([] if first else [came]))


def attention_kernel(
    place_ref, qm_ref, qc_ref, kc_ref, vc_ref, km_ref, kt_ref, vm_ref, vt_ref, *rest
):
    o_ref, last_ref = rest[-2:]
    length, here, first = place_ref[0], place_ref[1], place_ref[2]
    rows, block = qm_ref.shape[0], km_ref.shape[0]
    half = block // 2
    total = lambda mine, came: (mine + came.astype(jnp.float32)).astype(jnp.bfloat16)
    factor = 1.4426950408889634 / HEAD_SIZE**0.5
    row = lax.broadcasted_iota(jnp.int32, (rows, 1), 0) + here * half
    col = lax.broadcasted_iota(jnp.int32, (rows, block), 1)
    col = jnp.where(col < half, col + first * half, col - first * half)
    allowed = (col <= row) & (col < length)
    contract = (((1,), (1,)), ((), ()))
    at = row == length - 1
    keys = total(km_ref[...], kt_ref[...])
    values = total(vm_ref[...], vt_ref[...])
    stack = 2
    allowed = jnp.concatenate([allowed] * stack, axis=0)
    for member in range(0, QUERY_PER_GROUP, stack):
        each = [
            slice((member + i) * HEAD_SIZE, (member + i + 1) * HEAD_SIZE) for i in range(stack)
        ]
        q = jnp.concatenate([total(qm_ref[:, cols], qc_ref[:, cols]) for cols in each], axis=0)
        s1 = lax.dot_general(q, kc_ref[...], contract, preferred_element_type=jnp.float32)
        s2 = lax.dot_general(q, keys, contract, preferred_element_type=jnp.float32)
        s2 = jnp.where(allowed, s2, -jnp.inf)
        top = jnp.maximum(jnp.max(s1, axis=1, keepdims=True), jnp.max(s2, axis=1, keepdims=True))
        p1 = jnp.exp2((s1 - top) * factor)
        p2 = jnp.exp2((s2 - top) * factor)
        norm = jnp.sum(p1, axis=1, keepdims=True) + jnp.sum(p2, axis=1, keepdims=True)
        both = dot(p1.astype(jnp.bfloat16), vc_ref[...]) + dot(p2.astype(jnp.bfloat16), values)
        both = both / norm
        for i, cols in enumerate(each):
            out = both[i * rows : (i + 1) * rows]
            o_ref[:, cols] = out.astype(o_ref.dtype)
            last_ref[:, cols] = jnp.sum(jnp.where(at, out, 0.0), axis=0, keepdims=True).astype(
                last_ref.dtype
            )


def attend(place, q, which, k_cache, v_cache, kv, start, shape, buffer, limit):
    cols = q[0].shape[1]
    wide = QUERY_PER_GROUP * HEAD_SIZE
    cached, block = k_cache.shape[0], kv[0].shape[0]
    rows = block // 2
    heads = k_cache.shape[1] // HEAD_SIZE
    groups = cols // wide
    begin = start // wide
    column = lambda i, place: (0, begin + i)
    after = lambda i, place: (0, heads + begin + i)
    mine = lambda i, place: (which, i)
    buffers = [] if buffer is None else [buffer]
    return pl.pallas_call(
        attention_kernel,
        grid_spec=pltpu.PrefetchScalarGridSpec(
            num_scalar_prefetch=1,
            grid=(groups,),
            in_specs=[
                pl.BlockSpec((rows, wide), mine),
                pl.BlockSpec((rows, wide), mine),
                pl.BlockSpec((cached, HEAD_SIZE), column),
                pl.BlockSpec((cached, HEAD_SIZE), column),
                pl.BlockSpec((block, HEAD_SIZE), column),
                pl.BlockSpec((block, HEAD_SIZE), column),
                pl.BlockSpec((block, HEAD_SIZE), after),
                pl.BlockSpec((block, HEAD_SIZE), after),
            ]
            + [pl.BlockSpec(memory_space=pl.ANY)] * len(buffers),
            out_specs=[
                pl.BlockSpec((rows, wide), lambda i, place: (place[1], begin + i)),
                pl.BlockSpec((1, wide), lambda i, place: (0, i)),
            ],
        ),
        out_shape=[
            jax.ShapeDtypeStruct(shape, jnp.bfloat16),
            jax.ShapeDtypeStruct((1, cols), jnp.bfloat16),
        ],
        input_output_aliases={9: 0} if buffers else {},
        compiler_params=pltpu.CompilerParams(vmem_limit_bytes=limit),
        cost_estimate=pl.CostEstimate(flops=0, bytes_accessed=COST, transcendentals=0),
        name="attention",
    )(place, *q, k_cache, v_cache, *kv, *kv, *buffers)


def shards(tokens_in, w_query, w_key, w_value, stored_key_cache, stored_value_cache, prompt_len):
    n_inst, n_tp = lax.axis_size("inst"), lax.axis_size("tp")
    outer = n_inst // INNER
    me = lax.axis_index("inst")
    z, w = me // INNER, me % INNER
    x = lax.axis_index("tp")
    rows, local = tokens_in.shape
    half = rows // 2
    part = local // outer

    first = (prompt_len[0] - 1) // half

    def over_inst(value, bits):
        return lax.ppermute(value, "inst", [(i, i ^ bits) for i in range(n_inst)])

    def over_outer(value, bits):
        return over_inst(value, bits * INNER)

    def over_tp(value):
        return lax.ppermute(value, "tp", [(0, 1), (1, 0)])

    def swapped_if(flag, a, b, axis):
        return jnp.where(
            flag, jnp.concatenate([b, a], axis=axis), jnp.concatenate([a, b], axis=axis)
        )

    last_step = [None]

    def step(*values):
        if last_step[0] is not None:
            *values, _ = lax.optimization_barrier((*values, last_step[0]))
        last_step[0] = values[0]
        return values[0] if len(values) == 1 else values

    heads = w_key.shape[1] // HEAD_SIZE
    wide = QUERY_PER_GROUP * HEAD_SIZE
    pieces = 2 if heads % 2 == 0 else 1
    chunk = heads * wide // pieces
    fast = outer == 4 and n_tp == 2

    groups = [list(range(o * INNER, (o + 1) * INNER)) for o in range(outer)]

    def group_gather(value):
        return lax.all_gather(value, "inst", axis=0, tiled=True, axis_index_groups=groups)

    weights = {}

    weights["kv"] = group_gather(jnp.concatenate([w_key, w_value], axis=1))

    def gather_queries():
        source = step(w_query) if fast else w_query
        for piece in range(pieces):
            part_of = source[:, piece * chunk : (piece + 1) * chunk]
            weights[piece] = group_gather(part_of)

    tokens = {}
    if fast:

        def cut(source, j, p):
            column = (((z % 2) ^ j) * n_tp + p) * part
            return jnp.concatenate(
                [
                    lax.dynamic_slice(source, (h * half, column), (half, part))
                    for h in (first, 1 - first)
                ],
                axis=0,
            )

        swap = {1: over_tp(step(cut(tokens_in, 1, 1 - x)))}
        source = step(tokens_in)
        swap[0] = over_tp(step(cut(source, 0, 1 - x)))
        mine = z // 2 == x
        held, came = {}, {}
        swap[1] = step(swap[1])
        own = cut(source, 1, x)
        send = {b: jnp.where(mine == (b < 2), own, swap[1]) for b in (1, 3)}
        send[1], send[3] = step(send[1], send[3])
        got = {b: over_outer(send[b], b) for b in (1, 3)}
        gather_queries()

        def tp_exchange(b):
            held[b] = step(got[b])
            came[b] = over_tp(held[b])

        tp_exchange(1)
        weights["kv"] = step(weights["kv"])
        tp_exchange(3)
        swap[0] = step(swap[0])
        own = cut(source, 0, x)
        send = {b: jnp.where(mine == (b < 2), own, swap[0]) for b in (2, 0)}
        send[2] = step(send[2])
        got[2], got[0] = over_outer(send[2], 2), send[0]
        tp_exchange(0)

        def arrived(b):
            if b not in tokens:
                tokens[b] = (swapped_if(x == 1, held[b], step(came[b]), 1),)

    else:
        gather_queries()
        swapped = jnp.where(first == 1, jnp.roll(tokens_in, half, axis=0), tokens_in)
        own = swapped.reshape(rows, outer // n_tp, n_tp, part)
        parts = lax.all_to_all(own, "tp", 2, 1, tiled=True).reshape(rows, outer, part)
        come = jnp.stack(
            [
                over_outer(lax.dynamic_index_in_dim(parts, z ^ b, 1, keepdims=False), b)
                for b in range(outer)
            ]
        )
        both = lax.all_gather(come.reshape(-1, part), "tp", axis=1, tiled=True)
        both = both.reshape(outer, rows, -1)
        tokens.update({b: (both[b],) for b in range(outer)})

        def arrived(b):
            pass

    def rows_of(values, h):
        if h is None:
            return values
        return tuple(value[h * half : (h + 1) * half] for value in values)

    def times(values, weight):
        total, row = None, 0
        for value in values:
            one = dot(value, weight[row : row + value.shape[1]])
            total = one if total is None else total + one
            row += value.shape[1]
        return total

    def first_send(h, name):
        weight = weights[name] = step(weights[name])
        bits = range(1, outer, 2)
        if h is None:
            come = {}
            for b in bits:
                arrived(b)
                come[b] = over_outer(step(times(tokens[b], weight).astype(jnp.bfloat16)), 1)
            return come
        if fast:
            send = half_product(tokens[1][0], tokens[3][0], h, weight)
            return over_outer(step(send), 1)
        joined = [jnp.concatenate(same) for same in zip(*[rows_of(tokens[b], h) for b in bits])]
        come = over_outer(step(times(joined, weight).astype(jnp.bfloat16)), 1)
        return {b: (come, i) for i, b in enumerate(bits)}

    def later_sends(h, name, come):
        weight = weights[name]
        arrived(0)
        if fast and h is not None:
            send, keep = half_product(tokens[0][0], tokens[2][0], h, weight, step(come))
            send, keep = step(send, keep)
            return keep, over_outer(send, 2)
        if h is None:
            bits = list(come)
            come = dict(zip(bits, step(*[come[b] for b in bits])))
            arrived(2)
        else:
            whole = step(next(iter(come.values()))[0])
            come = {b: whole[i * half : (i + 1) * half] for b, (_, i) in come.items()}

        def total(b, arrival):
            return times(rows_of(tokens[b], h), weight) + arrival.astype(jnp.float32)

        if outer == 4:
            moved = over_outer(step(total(2, come[3]).astype(jnp.bfloat16)), 2)
            return total(0, step(come[1])), moved
        sums = {b: total(b, come[b + 1]) for b in range(0, outer, 2)}
        bit = 2
        while True:
            for b in sorted(sums):
                if b & bit:
                    moved = over_outer(step(sums.pop(b).astype(jnp.bfloat16)), bit)
                    if 2 * bit == outer:
                        return sums[0], moved
                    sums[b ^ bit] = sums[b ^ bit] + moved.astype(jnp.float32)
            bit *= 2

    jobs = [(None, "kv")] + ([(None, 0)] if pieces == 2 else [])
    jobs += [(0, pieces - 1), (1, pieces - 1)]
    opened, parts_of, lasts = {}, {}, []
    attended = [None]

    def start(n):
        opened[n] = first_send(*jobs[n])

    def advance(n):
        parts_of[n] = later_sends(*jobs[n], opened[n])

    def arrive(n):
        came_in, mine = step(parts_of[n][1], parts_of[n][0])
        parts_of[n] = (mine, came_in)

    def attention(n, h):
        own_half, piece = jobs[n]
        which = h if own_half is None else 0
        place = jnp.stack([prompt_len[0], h ^ first, first]).astype(jnp.int32)
        caches = (stored_key_cache, stored_value_cache)
        shape = (rows, heads * wide)
        limit = VMEM_LIMIT if n < len(jobs) - 1 else 56 * 1024 * 1024
        where = (piece * chunk, shape, attended[0], limit)
        attended[0], last = attend(place, parts_of[n], which, *caches, parts_of[0], *where)
        lasts.append(step(last))

    def from_xor_order(values, index):
        out = jnp.stack(values)
        shape = out.shape
        bits = len(values).bit_length() - 1
        for bit in range(bits):
            out = out.reshape(len(values) >> (bit + 1), 2, 1 << bit, *shape[1:])
            out = jnp.where((index >> bit) % 2 == 1, out[:, ::-1], out)
        return out.reshape(shape)

    start(0)
    if fast:
        tp_exchange(2)
    start(1)
    advance(0)
    if pieces == 2:
        weights[1] = step(weights[1])
        start(2)
        advance(1)
        arrive(0)
        advance(2)
        start(3)
        arrive(1)
        attention(1, 0)
        advance(3)
        attention(1, 1)
        arrive(2)
        attention(2, 0)
        arrive(3)
        row = jnp.concatenate([lasts[0], lasts[2]], axis=1)
    else:
        start(2)
        advance(1)
        arrive(0)
        advance(2)
        arrive(1)
        attention(1, 0)
        arrive(2)
        row = lasts[0]
    row = step(row)
    in_group = [row] + [over_inst(row, m) for m in range(1, INNER)]
    attention(len(jobs) - 1, 1)
    in_group[1] = step(in_group[1])
    in_group = from_xor_order(in_group, w)
    over_all = [in_group] + [over_outer(in_group, b) for b in range(1, outer)]
    handoff = from_xor_order(over_all, z).reshape(n_inst, heads * wide)
    return (attended[0], handoff)


def solution(mesh):
    return jax.shard_map(
        shards,
        mesh=mesh,
        in_specs=(
            P("inst", "tp"),
            P("inst", "tp"),
            P("inst", "tp"),
            P("inst", "tp"),
            P("inst", "tp"),
            P("inst", "tp"),
            P("inst"),
        ),
        out_specs=(P("inst", "tp"), P(None, "tp")),
        check_vma=False,
    )
```

```python
import jax
import jax.numpy as jnp
from jax import lax
from jax.experimental import pallas as pl
from jax.experimental.pallas import tpu as pltpu
from jax.sharding import PartitionSpec as P

HEAD_SIZE = 128
QUERY_PER_GROUP = 4
VMEM_LIMIT = 32 * 1024 * 1024
COST = 1 << 10
INNER = 4


def dot(a, b):
    return jnp.dot(a, b, preferred_element_type=jnp.float32)


def first_kernel(low_ref, high_ref, w_ref, send_ref):
    t = jnp.concatenate([low_ref[...], high_ref[...]], axis=0)
    send_ref[...] = dot(t, w_ref[...]).astype(send_ref.dtype)


def later_kernel(low_ref, high_ref, w_ref, came_ref, send_ref, keep_ref):
    t = jnp.concatenate([low_ref[...], high_ref[...]], axis=0)
    out = dot(t, w_ref[...]) + came_ref[...].astype(jnp.float32)
    n = keep_ref.shape[0]
    keep_ref[...] = out[:n]
    send_ref[...] = out[n:].astype(send_ref.dtype)


def half_product(low, high, h, weight, came=None, tile=512):
    half, features, columns = low.shape[0] // 2, low.shape[1], weight.shape[1]
    tile = min(tile, columns)
    column = lambda i: (0, i)
    rows = pl.BlockSpec((half, features), lambda i: (h, 0))
    both = pl.BlockSpec((2 * half, tile), column)
    one = pl.BlockSpec((half, tile), column)
    shape = lambda n, dtype: jax.ShapeDtypeStruct((n, columns), dtype)
    first = came is None
    cost = 2 * features * columns * 2 if first else COST
    return pl.pallas_call(
        first_kernel if first else later_kernel,
        grid=(columns // tile,),
        in_specs=[rows, rows, pl.BlockSpec((features, tile), column)] + ([] if first else [both]),
        out_specs=both if first else [one, one],
        out_shape=shape(2 * half, jnp.bfloat16)
        if first
        else [shape(half, jnp.bfloat16), shape(half, jnp.float32)],
        compiler_params=pltpu.CompilerParams(vmem_limit_bytes=VMEM_LIMIT),
        cost_estimate=pl.CostEstimate(flops=0, bytes_accessed=cost, transcendentals=0),
        name="half_product",
    )(low, high, weight, *([] if first else [came]))


def attention_kernel(
    place_ref, qm_ref, qc_ref, kc_ref, vc_ref, km_ref, kt_ref, vm_ref, vt_ref, *rest
):
    o_ref, last_ref = rest[-2:]
    length, here, first = place_ref[0], place_ref[1], place_ref[2]
    rows, block = qm_ref.shape[0], km_ref.shape[0]
    half = block // 2
    total = lambda mine, came: (mine + came.astype(jnp.float32)).astype(jnp.bfloat16)
    factor = 1.4426950408889634 / HEAD_SIZE**0.5
    row = lax.broadcasted_iota(jnp.int32, (rows, 1), 0) + here * half
    col = lax.broadcasted_iota(jnp.int32, (rows, block), 1)
    col = jnp.where(col < half, col + first * half, col - first * half)
    allowed = (col <= row) & (col < length)
    contract = (((1,), (1,)), ((), ()))
    at = row == length - 1
    keys = total(km_ref[...], kt_ref[...])
    values = total(vm_ref[...], vt_ref[...])
    stack = 2
    allowed = jnp.concatenate([allowed] * stack, axis=0)
    for member in range(0, QUERY_PER_GROUP, stack):
        each = [
            slice((member + i) * HEAD_SIZE, (member + i + 1) * HEAD_SIZE) for i in range(stack)
        ]
        q = jnp.concatenate([total(qm_ref[:, cols], qc_ref[:, cols]) for cols in each], axis=0)
        s1 = lax.dot_general(q, kc_ref[...], contract, preferred_element_type=jnp.float32)
        s2 = lax.dot_general(q, keys, contract, preferred_element_type=jnp.float32)
        s2 = jnp.where(allowed, s2, -jnp.inf)
        top = jnp.maximum(jnp.max(s1, axis=1, keepdims=True), jnp.max(s2, axis=1, keepdims=True))
        p1 = jnp.exp2((s1 - top) * factor)
        p2 = jnp.exp2((s2 - top) * factor)
        norm = jnp.sum(p1, axis=1, keepdims=True) + jnp.sum(p2, axis=1, keepdims=True)
        both = dot(p1.astype(jnp.bfloat16), vc_ref[...]) + dot(p2.astype(jnp.bfloat16), values)
        both = both / norm
        for i, cols in enumerate(each):
            out = both[i * rows : (i + 1) * rows]
            o_ref[:, cols] = out.astype(o_ref.dtype)
            last_ref[:, cols] = jnp.sum(jnp.where(at, out, 0.0), axis=0, keepdims=True).astype(
                last_ref.dtype
            )


def attend(place, q, which, k_cache, v_cache, kv, start, shape, buffer, limit):
    cols = q[0].shape[1]
    wide = QUERY_PER_GROUP * HEAD_SIZE
    cached, block = k_cache.shape[0], kv[0].shape[0]
    rows = block // 2
    heads = k_cache.shape[1] // HEAD_SIZE
    groups = cols // wide
    begin = start // wide
    column = lambda i, place: (0, begin + i)
    after = lambda i, place: (0, heads + begin + i)
    mine = lambda i, place: (which, i)
    buffers = [] if buffer is None else [buffer]
    return pl.pallas_call(
        attention_kernel,
        grid_spec=pltpu.PrefetchScalarGridSpec(
            num_scalar_prefetch=1,
            grid=(groups,),
            in_specs=[
                pl.BlockSpec((rows, wide), mine),
                pl.BlockSpec((rows, wide), mine),
                pl.BlockSpec((cached, HEAD_SIZE), column),
                pl.BlockSpec((cached, HEAD_SIZE), column),
                pl.BlockSpec((block, HEAD_SIZE), column),
                pl.BlockSpec((block, HEAD_SIZE), column),
                pl.BlockSpec((block, HEAD_SIZE), after),
                pl.BlockSpec((block, HEAD_SIZE), after),
            ]
            + [pl.BlockSpec(memory_space=pl.ANY)] * len(buffers),
            out_specs=[
                pl.BlockSpec((rows, wide), lambda i, place: (place[1], begin + i)),
                pl.BlockSpec((1, wide), lambda i, place: (0, i)),
            ],
        ),
        out_shape=[
            jax.ShapeDtypeStruct(shape, jnp.bfloat16),
            jax.ShapeDtypeStruct((1, cols), jnp.bfloat16),
        ],
        input_output_aliases={9: 0} if buffers else {},
        compiler_params=pltpu.CompilerParams(vmem_limit_bytes=limit),
        cost_estimate=pl.CostEstimate(flops=0, bytes_accessed=COST, transcendentals=0),
        name="attention",
    )(place, *q, k_cache, v_cache, *kv, *kv, *buffers)


def shards(tokens_in, w_query, w_key, w_value, stored_key_cache, stored_value_cache, prompt_len):
    n_inst, n_tp = lax.axis_size("inst"), lax.axis_size("tp")
    outer = n_inst // INNER
    me = lax.axis_index("inst")
    z, w = me // INNER, me % INNER
    x = lax.axis_index("tp")
    rows, local = tokens_in.shape
    half = rows // 2
    part = local // outer

    first = (prompt_len[0] - 1) // half

    def over_inst(value, bits):
        return lax.ppermute(value, "inst", [(i, i ^ bits) for i in range(n_inst)])

    def over_outer(value, bits):
        return over_inst(value, bits * INNER)

    def over_tp(value):
        return lax.ppermute(value, "tp", [(0, 1), (1, 0)])

    def swapped_if(flag, a, b, axis):
        return jnp.where(
            flag, jnp.concatenate([b, a], axis=axis), jnp.concatenate([a, b], axis=axis)
        )

    last_step = [None]

    def step(*values):
        if last_step[0] is not None:
            *values, _ = lax.optimization_barrier((*values, last_step[0]))
        last_step[0] = values[0]
        return values[0] if len(values) == 1 else values

    heads = w_key.shape[1] // HEAD_SIZE
    wide = QUERY_PER_GROUP * HEAD_SIZE
    pieces = 2 if heads % 2 == 0 else 1
    chunk = heads * wide // pieces
    fast = outer == 4 and n_tp == 2

    groups = [list(range(o * INNER, (o + 1) * INNER)) for o in range(outer)]

    def group_gather(value):
        return lax.all_gather(value, "inst", axis=0, tiled=True, axis_index_groups=groups)

    weights = {}

    weights["kv"] = group_gather(jnp.concatenate([w_key, w_value], axis=1))

    def gather_queries():
        source = step(w_query) if fast else w_query
        for piece in range(pieces):
            part_of = source[:, piece * chunk : (piece + 1) * chunk]
            weights[piece] = group_gather(part_of)

    tokens = {}
    if fast:

        def cut(source, j, p):
            column = (((z % 2) ^ j) * n_tp + p) * part
            return jnp.concatenate(
                [
                    lax.dynamic_slice(source, (h * half, column), (half, part))
                    for h in (first, 1 - first)
                ],
                axis=0,
            )

        swap = {1: over_tp(step(cut(tokens_in, 1, 1 - x)))}
        source = step(tokens_in)
        swap[0] = over_tp(step(cut(source, 0, 1 - x)))
        mine = z // 2 == x
        held, came = {}, {}
        swap[1] = step(swap[1])
        own = cut(source, 1, x)
        send = {b: jnp.where(mine == (b < 2), own, swap[1]) for b in (1, 3)}
        send[1], send[3] = step(send[1], send[3])
        got = {b: over_outer(send[b], b) for b in (1, 3)}
        gather_queries()

        def tp_exchange(b):
            held[b] = step(got[b])
            came[b] = over_tp(held[b])

        tp_exchange(1)
        weights["kv"] = step(weights["kv"])
        tp_exchange(3)
        swap[0] = step(swap[0])
        own = cut(source, 0, x)
        send = {b: jnp.where(mine == (b < 2), own, swap[0]) for b in (2, 0)}
        send[2] = step(send[2])
        got[2], got[0] = over_outer(send[2], 2), send[0]

        def arrived(b):
            if b not in tokens:
                tokens[b] = (swapped_if(x == 1, held[b], step(came[b]), 1),)

    else:
        gather_queries()
        swapped = jnp.where(first == 1, jnp.roll(tokens_in, half, axis=0), tokens_in)
        own = swapped.reshape(rows, outer // n_tp, n_tp, part)
        parts = lax.all_to_all(own, "tp", 2, 1, tiled=True).reshape(rows, outer, part)
        come = jnp.stack(
            [
                over_outer(lax.dynamic_index_in_dim(parts, z ^ b, 1, keepdims=False), b)
                for b in range(outer)
            ]
        )
        both = lax.all_gather(come.reshape(-1, part), "tp", axis=1, tiled=True)
        both = both.reshape(outer, rows, -1)
        tokens.update({b: (both[b],) for b in range(outer)})

        def arrived(b):
            pass

    def rows_of(values, h):
        if h is None:
            return values
        return tuple(value[h * half : (h + 1) * half] for value in values)

    def times(values, weight):
        total, row = None, 0
        for value in values:
            one = dot(value, weight[row : row + value.shape[1]])
            total = one if total is None else total + one
            row += value.shape[1]
        return total

    def first_send(h, name):
        weight = weights[name] = step(weights[name])
        bits = range(1, outer, 2)
        if h is None:
            come = {}
            for b in bits:
                arrived(b)
                come[b] = over_outer(step(times(tokens[b], weight).astype(jnp.bfloat16)), 1)
            return come
        if fast:
            send = half_product(tokens[1][0], tokens[3][0], h, weight)
            return over_outer(step(send), 1)
        joined = [jnp.concatenate(same) for same in zip(*[rows_of(tokens[b], h) for b in bits])]
        come = over_outer(step(times(joined, weight).astype(jnp.bfloat16)), 1)
        return {b: (come, i) for i, b in enumerate(bits)}

    def later_sends(h, name, come):
        weight = weights[name]
        arrived(0)
        if fast and h is not None:
            send, keep = half_product(tokens[0][0], tokens[2][0], h, weight, step(come))
            send, keep = step(send, keep)
            return keep, over_outer(send, 2)
        if h is None:
            bits = list(come)
            come = dict(zip(bits, step(*[come[b] for b in bits])))
            arrived(2)
        else:
            whole = step(next(iter(come.values()))[0])
            come = {b: whole[i * half : (i + 1) * half] for b, (_, i) in come.items()}

        def total(b, arrival):
            return times(rows_of(tokens[b], h), weight) + arrival.astype(jnp.float32)

        if outer == 4:
            moved = over_outer(step(total(2, come[3]).astype(jnp.bfloat16)), 2)
            return total(0, step(come[1])), moved
        sums = {b: total(b, come[b + 1]) for b in range(0, outer, 2)}
        bit = 2
        while True:
            for b in sorted(sums):
                if b & bit:
                    moved = over_outer(step(sums.pop(b).astype(jnp.bfloat16)), bit)
                    if 2 * bit == outer:
                        return sums[0], moved
                    sums[b ^ bit] = sums[b ^ bit] + moved.astype(jnp.float32)
            bit *= 2

    jobs = [(None, "kv")] + ([(None, 0)] if pieces == 2 else [])
    jobs += [(0, pieces - 1), (1, pieces - 1)]
    opened, parts_of, lasts = {}, {}, []
    attended = [None]

    def start(n):
        opened[n] = first_send(*jobs[n])

    def advance(n):
        parts_of[n] = later_sends(*jobs[n], opened[n])

    def arrive(n):
        came_in, mine = step(parts_of[n][1], parts_of[n][0])
        parts_of[n] = (mine, came_in)

    def attention(n, h):
        own_half, piece = jobs[n]
        which = h if own_half is None else 0
        place = jnp.stack([prompt_len[0], h ^ first, first]).astype(jnp.int32)
        caches = (stored_key_cache, stored_value_cache)
        shape = (rows, heads * wide)
        limit = VMEM_LIMIT if n < len(jobs) - 1 else 56 * 1024 * 1024
        where = (piece * chunk, shape, attended[0], limit)
        attended[0], last = attend(place, parts_of[n], which, *caches, parts_of[0], *where)
        lasts.append(step(last))

    def from_xor_order(values, index):
        out = jnp.stack(values)
        shape = out.shape
        bits = len(values).bit_length() - 1
        for bit in range(bits):
            out = out.reshape(len(values) >> (bit + 1), 2, 1 << bit, *shape[1:])
            out = jnp.where((index >> bit) % 2 == 1, out[:, ::-1], out)
        return out.reshape(shape)

    start(0)
    if fast:
        tp_exchange(0)
        tp_exchange(2)
    start(1)
    advance(0)
    if pieces == 2:
        weights[1] = step(weights[1])
        advance(1)
        start(2)
        arrive(0)
        arrive(1)
        advance(2)
        start(3)
        attention(1, 0)
        attention(1, 1)
        advance(3)
        arrive(2)
        attention(2, 0)
        row = jnp.concatenate([lasts[0] + lasts[1], lasts[2]], axis=1)
    else:
        start(2)
        advance(1)
        arrive(0)
        advance(2)
        arrive(1)
        attention(1, 0)
        row = lasts[0]
    row = step(row)
    in_group = [row] + [over_inst(row, m) for m in range(1, INNER)]
    arrive(len(jobs) - 1)
    in_group[1] = step(in_group[1])
    in_group = from_xor_order(in_group, w)
    over_all = [in_group] + [over_outer(in_group, b) for b in range(1, outer)]
    attention(len(jobs) - 1, 1)
    over_all[1] = step(over_all[1])
    handoff = from_xor_order(over_all, z).reshape(n_inst, heads * wide)
    return (attended[0], handoff)


def solution(mesh):
    return jax.shard_map(
        shards,
        mesh=mesh,
        in_specs=(
            P("inst", "tp"),
            P("inst", "tp"),
            P("inst", "tp"),
            P("inst", "tp"),
            P("inst", "tp"),
            P("inst", "tp"),
            P("inst"),
        ),
        out_specs=(P("inst", "tp"), P(None, "tp")),
        check_vma=False,
    )
```

```python
import jax
import jax.numpy as jnp
from jax import lax
from jax.experimental import pallas as pl
from jax.experimental.pallas import tpu as pltpu
from jax.sharding import PartitionSpec as P

HEAD_SIZE = 128
QUERY_PER_GROUP = 4
VMEM_LIMIT = 32 * 1024 * 1024
COST = 1 << 10
INNER = 4


def dot(a, b):
    return jnp.dot(a, b, preferred_element_type=jnp.float32)


def first_kernel(low_ref, high_ref, w_ref, send_ref):
    t = jnp.concatenate([low_ref[...], high_ref[...]], axis=0)
    send_ref[...] = dot(t, w_ref[...]).astype(send_ref.dtype)


def later_kernel(low_ref, high_ref, w_ref, came_ref, send_ref, keep_ref):
    t = jnp.concatenate([low_ref[...], high_ref[...]], axis=0)
    out = dot(t, w_ref[...]) + came_ref[...].astype(jnp.float32)
    n = keep_ref.shape[0]
    keep_ref[...] = out[:n]
    send_ref[...] = out[n:].astype(send_ref.dtype)


def half_product(low, high, h, weight, came=None, tile=512):
    half, features, columns = low.shape[0] // 2, low.shape[1], weight.shape[1]
    tile = min(tile, columns)
    column = lambda i: (0, i)
    rows = pl.BlockSpec((half, features), lambda i: (h, 0))
    both = pl.BlockSpec((2 * half, tile), column)
    one = pl.BlockSpec((half, tile), column)
    shape = lambda n, dtype: jax.ShapeDtypeStruct((n, columns), dtype)
    first = came is None
    cost = 2 * features * columns * 2 if first else COST
    return pl.pallas_call(
        first_kernel if first else later_kernel,
        grid=(columns // tile,),
        in_specs=[rows, rows, pl.BlockSpec((features, tile), column)] + ([] if first else [both]),
        out_specs=both if first else [one, one],
        out_shape=shape(2 * half, jnp.bfloat16)
        if first
        else [shape(half, jnp.bfloat16), shape(half, jnp.float32)],
        compiler_params=pltpu.CompilerParams(vmem_limit_bytes=VMEM_LIMIT),
        cost_estimate=pl.CostEstimate(flops=0, bytes_accessed=cost, transcendentals=0),
        name="half_product",
    )(low, high, weight, *([] if first else [came]))


def attention_kernel(
    place_ref, qm_ref, qc_ref, kc_ref, vc_ref, km_ref, kt_ref, vm_ref, vt_ref, *rest
):
    o_ref, last_ref = rest[-2:]
    length, here, first = place_ref[0], place_ref[1], place_ref[2]
    rows, block = qm_ref.shape[0], km_ref.shape[0]
    half = block // 2
    total = lambda mine, came: (mine + came.astype(jnp.float32)).astype(jnp.bfloat16)
    factor = 1.4426950408889634 / HEAD_SIZE**0.5
    row = lax.broadcasted_iota(jnp.int32, (rows, 1), 0) + here * half
    col = lax.broadcasted_iota(jnp.int32, (rows, block), 1)
    col = jnp.where(col < half, col + first * half, col - first * half)
    allowed = (col <= row) & (col < length)
    contract = (((1,), (1,)), ((), ()))
    at = row == length - 1
    keys = total(km_ref[...], kt_ref[...])
    values = total(vm_ref[...], vt_ref[...])
    stack = 2
    allowed = jnp.concatenate([allowed] * stack, axis=0)
    for member in range(0, QUERY_PER_GROUP, stack):
        each = [
            slice((member + i) * HEAD_SIZE, (member + i + 1) * HEAD_SIZE) for i in range(stack)
        ]
        q = jnp.concatenate([total(qm_ref[:, cols], qc_ref[:, cols]) for cols in each], axis=0)
        s1 = lax.dot_general(q, kc_ref[...], contract, preferred_element_type=jnp.float32)
        s2 = lax.dot_general(q, keys, contract, preferred_element_type=jnp.float32)
        s2 = jnp.where(allowed, s2, -jnp.inf)
        top = jnp.maximum(jnp.max(s1, axis=1, keepdims=True), jnp.max(s2, axis=1, keepdims=True))
        p1 = jnp.exp2((s1 - top) * factor)
        p2 = jnp.exp2((s2 - top) * factor)
        norm = jnp.sum(p1, axis=1, keepdims=True) + jnp.sum(p2, axis=1, keepdims=True)
        both = dot(p1.astype(jnp.bfloat16), vc_ref[...]) + dot(p2.astype(jnp.bfloat16), values)
        both = both / norm
        for i, cols in enumerate(each):
            out = both[i * rows : (i + 1) * rows]
            o_ref[:, cols] = out.astype(o_ref.dtype)
            last_ref[:, cols] = jnp.sum(jnp.where(at, out, 0.0), axis=0, keepdims=True).astype(
                last_ref.dtype
            )


def attend(place, q, which, k_cache, v_cache, kv, start, shape, buffer, limit):
    cols = q[0].shape[1]
    wide = QUERY_PER_GROUP * HEAD_SIZE
    cached, block = k_cache.shape[0], kv[0].shape[0]
    rows = block // 2
    heads = k_cache.shape[1] // HEAD_SIZE
    groups = cols // wide
    begin = start // wide
    column = lambda i, place: (0, begin + i)
    after = lambda i, place: (0, heads + begin + i)
    mine = lambda i, place: (which, i)
    buffers = [] if buffer is None else [buffer]
    return pl.pallas_call(
        attention_kernel,
        grid_spec=pltpu.PrefetchScalarGridSpec(
            num_scalar_prefetch=1,
            grid=(groups,),
            in_specs=[
                pl.BlockSpec((rows, wide), mine),
                pl.BlockSpec((rows, wide), mine),
                pl.BlockSpec((cached, HEAD_SIZE), column),
                pl.BlockSpec((cached, HEAD_SIZE), column),
                pl.BlockSpec((block, HEAD_SIZE), column),
                pl.BlockSpec((block, HEAD_SIZE), column),
                pl.BlockSpec((block, HEAD_SIZE), after),
                pl.BlockSpec((block, HEAD_SIZE), after),
            ]
            + [pl.BlockSpec(memory_space=pl.ANY)] * len(buffers),
            out_specs=[
                pl.BlockSpec((rows, wide), lambda i, place: (place[1], begin + i)),
                pl.BlockSpec((1, wide), lambda i, place: (0, i)),
            ],
        ),
        out_shape=[
            jax.ShapeDtypeStruct(shape, jnp.bfloat16),
            jax.ShapeDtypeStruct((1, cols), jnp.bfloat16),
        ],
        input_output_aliases={9: 0} if buffers else {},
        compiler_params=pltpu.CompilerParams(vmem_limit_bytes=limit),
        cost_estimate=pl.CostEstimate(flops=0, bytes_accessed=COST, transcendentals=0),
        name="attention",
    )(place, *q, k_cache, v_cache, *kv, *kv, *buffers)


def shards(tokens_in, w_query, w_key, w_value, stored_key_cache, stored_value_cache, prompt_len):
    n_inst, n_tp = lax.axis_size("inst"), lax.axis_size("tp")
    outer = n_inst // INNER
    me = lax.axis_index("inst")
    z, w = me // INNER, me % INNER
    x = lax.axis_index("tp")
    rows, local = tokens_in.shape
    half = rows // 2
    part = local // outer

    first = (prompt_len[0] - 1) // half

    def over_inst(value, bits):
        return lax.ppermute(value, "inst", [(i, i ^ bits) for i in range(n_inst)])

    def over_outer(value, bits):
        return over_inst(value, bits * INNER)

    def over_tp(value):
        return lax.ppermute(value, "tp", [(0, 1), (1, 0)])

    def swapped_if(flag, a, b, axis):
        return jnp.where(
            flag, jnp.concatenate([b, a], axis=axis), jnp.concatenate([a, b], axis=axis)
        )

    last_step = [None]

    def step(*values):
        if last_step[0] is not None:
            *values, _ = lax.optimization_barrier((*values, last_step[0]))
        last_step[0] = values[0]
        return values[0] if len(values) == 1 else values

    heads = w_key.shape[1] // HEAD_SIZE
    wide = QUERY_PER_GROUP * HEAD_SIZE
    pieces = 2 if heads % 2 == 0 else 1
    chunk = heads * wide // pieces
    fast = outer == 4 and n_tp == 2

    groups = [list(range(o * INNER, (o + 1) * INNER)) for o in range(outer)]

    def group_gather(value):
        return lax.all_gather(value, "inst", axis=0, tiled=True, axis_index_groups=groups)

    weights = {}

    weights["kv"] = group_gather(jnp.concatenate([w_key, w_value], axis=1))

    def gather_queries():
        source = step(w_query) if fast else w_query
        for piece in range(pieces):
            part_of = source[:, piece * chunk : (piece + 1) * chunk]
            weights[piece] = group_gather(part_of)

    tokens = {}
    if fast:

        def cut(source, j, p):
            column = (((z % 2) ^ j) * n_tp + p) * part
            return jnp.concatenate(
                [
                    lax.dynamic_slice(source, (h * half, column), (half, part))
                    for h in (first, 1 - first)
                ],
                axis=0,
            )

        swap = {1: over_tp(step(cut(tokens_in, 1, 1 - x)))}
        source = step(tokens_in)
        swap[0] = over_tp(step(cut(source, 0, 1 - x)))
        mine = z // 2 == x
        held, came = {}, {}
        swap[1] = step(swap[1])
        own = cut(source, 1, x)
        send = {b: jnp.where(mine == (b < 2), own, swap[1]) for b in (1, 3)}
        send[1], send[3] = step(send[1], send[3])
        got = {b: over_outer(send[b], b) for b in (1, 3)}
        gather_queries()

        def tp_exchange(b):
            held[b] = step(got[b])
            came[b] = over_tp(held[b])

        tp_exchange(1)
        weights["kv"] = step(weights["kv"])
        tp_exchange(3)
        swap[0] = step(swap[0])
        own = cut(source, 0, x)
        send = {b: jnp.where(mine == (b < 2), own, swap[0]) for b in (2, 0)}
        send[2] = step(send[2])
        got[2], got[0] = over_outer(send[2], 2), send[0]

        def arrived(b):
            if b not in tokens:
                tokens[b] = (swapped_if(x == 1, held[b], step(came[b]), 1),)

    else:
        gather_queries()
        swapped = jnp.where(first == 1, jnp.roll(tokens_in, half, axis=0), tokens_in)
        own = swapped.reshape(rows, outer // n_tp, n_tp, part)
        parts = lax.all_to_all(own, "tp", 2, 1, tiled=True).reshape(rows, outer, part)
        come = jnp.stack(
            [
                over_outer(lax.dynamic_index_in_dim(parts, z ^ b, 1, keepdims=False), b)
                for b in range(outer)
            ]
        )
        both = lax.all_gather(come.reshape(-1, part), "tp", axis=1, tiled=True)
        both = both.reshape(outer, rows, -1)
        tokens.update({b: (both[b],) for b in range(outer)})

        def arrived(b):
            pass

    def rows_of(values, h):
        if h is None:
            return values
        return tuple(value[h * half : (h + 1) * half] for value in values)

    def times(values, weight):
        total, row = None, 0
        for value in values:
            one = dot(value, weight[row : row + value.shape[1]])
            total = one if total is None else total + one
            row += value.shape[1]
        return total

    def first_send(h, name):
        weight = weights[name] = step(weights[name])
        bits = range(1, outer, 2)
        if h is None:
            come = {}
            for b in bits:
                arrived(b)
                come[b] = over_outer(step(times(tokens[b], weight).astype(jnp.bfloat16)), 1)
            return come
        if fast:
            send = half_product(tokens[1][0], tokens[3][0], h, weight)
            return over_outer(step(send), 1)
        joined = [jnp.concatenate(same) for same in zip(*[rows_of(tokens[b], h) for b in bits])]
        come = over_outer(step(times(joined, weight).astype(jnp.bfloat16)), 1)
        return {b: (come, i) for i, b in enumerate(bits)}

    def later_sends(h, name, come):
        weight = weights[name]
        arrived(0)
        if fast and h is not None:
            send, keep = half_product(tokens[0][0], tokens[2][0], h, weight, step(come))
            send, keep = step(send, keep)
            return keep, over_outer(send, 2)
        if h is None:
            bits = list(come)
            come = dict(zip(bits, step(*[come[b] for b in bits])))
            arrived(2)
        else:
            whole = step(next(iter(come.values()))[0])
            come = {b: whole[i * half : (i + 1) * half] for b, (_, i) in come.items()}

        def total(b, arrival):
            return times(rows_of(tokens[b], h), weight) + arrival.astype(jnp.float32)

        if outer == 4:
            moved = over_outer(step(total(2, come[3]).astype(jnp.bfloat16)), 2)
            return total(0, step(come[1])), moved
        sums = {b: total(b, come[b + 1]) for b in range(0, outer, 2)}
        bit = 2
        while True:
            for b in sorted(sums):
                if b & bit:
                    moved = over_outer(step(sums.pop(b).astype(jnp.bfloat16)), bit)
                    if 2 * bit == outer:
                        return sums[0], moved
                    sums[b ^ bit] = sums[b ^ bit] + moved.astype(jnp.float32)
            bit *= 2

    jobs = [(None, "kv")] + ([(None, 0)] if pieces == 2 else [])
    jobs += [(0, pieces - 1), (1, pieces - 1)]
    opened, parts_of, lasts = {}, {}, []
    attended = [None]

    def start(n):
        opened[n] = first_send(*jobs[n])

    def advance(n):
        parts_of[n] = later_sends(*jobs[n], opened[n])

    def arrive(n):
        came_in, mine = step(parts_of[n][1], parts_of[n][0])
        parts_of[n] = (mine, came_in)

    def attention(n, h):
        own_half, piece = jobs[n]
        which = h if own_half is None else 0
        place = jnp.stack([prompt_len[0], h ^ first, first]).astype(jnp.int32)
        caches = (stored_key_cache, stored_value_cache)
        shape = (rows, heads * wide)
        limit = VMEM_LIMIT if n < len(jobs) - 1 else 56 * 1024 * 1024
        where = (piece * chunk, shape, attended[0], limit)
        attended[0], last = attend(place, parts_of[n], which, *caches, parts_of[0], *where)
        lasts.append(step(last))

    def from_xor_order(values, index):
        out = jnp.stack(values)
        shape = out.shape
        bits = len(values).bit_length() - 1
        for bit in range(bits):
            out = out.reshape(len(values) >> (bit + 1), 2, 1 << bit, *shape[1:])
            out = jnp.where((index >> bit) % 2 == 1, out[:, ::-1], out)
        return out.reshape(shape)

    start(0)
    if fast:
        tp_exchange(0)
        tp_exchange(2)
    start(1)
    advance(0)
    if pieces == 2:
        weights[1] = step(weights[1])
        start(2)
        advance(1)
        arrive(0)
        advance(2)
        start(3)
        arrive(1)
        attention(1, 0)
        attention(1, 1)
        advance(3)
        arrive(2)
        attention(2, 0)
        row = jnp.concatenate([lasts[0] + lasts[1], lasts[2]], axis=1)
    else:
        start(2)
        advance(1)
        arrive(0)
        advance(2)
        arrive(1)
        attention(1, 0)
        row = lasts[0]
    row = step(row)
    in_group = [row] + [over_inst(row, m) for m in range(1, INNER)]
    arrive(len(jobs) - 1)
    in_group[1] = step(in_group[1])
    in_group = from_xor_order(in_group, w)
    over_all = [in_group] + [over_outer(in_group, b) for b in range(1, outer)]
    attention(len(jobs) - 1, 1)
    over_all[1] = step(over_all[1])
    handoff = from_xor_order(over_all, z).reshape(n_inst, heads * wide)
    return (attended[0], handoff)


def solution(mesh):
    return jax.shard_map(
        shards,
        mesh=mesh,
        in_specs=(
            P("inst", "tp"),
            P("inst", "tp"),
            P("inst", "tp"),
            P("inst", "tp"),
            P("inst", "tp"),
            P("inst", "tp"),
            P("inst"),
        ),
        out_specs=(P("inst", "tp"), P(None, "tp")),
        check_vma=False,
    )
```

```python
import jax
import jax.numpy as jnp
from jax import lax
from jax.experimental import pallas as pl
from jax.experimental.pallas import tpu as pltpu
from jax.sharding import PartitionSpec as P

HEAD_SIZE = 128
QUERY_PER_GROUP = 4
VMEM_LIMIT = 32 * 1024 * 1024
COST = 1 << 10
INNER = 4


def dot(a, b):
    return jnp.dot(a, b, preferred_element_type=jnp.float32)


def first_kernel(low_ref, high_ref, w_ref, send_ref):
    t = jnp.concatenate([low_ref[...], high_ref[...]], axis=0)
    send_ref[...] = dot(t, w_ref[...]).astype(send_ref.dtype)


def later_kernel(low_ref, high_ref, w_ref, came_ref, send_ref, keep_ref):
    t = jnp.concatenate([low_ref[...], high_ref[...]], axis=0)
    out = dot(t, w_ref[...]) + came_ref[...].astype(jnp.float32)
    n = keep_ref.shape[0]
    keep_ref[...] = out[:n]
    send_ref[...] = out[n:].astype(send_ref.dtype)


def half_product(low, high, h, weight, came=None, tile=512):
    half, features, columns = low.shape[0] // 2, low.shape[1], weight.shape[1]
    tile = min(tile, columns)
    column = lambda i: (0, i)
    rows = pl.BlockSpec((half, features), lambda i: (h, 0))
    both = pl.BlockSpec((2 * half, tile), column)
    one = pl.BlockSpec((half, tile), column)
    shape = lambda n, dtype: jax.ShapeDtypeStruct((n, columns), dtype)
    first = came is None
    cost = 2 * features * columns * 2 if first else COST
    return pl.pallas_call(
        first_kernel if first else later_kernel,
        grid=(columns // tile,),
        in_specs=[rows, rows, pl.BlockSpec((features, tile), column)] + ([] if first else [both]),
        out_specs=both if first else [one, one],
        out_shape=shape(2 * half, jnp.bfloat16)
        if first
        else [shape(half, jnp.bfloat16), shape(half, jnp.float32)],
        compiler_params=pltpu.CompilerParams(vmem_limit_bytes=VMEM_LIMIT),
        cost_estimate=pl.CostEstimate(flops=0, bytes_accessed=cost, transcendentals=0),
        name="half_product",
    )(low, high, weight, *([] if first else [came]))


def attention_kernel(
    place_ref, qm_ref, qc_ref, kc_ref, vc_ref, km_ref, kt_ref, vm_ref, vt_ref, *rest
):
    o_ref, last_ref = rest[-2:]
    length, here, first = place_ref[0], place_ref[1], place_ref[2]
    rows, block = qm_ref.shape[0], km_ref.shape[0]
    half = block // 2
    total = lambda mine, came: (mine + came.astype(jnp.float32)).astype(jnp.bfloat16)
    factor = 1.4426950408889634 / HEAD_SIZE**0.5
    row = lax.broadcasted_iota(jnp.int32, (rows, 1), 0) + here * half
    col = lax.broadcasted_iota(jnp.int32, (rows, block), 1)
    col = jnp.where(col < half, col + first * half, col - first * half)
    allowed = (col <= row) & (col < length)
    contract = (((1,), (1,)), ((), ()))
    at = row == length - 1
    keys = total(km_ref[...], kt_ref[...])
    values = total(vm_ref[...], vt_ref[...])
    stack = 2
    allowed = jnp.concatenate([allowed] * stack, axis=0)
    for member in range(0, QUERY_PER_GROUP, stack):
        each = [
            slice((member + i) * HEAD_SIZE, (member + i + 1) * HEAD_SIZE) for i in range(stack)
        ]
        q = jnp.concatenate([total(qm_ref[:, cols], qc_ref[:, cols]) for cols in each], axis=0)
        s1 = lax.dot_general(q, kc_ref[...], contract, preferred_element_type=jnp.float32)
        s2 = lax.dot_general(q, keys, contract, preferred_element_type=jnp.float32)
        s2 = jnp.where(allowed, s2, -jnp.inf)
        top = jnp.maximum(jnp.max(s1, axis=1, keepdims=True), jnp.max(s2, axis=1, keepdims=True))
        p1 = jnp.exp2((s1 - top) * factor)
        p2 = jnp.exp2((s2 - top) * factor)
        norm = jnp.sum(p1, axis=1, keepdims=True) + jnp.sum(p2, axis=1, keepdims=True)
        both = dot(p1.astype(jnp.bfloat16), vc_ref[...]) + dot(p2.astype(jnp.bfloat16), values)
        both = both / norm
        for i, cols in enumerate(each):
            out = both[i * rows : (i + 1) * rows]
            o_ref[:, cols] = out.astype(o_ref.dtype)
            last_ref[:, cols] = jnp.sum(jnp.where(at, out, 0.0), axis=0, keepdims=True).astype(
                last_ref.dtype
            )


def attend(place, q, which, k_cache, v_cache, kv, start, shape, buffer, limit):
    cols = q[0].shape[1]
    wide = QUERY_PER_GROUP * HEAD_SIZE
    cached, block = k_cache.shape[0], kv[0].shape[0]
    rows = block // 2
    heads = k_cache.shape[1] // HEAD_SIZE
    groups = cols // wide
    begin = start // wide
    column = lambda i, place: (0, begin + i)
    after = lambda i, place: (0, heads + begin + i)
    mine = lambda i, place: (which, i)
    buffers = [] if buffer is None else [buffer]
    return pl.pallas_call(
        attention_kernel,
        grid_spec=pltpu.PrefetchScalarGridSpec(
            num_scalar_prefetch=1,
            grid=(groups,),
            in_specs=[
                pl.BlockSpec((rows, wide), mine),
                pl.BlockSpec((rows, wide), mine),
                pl.BlockSpec((cached, HEAD_SIZE), column),
                pl.BlockSpec((cached, HEAD_SIZE), column),
                pl.BlockSpec((block, HEAD_SIZE), column),
                pl.BlockSpec((block, HEAD_SIZE), column),
                pl.BlockSpec((block, HEAD_SIZE), after),
                pl.BlockSpec((block, HEAD_SIZE), after),
            ]
            + [pl.BlockSpec(memory_space=pl.ANY)] * len(buffers),
            out_specs=[
                pl.BlockSpec((rows, wide), lambda i, place: (place[1], begin + i)),
                pl.BlockSpec((1, wide), lambda i, place: (0, i)),
            ],
        ),
        out_shape=[
            jax.ShapeDtypeStruct(shape, jnp.bfloat16),
            jax.ShapeDtypeStruct((1, cols), jnp.bfloat16),
        ],
        input_output_aliases={9: 0} if buffers else {},
        compiler_params=pltpu.CompilerParams(vmem_limit_bytes=limit),
        cost_estimate=pl.CostEstimate(flops=0, bytes_accessed=COST, transcendentals=0),
        name="attention",
    )(place, *q, k_cache, v_cache, *kv, *kv, *buffers)


def shards(tokens_in, w_query, w_key, w_value, stored_key_cache, stored_value_cache, prompt_len):
    n_inst, n_tp = lax.axis_size("inst"), lax.axis_size("tp")
    outer = n_inst // INNER
    me = lax.axis_index("inst")
    z, w = me // INNER, me % INNER
    x = lax.axis_index("tp")
    rows, local = tokens_in.shape
    half = rows // 2
    part = local // outer

    first = (prompt_len[0] - 1) // half

    def over_inst(value, bits):
        return lax.ppermute(value, "inst", [(i, i ^ bits) for i in range(n_inst)])

    def over_outer(value, bits):
        return over_inst(value, bits * INNER)

    def over_tp(value):
        return lax.ppermute(value, "tp", [(0, 1), (1, 0)])

    def swapped_if(flag, a, b, axis):
        return jnp.where(
            flag, jnp.concatenate([b, a], axis=axis), jnp.concatenate([a, b], axis=axis)
        )

    last_step = [None]

    def step(*values):
        if last_step[0] is not None:
            *values, _ = lax.optimization_barrier((*values, last_step[0]))
        last_step[0] = values[0]
        return values[0] if len(values) == 1 else values

    heads = w_key.shape[1] // HEAD_SIZE
    wide = QUERY_PER_GROUP * HEAD_SIZE
    pieces = 2 if heads % 2 == 0 else 1
    chunk = heads * wide // pieces
    fast = outer == 4 and n_tp == 2

    groups = [list(range(o * INNER, (o + 1) * INNER)) for o in range(outer)]

    def group_gather(value):
        return lax.all_gather(value, "inst", axis=0, tiled=True, axis_index_groups=groups)

    weights = {}

    weights["kv"] = group_gather(jnp.concatenate([w_key, w_value], axis=1))

    def gather_queries():
        source = step(w_query) if fast else w_query
        for piece in range(pieces):
            part_of = source[:, piece * chunk : (piece + 1) * chunk]
            weights[piece] = group_gather(part_of)

    tokens = {}
    if fast:

        def cut(source, j, p):
            column = (((z % 2) ^ j) * n_tp + p) * part
            return jnp.concatenate(
                [
                    lax.dynamic_slice(source, (h * half, column), (half, part))
                    for h in (first, 1 - first)
                ],
                axis=0,
            )

        swap = {1: over_tp(step(cut(tokens_in, 1, 1 - x)))}
        source = step(tokens_in)
        swap[0] = over_tp(step(cut(source, 0, 1 - x)))
        mine = z // 2 == x
        held, came = {}, {}
        swap[1] = step(swap[1])
        own = cut(source, 1, x)
        send = {b: jnp.where(mine == (b < 2), own, swap[1]) for b in (1, 3)}
        send[1], send[3] = step(send[1], send[3])
        got = {b: over_outer(send[b], b) for b in (1, 3)}
        gather_queries()

        def tp_exchange(b):
            held[b] = step(got[b])
            came[b] = over_tp(held[b])

        tp_exchange(1)
        weights["kv"] = step(weights["kv"])
        tp_exchange(3)
        swap[0] = step(swap[0])
        own = cut(source, 0, x)
        send = {b: jnp.where(mine == (b < 2), own, swap[0]) for b in (2, 0)}
        send[2] = step(send[2])
        got[2], got[0] = over_outer(send[2], 2), send[0]

        def arrived(b):
            if b not in tokens:
                tokens[b] = (swapped_if(x == 1, held[b], step(came[b]), 1),)

    else:
        gather_queries()
        swapped = jnp.where(first == 1, jnp.roll(tokens_in, half, axis=0), tokens_in)
        own = swapped.reshape(rows, outer // n_tp, n_tp, part)
        parts = lax.all_to_all(own, "tp", 2, 1, tiled=True).reshape(rows, outer, part)
        come = jnp.stack(
            [
                over_outer(lax.dynamic_index_in_dim(parts, z ^ b, 1, keepdims=False), b)
                for b in range(outer)
            ]
        )
        both = lax.all_gather(come.reshape(-1, part), "tp", axis=1, tiled=True)
        both = both.reshape(outer, rows, -1)
        tokens.update({b: (both[b],) for b in range(outer)})

        def arrived(b):
            pass

    def rows_of(values, h):
        if h is None:
            return values
        return tuple(value[h * half : (h + 1) * half] for value in values)

    def times(values, weight):
        total, row = None, 0
        for value in values:
            one = dot(value, weight[row : row + value.shape[1]])
            total = one if total is None else total + one
            row += value.shape[1]
        return total

    def first_send(h, name):
        weight = weights[name] = step(weights[name])
        bits = range(1, outer, 2)
        if h is None:
            come = {}
            for b in bits:
                arrived(b)
                come[b] = over_outer(step(times(tokens[b], weight).astype(jnp.bfloat16)), 1)
            return come
        if fast:
            send = half_product(tokens[1][0], tokens[3][0], h, weight)
            return over_outer(step(send), 1)
        joined = [jnp.concatenate(same) for same in zip(*[rows_of(tokens[b], h) for b in bits])]
        come = over_outer(step(times(joined, weight).astype(jnp.bfloat16)), 1)
        return {b: (come, i) for i, b in enumerate(bits)}

    def later_sends(h, name, come):
        weight = weights[name]
        arrived(0)
        arrived(2)
        if fast and h is not None:
            send, keep = half_product(tokens[0][0], tokens[2][0], h, weight, step(come))
            send, keep = step(send, keep)
            return keep, over_outer(send, 2)
        if h is None:
            bits = list(come)
            come = dict(zip(bits, step(*[come[b] for b in bits])))
        else:
            whole = step(next(iter(come.values()))[0])
            come = {b: whole[i * half : (i + 1) * half] for b, (_, i) in come.items()}

        def total(b, arrival):
            return times(rows_of(tokens[b], h), weight) + arrival.astype(jnp.float32)

        if outer == 4:
            moved = over_outer(step(total(2, come[3]).astype(jnp.bfloat16)), 2)
            return total(0, step(come[1])), moved
        sums = {b: total(b, come[b + 1]) for b in range(0, outer, 2)}
        bit = 2
        while True:
            for b in sorted(sums):
                if b & bit:
                    moved = over_outer(step(sums.pop(b).astype(jnp.bfloat16)), bit)
                    if 2 * bit == outer:
                        return sums[0], moved
                    sums[b ^ bit] = sums[b ^ bit] + moved.astype(jnp.float32)
            bit *= 2

    jobs = [(None, "kv")] + ([(None, 0)] if pieces == 2 else [])
    jobs += [(0, pieces - 1), (1, pieces - 1)]
    opened, parts_of, lasts = {}, {}, []
    attended = [None]

    def start(n):
        opened[n] = first_send(*jobs[n])

    def advance(n):
        parts_of[n] = later_sends(*jobs[n], opened[n])

    def arrive(n):
        came_in, mine = step(parts_of[n][1], parts_of[n][0])
        parts_of[n] = (mine, came_in)

    def attention(n, h):
        own_half, piece = jobs[n]
        which = h if own_half is None else 0
        place = jnp.stack([prompt_len[0], h ^ first, first]).astype(jnp.int32)
        caches = (stored_key_cache, stored_value_cache)
        shape = (rows, heads * wide)
        limit = VMEM_LIMIT if n < len(jobs) - 1 else 56 * 1024 * 1024
        where = (piece * chunk, shape, attended[0], limit)
        attended[0], last = attend(place, parts_of[n], which, *caches, parts_of[0], *where)
        lasts.append(step(last))

    def from_xor_order(values, index):
        out = jnp.stack(values)
        shape = out.shape
        bits = len(values).bit_length() - 1
        for bit in range(bits):
            out = out.reshape(len(values) >> (bit + 1), 2, 1 << bit, *shape[1:])
            out = jnp.where((index >> bit) % 2 == 1, out[:, ::-1], out)
        return out.reshape(shape)

    start(0)
    if fast:
        tp_exchange(0)
        tp_exchange(2)
    start(1)
    advance(0)
    if pieces == 2:
        weights[1] = step(weights[1])
        start(2)
        advance(1)
        start(3)
        arrive(0)
        advance(2)
        arrive(1)
        attention(1, 0)
        advance(3)
        attention(1, 1)
        arrive(2)
        attention(2, 0)
        row = jnp.concatenate([lasts[0] + lasts[1], lasts[2]], axis=1)
    else:
        start(2)
        advance(1)
        arrive(0)
        advance(2)
        arrive(1)
        attention(1, 0)
        row = lasts[0]
    row = step(row)
    in_group = [row] + [over_inst(row, m) for m in range(1, INNER)]
    arrive(len(jobs) - 1)
    in_group[1] = step(in_group[1])
    in_group = from_xor_order(in_group, w)
    over_all = [in_group] + [over_outer(in_group, b) for b in range(1, outer)]
    attention(len(jobs) - 1, 1)
    over_all[1] = step(over_all[1])
    handoff = from_xor_order(over_all, z).reshape(n_inst, heads * wide)
    return (attended[0], handoff)


def solution(mesh):
    return jax.shard_map(
        shards,
        mesh=mesh,
        in_specs=(
            P("inst", "tp"),
            P("inst", "tp"),
            P("inst", "tp"),
            P("inst", "tp"),
            P("inst", "tp"),
            P("inst", "tp"),
            P("inst"),
        ),
        out_specs=(P("inst", "tp"), P(None, "tp")),
        check_vma=False,
    )
```

```python
import jax
import jax.numpy as jnp
from jax import lax
from jax.experimental import pallas as pl
from jax.experimental.pallas import tpu as pltpu
from jax.sharding import PartitionSpec as P

HEAD_SIZE = 128
QUERY_PER_GROUP = 4
VMEM_LIMIT = 32 * 1024 * 1024
COST = 1 << 10
INNER = 4


def dot(a, b):
    return jnp.dot(a, b, preferred_element_type=jnp.float32)


def first_kernel(low_ref, high_ref, w_ref, send_ref):
    t = jnp.concatenate([low_ref[...], high_ref[...]], axis=0)
    send_ref[...] = dot(t, w_ref[...]).astype(send_ref.dtype)


def later_kernel(low_ref, high_ref, w_ref, came_ref, send_ref, keep_ref):
    t = jnp.concatenate([low_ref[...], high_ref[...]], axis=0)
    out = dot(t, w_ref[...]) + came_ref[...].astype(jnp.float32)
    n = keep_ref.shape[0]
    keep_ref[...] = out[:n]
    send_ref[...] = out[n:].astype(send_ref.dtype)


def half_product(low, high, h, weight, came=None, tile=512):
    half, features, columns = low.shape[0] // 2, low.shape[1], weight.shape[1]
    tile = min(tile, columns)
    column = lambda i: (0, i)
    rows = pl.BlockSpec((half, features), lambda i: (h, 0))
    both = pl.BlockSpec((2 * half, tile), column)
    one = pl.BlockSpec((half, tile), column)
    shape = lambda n, dtype: jax.ShapeDtypeStruct((n, columns), dtype)
    first = came is None
    cost = 2 * features * columns * 2 if first else COST
    return pl.pallas_call(
        first_kernel if first else later_kernel,
        grid=(columns // tile,),
        in_specs=[rows, rows, pl.BlockSpec((features, tile), column)] + ([] if first else [both]),
        out_specs=both if first else [one, one],
        out_shape=shape(2 * half, jnp.bfloat16)
        if first
        else [shape(half, jnp.bfloat16), shape(half, jnp.float32)],
        compiler_params=pltpu.CompilerParams(vmem_limit_bytes=VMEM_LIMIT),
        cost_estimate=pl.CostEstimate(flops=0, bytes_accessed=cost, transcendentals=0),
        name="half_product",
    )(low, high, weight, *([] if first else [came]))


def attention_kernel(
    place_ref, qm_ref, qc_ref, kc_ref, vc_ref, km_ref, kt_ref, vm_ref, vt_ref, *rest
):
    o_ref, last_ref = rest[-2:]
    length, here, first = place_ref[0], place_ref[1], place_ref[2]
    rows, block = qm_ref.shape[0], km_ref.shape[0]
    half = block // 2
    total = lambda mine, came: (mine + came.astype(jnp.float32)).astype(jnp.bfloat16)
    factor = 1.4426950408889634 / HEAD_SIZE**0.5
    row = lax.broadcasted_iota(jnp.int32, (rows, 1), 0) + here * half
    col = lax.broadcasted_iota(jnp.int32, (rows, block), 1)
    col = jnp.where(col < half, col + first * half, col - first * half)
    allowed = (col <= row) & (col < length)
    contract = (((1,), (1,)), ((), ()))
    at = row == length - 1
    keys = total(km_ref[...], kt_ref[...])
    values = total(vm_ref[...], vt_ref[...])
    stack = 2
    allowed = jnp.concatenate([allowed] * stack, axis=0)
    for member in range(0, QUERY_PER_GROUP, stack):
        each = [
            slice((member + i) * HEAD_SIZE, (member + i + 1) * HEAD_SIZE) for i in range(stack)
        ]
        q = jnp.concatenate([total(qm_ref[:, cols], qc_ref[:, cols]) for cols in each], axis=0)
        s1 = lax.dot_general(q, kc_ref[...], contract, preferred_element_type=jnp.float32)
        s2 = lax.dot_general(q, keys, contract, preferred_element_type=jnp.float32)
        s2 = jnp.where(allowed, s2, -jnp.inf)
        top = jnp.maximum(jnp.max(s1, axis=1, keepdims=True), jnp.max(s2, axis=1, keepdims=True))
        p1 = jnp.exp2((s1 - top) * factor)
        p2 = jnp.exp2((s2 - top) * factor)
        norm = jnp.sum(p1, axis=1, keepdims=True) + jnp.sum(p2, axis=1, keepdims=True)
        both = dot(p1.astype(jnp.bfloat16), vc_ref[...]) + dot(p2.astype(jnp.bfloat16), values)
        both = both / norm
        for i, cols in enumerate(each):
            out = both[i * rows : (i + 1) * rows]
            o_ref[:, cols] = out.astype(o_ref.dtype)
            last_ref[:, cols] = jnp.sum(jnp.where(at, out, 0.0), axis=0, keepdims=True).astype(
                last_ref.dtype
            )


def attend(place, q, which, k_cache, v_cache, kv, start, shape, buffer, limit):
    cols = q[0].shape[1]
    wide = QUERY_PER_GROUP * HEAD_SIZE
    cached, block = k_cache.shape[0], kv[0].shape[0]
    rows = block // 2
    heads = k_cache.shape[1] // HEAD_SIZE
    groups = cols // wide
    begin = start // wide
    column = lambda i, place: (0, begin + i)
    after = lambda i, place: (0, heads + begin + i)
    mine = lambda i, place: (which, i)
    buffers = [] if buffer is None else [buffer]
    return pl.pallas_call(
        attention_kernel,
        grid_spec=pltpu.PrefetchScalarGridSpec(
            num_scalar_prefetch=1,
            grid=(groups,),
            in_specs=[
                pl.BlockSpec((rows, wide), mine),
                pl.BlockSpec((rows, wide), mine),
                pl.BlockSpec((cached, HEAD_SIZE), column),
                pl.BlockSpec((cached, HEAD_SIZE), column),
                pl.BlockSpec((block, HEAD_SIZE), column),
                pl.BlockSpec((block, HEAD_SIZE), column),
                pl.BlockSpec((block, HEAD_SIZE), after),
                pl.BlockSpec((block, HEAD_SIZE), after),
            ]
            + [pl.BlockSpec(memory_space=pl.ANY)] * len(buffers),
            out_specs=[
                pl.BlockSpec((rows, wide), lambda i, place: (place[1], begin + i)),
                pl.BlockSpec((1, wide), lambda i, place: (0, i)),
            ],
        ),
        out_shape=[
            jax.ShapeDtypeStruct(shape, jnp.bfloat16),
            jax.ShapeDtypeStruct((1, cols), jnp.bfloat16),
        ],
        input_output_aliases={9: 0} if buffers else {},
        compiler_params=pltpu.CompilerParams(vmem_limit_bytes=limit),
        cost_estimate=pl.CostEstimate(flops=0, bytes_accessed=COST, transcendentals=0),
        name="attention",
    )(place, *q, k_cache, v_cache, *kv, *kv, *buffers)


def shards(tokens_in, w_query, w_key, w_value, stored_key_cache, stored_value_cache, prompt_len):
    n_inst, n_tp = lax.axis_size("inst"), lax.axis_size("tp")
    outer = n_inst // INNER
    me = lax.axis_index("inst")
    z, w = me // INNER, me % INNER
    x = lax.axis_index("tp")
    rows, local = tokens_in.shape
    half = rows // 2
    part = local // outer

    first = (prompt_len[0] - 1) // half

    def over_inst(value, bits):
        return lax.ppermute(value, "inst", [(i, i ^ bits) for i in range(n_inst)])

    def over_outer(value, bits):
        return over_inst(value, bits * INNER)

    def over_tp(value):
        return lax.ppermute(value, "tp", [(0, 1), (1, 0)])

    def swapped_if(flag, a, b, axis):
        return jnp.where(
            flag, jnp.concatenate([b, a], axis=axis), jnp.concatenate([a, b], axis=axis)
        )

    last_step = [None]

    def step(*values):
        if last_step[0] is not None:
            *values, _ = lax.optimization_barrier((*values, last_step[0]))
        last_step[0] = values[0]
        return values[0] if len(values) == 1 else values

    heads = w_key.shape[1] // HEAD_SIZE
    wide = QUERY_PER_GROUP * HEAD_SIZE
    pieces = 2 if heads % 2 == 0 else 1
    chunk = heads * wide // pieces
    fast = outer == 4 and n_tp == 2

    groups = [list(range(o * INNER, (o + 1) * INNER)) for o in range(outer)]

    def group_gather(value):
        return lax.all_gather(value, "inst", axis=0, tiled=True, axis_index_groups=groups)

    weights = {}

    weights["kv"] = group_gather(jnp.concatenate([w_key, w_value], axis=1))

    def gather_queries():
        source = step(w_query) if fast else w_query
        for piece in range(pieces):
            part_of = source[:, piece * chunk : (piece + 1) * chunk]
            weights[piece] = group_gather(part_of)

    tokens = {}
    if fast:

        def cut(source, j, p):
            column = (((z % 2) ^ j) * n_tp + p) * part
            return jnp.concatenate(
                [
                    lax.dynamic_slice(source, (h * half, column), (half, part))
                    for h in (first, 1 - first)
                ],
                axis=0,
            )

        swap = {1: over_tp(step(cut(tokens_in, 1, 1 - x)))}
        source = tokens_in
        swap[0] = over_tp(step(cut(source, 0, 1 - x)))
        mine = z // 2 == x
        held, came = {}, {}
        swap[1] = step(swap[1])
        own = cut(source, 1, x)
        send = {b: jnp.where(mine == (b < 2), own, swap[1]) for b in (1, 3)}
        send[1], send[3] = step(send[1], send[3])
        got = {b: over_outer(send[b], b) for b in (1, 3)}
        gather_queries()

        def tp_exchange(b):
            held[b] = step(got[b])
            came[b] = over_tp(held[b])

        tp_exchange(1)
        weights["kv"] = step(weights["kv"])
        tp_exchange(3)
        swap[0] = step(swap[0])
        own = cut(source, 0, x)
        send = {b: jnp.where(mine == (b < 2), own, swap[0]) for b in (2, 0)}
        send[2] = step(send[2])
        got[2], got[0] = over_outer(send[2], 2), send[0]

        def arrived(b):
            if b not in tokens:
                tokens[b] = (swapped_if(x == 1, held[b], step(came[b]), 1),)

    else:
        gather_queries()
        swapped = jnp.where(first == 1, jnp.roll(tokens_in, half, axis=0), tokens_in)
        own = swapped.reshape(rows, outer // n_tp, n_tp, part)
        parts = lax.all_to_all(own, "tp", 2, 1, tiled=True).reshape(rows, outer, part)
        come = jnp.stack(
            [
                over_outer(lax.dynamic_index_in_dim(parts, z ^ b, 1, keepdims=False), b)
                for b in range(outer)
            ]
        )
        both = lax.all_gather(come.reshape(-1, part), "tp", axis=1, tiled=True)
        both = both.reshape(outer, rows, -1)
        tokens.update({b: (both[b],) for b in range(outer)})

        def arrived(b):
            pass

    def rows_of(values, h):
        if h is None:
            return values
        return tuple(value[h * half : (h + 1) * half] for value in values)

    def times(values, weight):
        total, row = None, 0
        for value in values:
            one = dot(value, weight[row : row + value.shape[1]])
            total = one if total is None else total + one
            row += value.shape[1]
        return total

    def first_send(h, name):
        weight = weights[name] = step(weights[name])
        bits = range(1, outer, 2)
        if h is None:
            come = {}
            for b in bits:
                arrived(b)
                come[b] = over_outer(step(times(tokens[b], weight).astype(jnp.bfloat16)), 1)
            return come
        if fast:
            send = half_product(tokens[1][0], tokens[3][0], h, weight)
            return over_outer(step(send), 1)
        joined = [jnp.concatenate(same) for same in zip(*[rows_of(tokens[b], h) for b in bits])]
        come = over_outer(step(times(joined, weight).astype(jnp.bfloat16)), 1)
        return {b: (come, i) for i, b in enumerate(bits)}

    def later_sends(h, name, come):
        weight = weights[name]
        arrived(0)
        arrived(2)
        if fast and h is not None:
            send, keep = half_product(tokens[0][0], tokens[2][0], h, weight, step(come))
            send, keep = step(send, keep)
            return keep, over_outer(send, 2)
        if h is None:
            bits = list(come)
            come = dict(zip(bits, step(*[come[b] for b in bits])))
        else:
            whole = step(next(iter(come.values()))[0])
            come = {b: whole[i * half : (i + 1) * half] for b, (_, i) in come.items()}

        def total(b, arrival):
            return times(rows_of(tokens[b], h), weight) + arrival.astype(jnp.float32)

        if outer == 4:
            moved = over_outer(step(total(2, come[3]).astype(jnp.bfloat16)), 2)
            return total(0, step(come[1])), moved
        sums = {b: total(b, come[b + 1]) for b in range(0, outer, 2)}
        bit = 2
        while True:
            for b in sorted(sums):
                if b & bit:
                    moved = over_outer(step(sums.pop(b).astype(jnp.bfloat16)), bit)
                    if 2 * bit == outer:
                        return sums[0], moved
                    sums[b ^ bit] = sums[b ^ bit] + moved.astype(jnp.float32)
            bit *= 2

    jobs = [(None, "kv")] + ([(None, 0)] if pieces == 2 else [])
    jobs += [(0, pieces - 1), (1, pieces - 1)]
    opened, parts_of, lasts = {}, {}, []
    attended = [None]

    def start(n):
        opened[n] = first_send(*jobs[n])

    def advance(n):
        parts_of[n] = later_sends(*jobs[n], opened[n])

    def arrive(n):
        came_in, mine = step(parts_of[n][1], parts_of[n][0])
        parts_of[n] = (mine, came_in)

    def attention(n, h):
        own_half, piece = jobs[n]
        which = h if own_half is None else 0
        place = jnp.stack([prompt_len[0], h ^ first, first]).astype(jnp.int32)
        caches = (stored_key_cache, stored_value_cache)
        shape = (rows, heads * wide)
        limit = VMEM_LIMIT if n < len(jobs) - 1 else 56 * 1024 * 1024
        where = (piece * chunk, shape, attended[0], limit)
        attended[0], last = attend(place, parts_of[n], which, *caches, parts_of[0], *where)
        lasts.append(step(last))

    def from_xor_order(values, index):
        out = jnp.stack(values)
        shape = out.shape
        bits = len(values).bit_length() - 1
        for bit in range(bits):
            out = out.reshape(len(values) >> (bit + 1), 2, 1 << bit, *shape[1:])
            out = jnp.where((index >> bit) % 2 == 1, out[:, ::-1], out)
        return out.reshape(shape)

    start(0)
    if fast:
        tp_exchange(0)
        tp_exchange(2)
    start(1)
    advance(0)
    if pieces == 2:
        weights[1] = step(weights[1])
        advance(1)
        start(2)
        start(3)
        arrive(0)
        arrive(1)
        advance(2)
        attention(1, 0)
        advance(3)
        attention(1, 1)
        arrive(2)
        attention(2, 0)
        row = jnp.concatenate([lasts[0] + lasts[1], lasts[2]], axis=1)
    else:
        start(2)
        advance(1)
        arrive(0)
        advance(2)
        arrive(1)
        attention(1, 0)
        row = lasts[0]
    row = step(row)
    in_group = [row] + [over_inst(row, m) for m in range(1, INNER)]
    arrive(len(jobs) - 1)
    in_group[1] = step(in_group[1])
    in_group = from_xor_order(in_group, w)
    over_all = [in_group] + [over_outer(in_group, b) for b in range(1, outer)]
    attention(len(jobs) - 1, 1)
    over_all[1] = step(over_all[1])
    handoff = from_xor_order(over_all, z).reshape(n_inst, heads * wide)
    return (attended[0], handoff)


def solution(mesh):
    return jax.shard_map(
        shards,
        mesh=mesh,
        in_specs=(
            P("inst", "tp"),
            P("inst", "tp"),
            P("inst", "tp"),
            P("inst", "tp"),
            P("inst", "tp"),
            P("inst", "tp"),
            P("inst"),
        ),
        out_specs=(P("inst", "tp"), P(None, "tp")),
        check_vma=False,
    )
```

```python
import jax
import jax.numpy as jnp
from jax import lax
from jax.experimental import pallas as pl
from jax.experimental.pallas import tpu as pltpu
from jax.sharding import PartitionSpec as P

HEAD_SIZE = 128
QUERY_PER_GROUP = 4
VMEM_LIMIT = 32 * 1024 * 1024
COST = 1 << 10
INNER = 4


def dot(a, b):
    return jnp.dot(a, b, preferred_element_type=jnp.float32)


def first_kernel(low_ref, high_ref, w_ref, send_ref):
    t = jnp.concatenate([low_ref[...], high_ref[...]], axis=0)
    send_ref[...] = dot(t, w_ref[...]).astype(send_ref.dtype)


def later_kernel(low_ref, high_ref, w_ref, came_ref, send_ref, keep_ref):
    t = jnp.concatenate([low_ref[...], high_ref[...]], axis=0)
    out = dot(t, w_ref[...]) + came_ref[...].astype(jnp.float32)
    n = keep_ref.shape[0]
    keep_ref[...] = out[:n]
    send_ref[...] = out[n:].astype(send_ref.dtype)


def half_product(low, high, h, weight, came=None, tile=512):
    half, features, columns = low.shape[0] // 2, low.shape[1], weight.shape[1]
    tile = min(tile, columns)
    column = lambda i: (0, i)
    rows = pl.BlockSpec((half, features), lambda i: (h, 0))
    both = pl.BlockSpec((2 * half, tile), column)
    one = pl.BlockSpec((half, tile), column)
    shape = lambda n, dtype: jax.ShapeDtypeStruct((n, columns), dtype)
    first = came is None
    cost = 2 * features * columns * 2 if first else COST
    return pl.pallas_call(
        first_kernel if first else later_kernel,
        grid=(columns // tile,),
        in_specs=[rows, rows, pl.BlockSpec((features, tile), column)] + ([] if first else [both]),
        out_specs=both if first else [one, one],
        out_shape=shape(2 * half, jnp.bfloat16)
        if first
        else [shape(half, jnp.bfloat16), shape(half, jnp.float32)],
        compiler_params=pltpu.CompilerParams(vmem_limit_bytes=VMEM_LIMIT),
        cost_estimate=pl.CostEstimate(flops=0, bytes_accessed=cost, transcendentals=0),
        name="half_product",
    )(low, high, weight, *([] if first else [came]))


def order_kernel(index_ref, *refs):
    out_ref = refs[-1]
    for m, ref in enumerate(refs[:-1]):
        out_ref[index_ref[0] ^ m] = ref[...]


def from_xor_order(values, index):
    shape = values[0].shape
    return pl.pallas_call(
        order_kernel,
        in_specs=[pl.BlockSpec(memory_space=pltpu.SMEM)]
        + [pl.BlockSpec(memory_space=pltpu.VMEM)] * len(values),
        out_specs=pl.BlockSpec(memory_space=pltpu.VMEM),
        out_shape=jax.ShapeDtypeStruct((len(values), *shape), values[0].dtype),
        cost_estimate=pl.CostEstimate(flops=0, bytes_accessed=COST, transcendentals=0),
        name="order",
    )(index[None].astype(jnp.int32), *values)


def attention_kernel(
    place_ref, qm_ref, qc_ref, kc_ref, vc_ref, km_ref, kt_ref, vm_ref, vt_ref, *rest
):
    o_ref, last_ref = rest[-2:]
    length, here, first = place_ref[0], place_ref[1], place_ref[2]
    rows, block = qm_ref.shape[0], km_ref.shape[0]
    half = block // 2
    total = lambda mine, came: (mine + came.astype(jnp.float32)).astype(jnp.bfloat16)
    factor = 1.4426950408889634 / HEAD_SIZE**0.5
    row = lax.broadcasted_iota(jnp.int32, (rows, 1), 0) + here * half
    col = lax.broadcasted_iota(jnp.int32, (rows, block), 1)
    col = jnp.where(col < half, col + first * half, col - first * half)
    allowed = (col <= row) & (col < length)
    contract = (((1,), (1,)), ((), ()))
    at = row == length - 1
    keys = total(km_ref[...], kt_ref[...])
    values = total(vm_ref[...], vt_ref[...])
    stack = 2
    allowed = jnp.concatenate([allowed] * stack, axis=0)
    for member in range(0, QUERY_PER_GROUP, stack):
        each = [
            slice((member + i) * HEAD_SIZE, (member + i + 1) * HEAD_SIZE) for i in range(stack)
        ]
        q = jnp.concatenate([total(qm_ref[:, cols], qc_ref[:, cols]) for cols in each], axis=0)
        s1 = lax.dot_general(q, kc_ref[...], contract, preferred_element_type=jnp.float32)
        s2 = lax.dot_general(q, keys, contract, preferred_element_type=jnp.float32)
        s2 = jnp.where(allowed, s2, -jnp.inf)
        top = jnp.maximum(jnp.max(s1, axis=1, keepdims=True), jnp.max(s2, axis=1, keepdims=True))
        p1 = jnp.exp2((s1 - top) * factor)
        p2 = jnp.exp2((s2 - top) * factor)
        norm = jnp.sum(p1, axis=1, keepdims=True) + jnp.sum(p2, axis=1, keepdims=True)
        both = dot(p1.astype(jnp.bfloat16), vc_ref[...]) + dot(p2.astype(jnp.bfloat16), values)
        both = both / norm
        for i, cols in enumerate(each):
            out = both[i * rows : (i + 1) * rows]
            o_ref[:, cols] = out.astype(o_ref.dtype)
            last_ref[:, cols] = jnp.sum(jnp.where(at, out, 0.0), axis=0, keepdims=True).astype(
                last_ref.dtype
            )


def attend(place, q, which, k_cache, v_cache, kv, start, shape, buffer, limit):
    cols = q[0].shape[1]
    wide = QUERY_PER_GROUP * HEAD_SIZE
    cached, block = k_cache.shape[0], kv[0].shape[0]
    rows = block // 2
    heads = k_cache.shape[1] // HEAD_SIZE
    groups = cols // wide
    begin = start // wide
    column = lambda i, place: (0, begin + i)
    after = lambda i, place: (0, heads + begin + i)
    mine = lambda i, place: (which, i)
    buffers = [] if buffer is None else [buffer]
    return pl.pallas_call(
        attention_kernel,
        grid_spec=pltpu.PrefetchScalarGridSpec(
            num_scalar_prefetch=1,
            grid=(groups,),
            in_specs=[
                pl.BlockSpec((rows, wide), mine),
                pl.BlockSpec((rows, wide), mine),
                pl.BlockSpec((cached, HEAD_SIZE), column),
                pl.BlockSpec((cached, HEAD_SIZE), column),
                pl.BlockSpec((block, HEAD_SIZE), column),
                pl.BlockSpec((block, HEAD_SIZE), column),
                pl.BlockSpec((block, HEAD_SIZE), after),
                pl.BlockSpec((block, HEAD_SIZE), after),
            ]
            + [pl.BlockSpec(memory_space=pl.ANY)] * len(buffers),
            out_specs=[
                pl.BlockSpec((rows, wide), lambda i, place: (place[1], begin + i)),
                pl.BlockSpec((1, wide), lambda i, place: (0, i)),
            ],
        ),
        out_shape=[
            jax.ShapeDtypeStruct(shape, jnp.bfloat16),
            jax.ShapeDtypeStruct((1, cols), jnp.bfloat16),
        ],
        input_output_aliases={9: 0} if buffers else {},
        compiler_params=pltpu.CompilerParams(vmem_limit_bytes=limit),
        cost_estimate=pl.CostEstimate(flops=0, bytes_accessed=COST, transcendentals=0),
        name="attention",
    )(place, *q, k_cache, v_cache, *kv, *kv, *buffers)


def shards(tokens_in, w_query, w_key, w_value, stored_key_cache, stored_value_cache, prompt_len):
    n_inst, n_tp = lax.axis_size("inst"), lax.axis_size("tp")
    outer = n_inst // INNER
    me = lax.axis_index("inst")
    z, w = me // INNER, me % INNER
    x = lax.axis_index("tp")
    rows, local = tokens_in.shape
    half = rows // 2
    part = local // outer

    first = (prompt_len[0] - 1) // half

    def over_inst(value, bits):
        return lax.ppermute(value, "inst", [(i, i ^ bits) for i in range(n_inst)])

    def over_outer(value, bits):
        return over_inst(value, bits * INNER)

    def over_tp(value):
        return lax.ppermute(value, "tp", [(0, 1), (1, 0)])

    def swapped_if(flag, a, b, axis):
        return jnp.where(
            flag, jnp.concatenate([b, a], axis=axis), jnp.concatenate([a, b], axis=axis)
        )

    last_step = [None]

    def step(*values):
        if last_step[0] is not None:
            *values, _ = lax.optimization_barrier((*values, last_step[0]))
        last_step[0] = values[0]
        return values[0] if len(values) == 1 else values

    heads = w_key.shape[1] // HEAD_SIZE
    wide = QUERY_PER_GROUP * HEAD_SIZE
    pieces = 2 if heads % 2 == 0 else 1
    chunk = heads * wide // pieces
    fast = outer == 4 and n_tp == 2

    groups = [list(range(o * INNER, (o + 1) * INNER)) for o in range(outer)]

    def group_gather(value):
        return lax.all_gather(value, "inst", axis=0, tiled=True, axis_index_groups=groups)

    weights = {}

    weights["kv"] = group_gather(jnp.concatenate([w_key, w_value], axis=1))

    def gather_queries():
        source = step(w_query) if fast else w_query
        for piece in range(pieces):
            part_of = source[:, piece * chunk : (piece + 1) * chunk]
            weights[piece] = group_gather(part_of)

    tokens = {}
    if fast:

        def cut(source, j, p):
            column = (((z % 2) ^ j) * n_tp + p) * part
            return jnp.concatenate(
                [
                    lax.dynamic_slice(source, (h * half, column), (half, part))
                    for h in (first, 1 - first)
                ],
                axis=0,
            )

        swap = {1: over_tp(step(cut(tokens_in, 1, 1 - x)))}
        source = step(tokens_in)
        swap[0] = over_tp(step(cut(source, 0, 1 - x)))
        mine = z // 2 == x
        held, came = {}, {}
        swap[1] = step(swap[1])
        own = cut(source, 1, x)
        send = {b: jnp.where(mine == (b < 2), own, swap[1]) for b in (1, 3)}
        send[1], send[3] = step(send[1], send[3])
        got = {b: over_outer(send[b], b) for b in (1, 3)}
        gather_queries()

        def tp_exchange(b):
            held[b] = step(got[b])
            came[b] = over_tp(held[b])

        tp_exchange(1)
        weights["kv"] = step(weights["kv"])
        tp_exchange(3)
        swap[0] = step(swap[0])
        own = cut(source, 0, x)
        send = {b: jnp.where(mine == (b < 2), own, swap[0]) for b in (2, 0)}
        send[2] = step(send[2])
        got[2], got[0] = over_outer(send[2], 2), send[0]

        def arrived(b):
            if b not in tokens:
                tokens[b] = (swapped_if(x == 1, held[b], step(came[b]), 1),)

    else:
        gather_queries()
        swapped = jnp.where(first == 1, jnp.roll(tokens_in, half, axis=0), tokens_in)
        own = swapped.reshape(rows, outer // n_tp, n_tp, part)
        parts = lax.all_to_all(own, "tp", 2, 1, tiled=True).reshape(rows, outer, part)
        come = jnp.stack(
            [
                over_outer(lax.dynamic_index_in_dim(parts, z ^ b, 1, keepdims=False), b)
                for b in range(outer)
            ]
        )
        both = lax.all_gather(come.reshape(-1, part), "tp", axis=1, tiled=True)
        both = both.reshape(outer, rows, -1)
        tokens.update({b: (both[b],) for b in range(outer)})

        def arrived(b):
            pass

    def rows_of(values, h):
        if h is None:
            return values
        return tuple(value[h * half : (h + 1) * half] for value in values)

    def times(values, weight):
        total, row = None, 0
        for value in values:
            one = dot(value, weight[row : row + value.shape[1]])
            total = one if total is None else total + one
            row += value.shape[1]
        return total

    def first_send(h, name):
        weight = weights[name] = step(weights[name])
        bits = range(1, outer, 2)
        if h is None:
            come = {}
            for b in bits:
                arrived(b)
                come[b] = over_outer(step(times(tokens[b], weight).astype(jnp.bfloat16)), 1)
            return come
        if fast:
            send = half_product(tokens[1][0], tokens[3][0], h, weight)
            return over_outer(step(send), 1)
        joined = [jnp.concatenate(same) for same in zip(*[rows_of(tokens[b], h) for b in bits])]
        come = over_outer(step(times(joined, weight).astype(jnp.bfloat16)), 1)
        return {b: (come, i) for i, b in enumerate(bits)}

    def later_sends(h, name, come):
        weight = weights[name]
        arrived(0)
        if fast and h is not None:
            send, keep = half_product(tokens[0][0], tokens[2][0], h, weight, step(come))
            send, keep = step(send, keep)
            return keep, over_outer(send, 2)
        if h is None:
            bits = list(come)
            come = dict(zip(bits, step(*[come[b] for b in bits])))
            arrived(2)
        else:
            whole = step(next(iter(come.values()))[0])
            come = {b: whole[i * half : (i + 1) * half] for b, (_, i) in come.items()}

        def total(b, arrival):
            return times(rows_of(tokens[b], h), weight) + arrival.astype(jnp.float32)

        if outer == 4:
            moved = over_outer(step(total(2, come[3]).astype(jnp.bfloat16)), 2)
            return total(0, step(come[1])), moved
        sums = {b: total(b, come[b + 1]) for b in range(0, outer, 2)}
        bit = 2
        while True:
            for b in sorted(sums):
                if b & bit:
                    moved = over_outer(step(sums.pop(b).astype(jnp.bfloat16)), bit)
                    if 2 * bit == outer:
                        return sums[0], moved
                    sums[b ^ bit] = sums[b ^ bit] + moved.astype(jnp.float32)
            bit *= 2

    jobs = [(None, "kv")] + ([(None, 0)] if pieces == 2 else [])
    jobs += [(0, pieces - 1), (1, pieces - 1)]
    opened, parts_of, lasts = {}, {}, []
    attended = [None]

    def start(n):
        opened[n] = first_send(*jobs[n])

    def advance(n):
        parts_of[n] = later_sends(*jobs[n], opened[n])

    def arrive(n):
        came_in, mine = step(parts_of[n][1], parts_of[n][0])
        parts_of[n] = (mine, came_in)

    def attention(n, h):
        own_half, piece = jobs[n]
        which = h if own_half is None else 0
        place = jnp.stack([prompt_len[0], h ^ first, first]).astype(jnp.int32)
        caches = (stored_key_cache, stored_value_cache)
        shape = (rows, heads * wide)
        limit = VMEM_LIMIT if n < len(jobs) - 1 else 56 * 1024 * 1024
        where = (piece * chunk, shape, attended[0], limit)
        attended[0], last = attend(place, parts_of[n], which, *caches, parts_of[0], *where)
        lasts.append(step(last))

    start(0)
    if fast:
        tp_exchange(0)
        tp_exchange(2)
    start(1)
    advance(0)
    if pieces == 2:
        weights[1] = step(weights[1])
        start(2)
        advance(1)
        arrive(0)
        advance(2)
        start(3)
        arrive(1)
        attention(1, 0)
        attention(1, 1)
        advance(3)
        arrive(2)
        attention(2, 0)
        row = jnp.concatenate([lasts[0] + lasts[1], lasts[2]], axis=1)
    else:
        start(2)
        advance(1)
        arrive(0)
        advance(2)
        arrive(1)
        attention(1, 0)
        row = lasts[0]
    row = step(row)
    in_group = [row] + [over_inst(row, m) for m in range(1, INNER)]
    in_group = from_xor_order(in_group, w)
    over_all = [in_group] + [over_outer(in_group, b) for b in range(1, outer)]
    arrive(len(jobs) - 1)
    attention(len(jobs) - 1, 1)
    handoff = from_xor_order(over_all, z).reshape(n_inst, heads * wide)
    return (attended[0], handoff)


def solution(mesh):
    return jax.shard_map(
        shards,
        mesh=mesh,
        in_specs=(
            P("inst", "tp"),
            P("inst", "tp"),
            P("inst", "tp"),
            P("inst", "tp"),
            P("inst", "tp"),
            P("inst", "tp"),
            P("inst"),
        ),
        out_specs=(P("inst", "tp"), P(None, "tp")),
        check_vma=False,
    )
```

```python
import jax
import jax.numpy as jnp
from jax import lax
from jax.experimental import pallas as pl
from jax.experimental.pallas import tpu as pltpu
from jax.sharding import PartitionSpec as P

HEAD_SIZE = 128
QUERY_PER_GROUP = 4
VMEM_LIMIT = 32 * 1024 * 1024
COST = 1 << 10
INNER = 4


def dot(a, b):
    return jnp.dot(a, b, preferred_element_type=jnp.float32)


def first_kernel(low_ref, high_ref, w_ref, send_ref):
    t = jnp.concatenate([low_ref[...], high_ref[...]], axis=0)
    send_ref[...] = dot(t, w_ref[...]).astype(send_ref.dtype)


def later_kernel(low_ref, high_ref, w_ref, came_ref, send_ref, keep_ref):
    t = jnp.concatenate([low_ref[...], high_ref[...]], axis=0)
    out = dot(t, w_ref[...]) + came_ref[...].astype(jnp.float32)
    n = keep_ref.shape[0]
    keep_ref[...] = out[:n]
    send_ref[...] = out[n:].astype(send_ref.dtype)


def half_product(low, high, h, weight, came=None, tile=512):
    half, features, columns = low.shape[0] // 2, low.shape[1], weight.shape[1]
    tile = min(tile, columns)
    column = lambda i: (0, i)
    rows = pl.BlockSpec((half, features), lambda i: (h, 0))
    both = pl.BlockSpec((2 * half, tile), column)
    one = pl.BlockSpec((half, tile), column)
    shape = lambda n, dtype: jax.ShapeDtypeStruct((n, columns), dtype)
    first = came is None
    cost = 2 * features * columns * 2 if first else COST
    return pl.pallas_call(
        first_kernel if first else later_kernel,
        grid=(columns // tile,),
        in_specs=[rows, rows, pl.BlockSpec((features, tile), column)] + ([] if first else [both]),
        out_specs=both if first else [one, one],
        out_shape=shape(2 * half, jnp.bfloat16)
        if first
        else [shape(half, jnp.bfloat16), shape(half, jnp.float32)],
        compiler_params=pltpu.CompilerParams(vmem_limit_bytes=VMEM_LIMIT),
        cost_estimate=pl.CostEstimate(flops=0, bytes_accessed=cost, transcendentals=0),
        name="half_product",
    )(low, high, weight, *([] if first else [came]))


def order_kernel(index_ref, *refs):
    out_ref = refs[-1]
    for m, ref in enumerate(refs[:-1]):
        out_ref[index_ref[0] ^ m] = ref[...]


def ordered(values, index):
    return pl.pallas_call(
        order_kernel,
        in_specs=[pl.BlockSpec(memory_space=pltpu.SMEM)]
        + [pl.BlockSpec(memory_space=pltpu.VMEM)] * len(values),
        out_specs=pl.BlockSpec(memory_space=pltpu.VMEM),
        out_shape=jax.ShapeDtypeStruct((len(values), *values[0].shape), values[0].dtype),
        cost_estimate=pl.CostEstimate(flops=0, bytes_accessed=COST, transcendentals=0),
        name="order",
    )(index[None].astype(jnp.int32), *values)


def attention_kernel(
    place_ref, qm_ref, qc_ref, kc_ref, vc_ref, km_ref, kt_ref, vm_ref, vt_ref, *rest
):
    o_ref, last_ref = rest[-2:]
    length, here, first = place_ref[0], place_ref[1], place_ref[2]
    rows, block = qm_ref.shape[0], km_ref.shape[0]
    half = block // 2
    total = lambda mine, came: (mine + came.astype(jnp.float32)).astype(jnp.bfloat16)
    factor = 1.4426950408889634 / HEAD_SIZE**0.5
    row = lax.broadcasted_iota(jnp.int32, (rows, 1), 0) + here * half
    col = lax.broadcasted_iota(jnp.int32, (rows, block), 1)
    col = jnp.where(col < half, col + first * half, col - first * half)
    allowed = (col <= row) & (col < length)
    contract = (((1,), (1,)), ((), ()))
    at = row == length - 1
    keys = total(km_ref[...], kt_ref[...])
    values = total(vm_ref[...], vt_ref[...])
    stack = 2
    allowed = jnp.concatenate([allowed] * stack, axis=0)
    for member in range(0, QUERY_PER_GROUP, stack):
        each = [
            slice((member + i) * HEAD_SIZE, (member + i + 1) * HEAD_SIZE) for i in range(stack)
        ]
        q = [qm_ref[:, cols] + qc_ref[:, cols].astype(jnp.float32) for cols in each]
        q = (jnp.concatenate(q, axis=0) * factor).astype(jnp.bfloat16)
        s1 = lax.dot_general(q, kc_ref[...], contract, preferred_element_type=jnp.float32)
        s2 = lax.dot_general(q, keys, contract, preferred_element_type=jnp.float32)
        s2 = jnp.where(allowed, s2, -jnp.inf)
        top = jnp.maximum(jnp.max(s1, axis=1, keepdims=True), jnp.max(s2, axis=1, keepdims=True))
        p1 = jnp.exp2(s1 - top)
        p2 = jnp.exp2(s2 - top)
        norm = jnp.sum(p1, axis=1, keepdims=True) + jnp.sum(p2, axis=1, keepdims=True)
        both = dot(p1.astype(jnp.bfloat16), vc_ref[...]) + dot(p2.astype(jnp.bfloat16), values)
        both = both / norm
        for i, cols in enumerate(each):
            out = both[i * rows : (i + 1) * rows]
            o_ref[:, cols] = out.astype(o_ref.dtype)
            last_ref[:, cols] = jnp.sum(jnp.where(at, out, 0.0), axis=0, keepdims=True).astype(
                last_ref.dtype
            )


def attend(place, q, which, k_cache, v_cache, kv, start, shape, buffer, limit):
    cols = q[0].shape[1]
    wide = QUERY_PER_GROUP * HEAD_SIZE
    cached, block = k_cache.shape[0], kv[0].shape[0]
    rows = block // 2
    heads = k_cache.shape[1] // HEAD_SIZE
    groups = cols // wide
    begin = start // wide
    column = lambda i, place: (0, begin + i)
    after = lambda i, place: (0, heads + begin + i)
    mine = lambda i, place: (which, i)
    buffers = [] if buffer is None else [buffer]
    return pl.pallas_call(
        attention_kernel,
        grid_spec=pltpu.PrefetchScalarGridSpec(
            num_scalar_prefetch=1,
            grid=(groups,),
            in_specs=[
                pl.BlockSpec((rows, wide), mine),
                pl.BlockSpec((rows, wide), mine),
                pl.BlockSpec((cached, HEAD_SIZE), column),
                pl.BlockSpec((cached, HEAD_SIZE), column),
                pl.BlockSpec((block, HEAD_SIZE), column),
                pl.BlockSpec((block, HEAD_SIZE), column),
                pl.BlockSpec((block, HEAD_SIZE), after),
                pl.BlockSpec((block, HEAD_SIZE), after),
            ]
            + [pl.BlockSpec(memory_space=pl.ANY)] * len(buffers),
            out_specs=[
                pl.BlockSpec((rows, wide), lambda i, place: (place[1], begin + i)),
                pl.BlockSpec((1, wide), lambda i, place: (0, i)),
            ],
        ),
        out_shape=[
            jax.ShapeDtypeStruct(shape, jnp.bfloat16),
            jax.ShapeDtypeStruct((1, cols), jnp.bfloat16),
        ],
        input_output_aliases={9: 0} if buffers else {},
        compiler_params=pltpu.CompilerParams(vmem_limit_bytes=limit),
        cost_estimate=pl.CostEstimate(flops=0, bytes_accessed=COST, transcendentals=0),
        name="attention",
    )(place, *q, k_cache, v_cache, *kv, *kv, *buffers)


def shards(tokens_in, w_query, w_key, w_value, stored_key_cache, stored_value_cache, prompt_len):
    n_inst, n_tp = lax.axis_size("inst"), lax.axis_size("tp")
    outer = n_inst // INNER
    me = lax.axis_index("inst")
    z, w = me // INNER, me % INNER
    x = lax.axis_index("tp")
    rows, local = tokens_in.shape
    half = rows // 2
    part = local // outer

    first = (prompt_len[0] - 1) // half

    def over_inst(value, bits):
        return lax.ppermute(value, "inst", [(i, i ^ bits) for i in range(n_inst)])

    def over_outer(value, bits):
        return over_inst(value, bits * INNER)

    def over_tp(value):
        return lax.ppermute(value, "tp", [(0, 1), (1, 0)])

    def swapped_if(flag, a, b, axis):
        return jnp.where(
            flag, jnp.concatenate([b, a], axis=axis), jnp.concatenate([a, b], axis=axis)
        )

    last_step = [None]

    def step(*values):
        if last_step[0] is not None:
            *values, _ = lax.optimization_barrier((*values, last_step[0]))
        last_step[0] = values[0]
        return values[0] if len(values) == 1 else values

    heads = w_key.shape[1] // HEAD_SIZE
    wide = QUERY_PER_GROUP * HEAD_SIZE
    pieces = 2 if heads % 2 == 0 else 1
    chunk = heads * wide // pieces
    fast = outer == 4 and n_tp == 2

    groups = [list(range(o * INNER, (o + 1) * INNER)) for o in range(outer)]

    def group_gather(value):
        return lax.all_gather(value, "inst", axis=0, tiled=True, axis_index_groups=groups)

    weights = {}

    weights["kv"] = group_gather(jnp.concatenate([w_key, w_value], axis=1))

    def gather_queries():
        source = step(w_query) if fast else w_query
        for piece in range(pieces):
            part_of = source[:, piece * chunk : (piece + 1) * chunk]
            weights[piece] = group_gather(part_of)

    tokens = {}
    if fast:

        def cut(source, j, p):
            column = (((z % 2) ^ j) * n_tp + p) * part
            return jnp.concatenate(
                [
                    lax.dynamic_slice(source, (h * half, column), (half, part))
                    for h in (first, 1 - first)
                ],
                axis=0,
            )

        swap = {1: over_tp(step(cut(tokens_in, 1, 1 - x)))}
        source = step(tokens_in)
        swap[0] = over_tp(step(cut(source, 0, 1 - x)))
        mine = z // 2 == x
        held, came = {}, {}
        swap[1] = step(swap[1])
        own = cut(source, 1, x)
        send = {b: jnp.where(mine == (b < 2), own, swap[1]) for b in (1, 3)}
        send[1], send[3] = step(send[1], send[3])
        got = {b: over_outer(send[b], b) for b in (1, 3)}
        gather_queries()

        def tp_exchange(b):
            held[b] = step(got[b])
            came[b] = over_tp(held[b])

        tp_exchange(1)
        weights["kv"] = step(weights["kv"])
        tp_exchange(3)
        swap[0] = step(swap[0])
        own = cut(source, 0, x)
        send = {b: jnp.where(mine == (b < 2), own, swap[0]) for b in (2, 0)}
        send[2] = step(send[2])
        got[2], got[0] = over_outer(send[2], 2), send[0]

        def arrived(b):
            if b not in tokens:
                tokens[b] = (swapped_if(x == 1, held[b], step(came[b]), 1),)

    else:
        gather_queries()
        swapped = jnp.where(first == 1, jnp.roll(tokens_in, half, axis=0), tokens_in)
        own = swapped.reshape(rows, outer // n_tp, n_tp, part)
        parts = lax.all_to_all(own, "tp", 2, 1, tiled=True).reshape(rows, outer, part)
        come = jnp.stack(
            [
                over_outer(lax.dynamic_index_in_dim(parts, z ^ b, 1, keepdims=False), b)
                for b in range(outer)
            ]
        )
        both = lax.all_gather(come.reshape(-1, part), "tp", axis=1, tiled=True)
        both = both.reshape(outer, rows, -1)
        tokens.update({b: (both[b],) for b in range(outer)})

        def arrived(b):
            pass

    def rows_of(values, h):
        if h is None:
            return values
        return tuple(value[h * half : (h + 1) * half] for value in values)

    def times(values, weight):
        total, row = None, 0
        for value in values:
            one = dot(value, weight[row : row + value.shape[1]])
            total = one if total is None else total + one
            row += value.shape[1]
        return total

    def first_send(h, name):
        weight = weights[name] = step(weights[name])
        bits = range(1, outer, 2)
        if h is None:
            come = {}
            for b in bits:
                arrived(b)
                come[b] = over_outer(step(times(tokens[b], weight).astype(jnp.bfloat16)), 1)
            return come
        if fast:
            send = half_product(tokens[1][0], tokens[3][0], h, weight)
            return over_outer(step(send), 1)
        joined = [jnp.concatenate(same) for same in zip(*[rows_of(tokens[b], h) for b in bits])]
        come = over_outer(step(times(joined, weight).astype(jnp.bfloat16)), 1)
        return {b: (come, i) for i, b in enumerate(bits)}

    def later_sends(h, name, come):
        weight = weights[name]
        arrived(0)
        if fast and h is not None:
            send, keep = half_product(tokens[0][0], tokens[2][0], h, weight, step(come))
            send, keep = step(send, keep)
            return keep, over_outer(send, 2)
        if h is None:
            bits = list(come)
            come = dict(zip(bits, step(*[come[b] for b in bits])))
            arrived(2)
        else:
            whole = step(next(iter(come.values()))[0])
            come = {b: whole[i * half : (i + 1) * half] for b, (_, i) in come.items()}

        def total(b, arrival):
            return times(rows_of(tokens[b], h), weight) + arrival.astype(jnp.float32)

        if outer == 4:
            moved = over_outer(step(total(2, come[3]).astype(jnp.bfloat16)), 2)
            return total(0, step(come[1])), moved
        sums = {b: total(b, come[b + 1]) for b in range(0, outer, 2)}
        bit = 2
        while True:
            for b in sorted(sums):
                if b & bit:
                    moved = over_outer(step(sums.pop(b).astype(jnp.bfloat16)), bit)
                    if 2 * bit == outer:
                        return sums[0], moved
                    sums[b ^ bit] = sums[b ^ bit] + moved.astype(jnp.float32)
            bit *= 2

    jobs = [(None, "kv")] + ([(None, 0)] if pieces == 2 else [])
    jobs += [(0, pieces - 1), (1, pieces - 1)]
    opened, parts_of, lasts = {}, {}, []
    attended = [None]

    def start(n):
        opened[n] = first_send(*jobs[n])

    def advance(n):
        parts_of[n] = later_sends(*jobs[n], opened[n])

    def arrive(n):
        came_in, mine = step(parts_of[n][1], parts_of[n][0])
        parts_of[n] = (mine, came_in)

    def attention(n, h):
        own_half, piece = jobs[n]
        which = h if own_half is None else 0
        place = jnp.stack([prompt_len[0], h ^ first, first]).astype(jnp.int32)
        caches = (stored_key_cache, stored_value_cache)
        shape = (rows, heads * wide)
        limit = VMEM_LIMIT if n < len(jobs) - 1 else 56 * 1024 * 1024
        where = (piece * chunk, shape, attended[0], limit)
        attended[0], last = attend(place, parts_of[n], which, *caches, parts_of[0], *where)
        lasts.append(step(last))

    def from_xor_order(values, index):
        out = jnp.stack(values)
        shape = out.shape
        bits = len(values).bit_length() - 1
        for bit in range(bits):
            out = out.reshape(len(values) >> (bit + 1), 2, 1 << bit, *shape[1:])
            out = jnp.where((index >> bit) % 2 == 1, out[:, ::-1], out)
        return out.reshape(shape)

    start(0)
    if fast:
        tp_exchange(0)
        tp_exchange(2)
    start(1)
    advance(0)
    if pieces == 2:
        weights[1] = step(weights[1])
        start(2)
        advance(1)
        arrive(0)
        advance(2)
        start(3)
        arrive(1)
        attention(1, 0)
        attention(1, 1)
        advance(3)
        arrive(2)
        attention(2, 0)
        row = jnp.concatenate([lasts[0] + lasts[1], lasts[2]], axis=1)
    else:
        start(2)
        advance(1)
        arrive(0)
        advance(2)
        arrive(1)
        attention(1, 0)
        row = lasts[0]
    row = step(row)
    in_group = [row] + [over_inst(row, m) for m in range(1, INNER)]
    in_group = ordered(in_group, w)
    over_all = [in_group] + [over_outer(in_group, b) for b in range(1, outer)]
    arrive(len(jobs) - 1)
    attention(len(jobs) - 1, 1)
    attended[0], *over_all[1:] = step(attended[0], *over_all[1:])
    handoff = from_xor_order(over_all, z).reshape(n_inst, heads * wide)
    return (attended[0], handoff)


def solution(mesh):
    return jax.shard_map(
        shards,
        mesh=mesh,
        in_specs=(
            P("inst", "tp"),
            P("inst", "tp"),
            P("inst", "tp"),
            P("inst", "tp"),
            P("inst", "tp"),
            P("inst", "tp"),
            P("inst"),
        ),
        out_specs=(P("inst", "tp"), P(None, "tp")),
        check_vma=False,
    )
```

```python
import jax
import jax.numpy as jnp
from jax import lax
from jax.experimental import pallas as pl
from jax.experimental.pallas import tpu as pltpu
from jax.sharding import PartitionSpec as P

HEAD_SIZE = 128
QUERY_PER_GROUP = 4
VMEM_LIMIT = 32 * 1024 * 1024
COST = 1 << 10
INNER = 4


def dot(a, b):
    return jnp.dot(a, b, preferred_element_type=jnp.float32)


def first_kernel(low_ref, high_ref, w_ref, send_ref):
    t = jnp.concatenate([low_ref[...], high_ref[...]], axis=0)
    send_ref[...] = dot(t, w_ref[...]).astype(send_ref.dtype)


def later_kernel(low_ref, high_ref, w_ref, came_ref, send_ref, keep_ref):
    t = jnp.concatenate([low_ref[...], high_ref[...]], axis=0)
    out = dot(t, w_ref[...]) + came_ref[...].astype(jnp.float32)
    n = keep_ref.shape[0]
    keep_ref[...] = out[:n]
    send_ref[...] = out[n:].astype(send_ref.dtype)


def half_product(low, high, h, weight, came=None, tile=512):
    half, features, columns = low.shape[0] // 2, low.shape[1], weight.shape[1]
    tile = min(tile, columns)
    column = lambda i: (0, i)
    rows = pl.BlockSpec((half, features), lambda i: (h, 0))
    both = pl.BlockSpec((2 * half, tile), column)
    one = pl.BlockSpec((half, tile), column)
    shape = lambda n, dtype: jax.ShapeDtypeStruct((n, columns), dtype)
    first = came is None
    cost = 2 * features * columns * 2 if first else COST
    return pl.pallas_call(
        first_kernel if first else later_kernel,
        grid=(columns // tile,),
        in_specs=[rows, rows, pl.BlockSpec((features, tile), column)] + ([] if first else [both]),
        out_specs=both if first else [one, one],
        out_shape=shape(2 * half, jnp.bfloat16)
        if first
        else [shape(half, jnp.bfloat16), shape(half, jnp.float32)],
        compiler_params=pltpu.CompilerParams(vmem_limit_bytes=VMEM_LIMIT),
        cost_estimate=pl.CostEstimate(flops=0, bytes_accessed=cost, transcendentals=0),
        name="half_product",
    )(low, high, weight, *([] if first else [came]))


def beside_kernel(left_ref, right_ref, out_ref):
    columns = left_ref.shape[1]
    out_ref[:, :columns] = left_ref[...]
    out_ref[:, columns:] = right_ref[...]


def beside(left, right):
    rows, columns = left.shape
    return pl.pallas_call(
        beside_kernel,
        grid=(2,),
        in_specs=[pl.BlockSpec((rows // 2, columns), lambda i: (i, 0))] * 2,
        out_specs=pl.BlockSpec((rows // 2, 2 * columns), lambda i: (i, 0)),
        out_shape=jax.ShapeDtypeStruct((rows, 2 * columns), left.dtype),
        cost_estimate=pl.CostEstimate(flops=0, bytes_accessed=COST, transcendentals=0),
        name="beside",
    )(left, right)


def order_kernel(index_ref, *refs):
    out_ref = refs[-1]
    for m, ref in enumerate(refs[:-1]):
        out_ref[index_ref[0] ^ m] = ref[...]


def ordered(values, index):
    return pl.pallas_call(
        order_kernel,
        in_specs=[pl.BlockSpec(memory_space=pltpu.SMEM)]
        + [pl.BlockSpec(memory_space=pltpu.VMEM)] * len(values),
        out_specs=pl.BlockSpec(memory_space=pltpu.VMEM),
        out_shape=jax.ShapeDtypeStruct((len(values), *values[0].shape), values[0].dtype),
        cost_estimate=pl.CostEstimate(flops=0, bytes_accessed=COST, transcendentals=0),
        name="order",
    )(index[None].astype(jnp.int32), *values)


def attention_kernel(
    place_ref, qm_ref, qc_ref, kc_ref, vc_ref, km_ref, kt_ref, vm_ref, vt_ref, *rest
):
    o_ref, last_ref = rest[-2:]
    length, here, first = place_ref[0], place_ref[1], place_ref[2]
    rows, block = qm_ref.shape[0], km_ref.shape[0]
    half = block // 2
    total = lambda mine, came: (mine + came.astype(jnp.float32)).astype(jnp.bfloat16)
    factor = 1.4426950408889634 / HEAD_SIZE**0.5
    row = lax.broadcasted_iota(jnp.int32, (rows, 1), 0) + here * half
    col = lax.broadcasted_iota(jnp.int32, (rows, block), 1)
    col = jnp.where(col < half, col + first * half, col - first * half)
    allowed = (col <= row) & (col < length)
    contract = (((1,), (1,)), ((), ()))
    at = row == length - 1
    keys = total(km_ref[...], kt_ref[...])
    values = total(vm_ref[...], vt_ref[...])
    stack = 2
    allowed = jnp.concatenate([allowed] * stack, axis=0)
    for member in range(0, QUERY_PER_GROUP, stack):
        each = [
            slice((member + i) * HEAD_SIZE, (member + i + 1) * HEAD_SIZE) for i in range(stack)
        ]
        q = [qm_ref[:, cols] + qc_ref[:, cols].astype(jnp.float32) for cols in each]
        q = (jnp.concatenate(q, axis=0) * factor).astype(jnp.bfloat16)
        s1 = lax.dot_general(q, kc_ref[...], contract, preferred_element_type=jnp.float32)
        s2 = lax.dot_general(q, keys, contract, preferred_element_type=jnp.float32)
        s2 = jnp.where(allowed, s2, -jnp.inf)
        top = jnp.maximum(jnp.max(s1, axis=1, keepdims=True), jnp.max(s2, axis=1, keepdims=True))
        p1 = jnp.exp2(s1 - top)
        p2 = jnp.exp2(s2 - top)
        norm = jnp.sum(p1, axis=1, keepdims=True) + jnp.sum(p2, axis=1, keepdims=True)
        both = dot(p1.astype(jnp.bfloat16), vc_ref[...]) + dot(p2.astype(jnp.bfloat16), values)
        both = both / norm
        for i, cols in enumerate(each):
            out = both[i * rows : (i + 1) * rows]
            o_ref[:, cols] = out.astype(o_ref.dtype)
            last_ref[:, cols] = jnp.sum(jnp.where(at, out, 0.0), axis=0, keepdims=True).astype(
                last_ref.dtype
            )


def attend(place, q, which, k_cache, v_cache, kv, start, shape, buffer, limit):
    cols = q[0].shape[1]
    wide = QUERY_PER_GROUP * HEAD_SIZE
    cached, block = k_cache.shape[0], kv[0].shape[0]
    rows = block // 2
    heads = k_cache.shape[1] // HEAD_SIZE
    groups = cols // wide
    begin = start // wide
    column = lambda i, place: (0, begin + i)
    after = lambda i, place: (0, heads + begin + i)
    mine = lambda i, place: (which, i)
    buffers = [] if buffer is None else [buffer]
    return pl.pallas_call(
        attention_kernel,
        grid_spec=pltpu.PrefetchScalarGridSpec(
            num_scalar_prefetch=1,
            grid=(groups,),
            in_specs=[
                pl.BlockSpec((rows, wide), mine),
                pl.BlockSpec((rows, wide), mine),
                pl.BlockSpec((cached, HEAD_SIZE), column),
                pl.BlockSpec((cached, HEAD_SIZE), column),
                pl.BlockSpec((block, HEAD_SIZE), column),
                pl.BlockSpec((block, HEAD_SIZE), column),
                pl.BlockSpec((block, HEAD_SIZE), after),
                pl.BlockSpec((block, HEAD_SIZE), after),
            ]
            + [pl.BlockSpec(memory_space=pl.ANY)] * len(buffers),
            out_specs=[
                pl.BlockSpec((rows, wide), lambda i, place: (place[1], begin + i)),
                pl.BlockSpec((1, wide), lambda i, place: (0, i)),
            ],
        ),
        out_shape=[
            jax.ShapeDtypeStruct(shape, jnp.bfloat16),
            jax.ShapeDtypeStruct((1, cols), jnp.bfloat16),
        ],
        input_output_aliases={9: 0} if buffers else {},
        compiler_params=pltpu.CompilerParams(vmem_limit_bytes=limit),
        cost_estimate=pl.CostEstimate(flops=0, bytes_accessed=COST, transcendentals=0),
        name="attention",
    )(place, *q, k_cache, v_cache, *kv, *kv, *buffers)


def shards(tokens_in, w_query, w_key, w_value, stored_key_cache, stored_value_cache, prompt_len):
    n_inst, n_tp = lax.axis_size("inst"), lax.axis_size("tp")
    outer = n_inst // INNER
    me = lax.axis_index("inst")
    z, w = me // INNER, me % INNER
    x = lax.axis_index("tp")
    rows, local = tokens_in.shape
    half = rows // 2
    part = local // outer

    first = (prompt_len[0] - 1) // half

    def over_inst(value, bits):
        return lax.ppermute(value, "inst", [(i, i ^ bits) for i in range(n_inst)])

    def over_outer(value, bits):
        return over_inst(value, bits * INNER)

    def over_tp(value):
        return lax.ppermute(value, "tp", [(0, 1), (1, 0)])

    def swapped_if(flag, a, b, axis):
        return jnp.where(
            flag, jnp.concatenate([b, a], axis=axis), jnp.concatenate([a, b], axis=axis)
        )

    last_step = [None]

    def step(*values):
        if last_step[0] is not None:
            *values, _ = lax.optimization_barrier((*values, last_step[0]))
        last_step[0] = values[0]
        return values[0] if len(values) == 1 else values

    heads = w_key.shape[1] // HEAD_SIZE
    wide = QUERY_PER_GROUP * HEAD_SIZE
    pieces = 2 if heads % 2 == 0 else 1
    chunk = heads * wide // pieces
    fast = outer == 4 and n_tp == 2

    groups = [list(range(o * INNER, (o + 1) * INNER)) for o in range(outer)]

    def group_gather(value):
        return lax.all_gather(value, "inst", axis=0, tiled=True, axis_index_groups=groups)

    weights = {}

    weights["kv"] = group_gather(beside(w_key, w_value))

    def gather_queries():
        source = step(w_query) if fast else w_query
        for piece in range(pieces):
            part_of = source[:, piece * chunk : (piece + 1) * chunk]
            weights[piece] = group_gather(part_of)

    tokens = {}
    if fast:

        def cut(source, j, p):
            column = (((z % 2) ^ j) * n_tp + p) * part
            return jnp.concatenate(
                [
                    lax.dynamic_slice(source, (h * half, column), (half, part))
                    for h in (first, 1 - first)
                ],
                axis=0,
            )

        swap = {1: over_tp(step(cut(tokens_in, 1, 1 - x)))}
        source = step(tokens_in)
        swap[0] = over_tp(step(cut(source, 0, 1 - x)))
        mine = z // 2 == x
        held, came = {}, {}
        swap[1] = step(swap[1])
        own = cut(source, 1, x)
        send = {b: jnp.where(mine == (b < 2), own, swap[1]) for b in (1, 3)}
        send[1], send[3] = step(send[1], send[3])
        got = {b: over_outer(send[b], b) for b in (1, 3)}
        gather_queries()

        def tp_exchange(b):
            held[b] = step(got[b])
            came[b] = over_tp(held[b])

        tp_exchange(1)
        weights["kv"] = step(weights["kv"])
        tp_exchange(3)
        swap[0] = step(swap[0])
        own = cut(source, 0, x)
        send = {b: jnp.where(mine == (b < 2), own, swap[0]) for b in (2, 0)}
        send[2] = step(send[2])
        got[2], got[0] = over_outer(send[2], 2), send[0]

        def arrived(b):
            if b not in tokens:
                tokens[b] = (swapped_if(x == 1, held[b], step(came[b]), 1),)

    else:
        gather_queries()
        swapped = jnp.where(first == 1, jnp.roll(tokens_in, half, axis=0), tokens_in)
        own = swapped.reshape(rows, outer // n_tp, n_tp, part)
        parts = lax.all_to_all(own, "tp", 2, 1, tiled=True).reshape(rows, outer, part)
        come = jnp.stack(
            [
                over_outer(lax.dynamic_index_in_dim(parts, z ^ b, 1, keepdims=False), b)
                for b in range(outer)
            ]
        )
        both = lax.all_gather(come.reshape(-1, part), "tp", axis=1, tiled=True)
        both = both.reshape(outer, rows, -1)
        tokens.update({b: (both[b],) for b in range(outer)})

        def arrived(b):
            pass

    def rows_of(values, h):
        if h is None:
            return values
        return tuple(value[h * half : (h + 1) * half] for value in values)

    def times(values, weight):
        total, row = None, 0
        for value in values:
            one = dot(value, weight[row : row + value.shape[1]])
            total = one if total is None else total + one
            row += value.shape[1]
        return total

    def first_send(h, name):
        weight = weights[name] = step(weights[name])
        bits = range(1, outer, 2)
        if h is None:
            come = {}
            for b in bits:
                arrived(b)
                come[b] = over_outer(step(times(tokens[b], weight).astype(jnp.bfloat16)), 1)
            return come
        if fast:
            send = half_product(tokens[1][0], tokens[3][0], h, weight)
            return over_outer(step(send), 1)
        joined = [jnp.concatenate(same) for same in zip(*[rows_of(tokens[b], h) for b in bits])]
        come = over_outer(step(times(joined, weight).astype(jnp.bfloat16)), 1)
        return {b: (come, i) for i, b in enumerate(bits)}

    def later_sends(h, name, come):
        weight = weights[name]
        arrived(0)
        if fast and h is not None:
            send, keep = half_product(tokens[0][0], tokens[2][0], h, weight, step(come))
            send, keep = step(send, keep)
            return keep, over_outer(send, 2)
        if h is None:
            bits = list(come)
            come = dict(zip(bits, step(*[come[b] for b in bits])))
            arrived(2)
        else:
            whole = step(next(iter(come.values()))[0])
            come = {b: whole[i * half : (i + 1) * half] for b, (_, i) in come.items()}

        def total(b, arrival):
            return times(rows_of(tokens[b], h), weight) + arrival.astype(jnp.float32)

        if outer == 4:
            moved = over_outer(step(total(2, come[3]).astype(jnp.bfloat16)), 2)
            return total(0, step(come[1])), moved
        sums = {b: total(b, come[b + 1]) for b in range(0, outer, 2)}
        bit = 2
        while True:
            for b in sorted(sums):
                if b & bit:
                    moved = over_outer(step(sums.pop(b).astype(jnp.bfloat16)), bit)
                    if 2 * bit == outer:
                        return sums[0], moved
                    sums[b ^ bit] = sums[b ^ bit] + moved.astype(jnp.float32)
            bit *= 2

    jobs = [(None, "kv")] + ([(None, 0)] if pieces == 2 else [])
    jobs += [(0, pieces - 1), (1, pieces - 1)]
    opened, parts_of, lasts = {}, {}, []
    attended = [None]

    def start(n):
        opened[n] = first_send(*jobs[n])

    def advance(n):
        parts_of[n] = later_sends(*jobs[n], opened[n])

    def arrive(n):
        came_in, mine = step(parts_of[n][1], parts_of[n][0])
        parts_of[n] = (mine, came_in)

    def attention(n, h):
        own_half, piece = jobs[n]
        which = h if own_half is None else 0
        place = jnp.stack([prompt_len[0], h ^ first, first]).astype(jnp.int32)
        caches = (stored_key_cache, stored_value_cache)
        shape = (rows, heads * wide)
        limit = VMEM_LIMIT if n < len(jobs) - 1 else 56 * 1024 * 1024
        where = (piece * chunk, shape, attended[0], limit)
        attended[0], last = attend(place, parts_of[n], which, *caches, parts_of[0], *where)
        lasts.append(step(last))

    def from_xor_order(values, index):
        out = jnp.stack(values)
        shape = out.shape
        bits = len(values).bit_length() - 1
        for bit in range(bits):
            out = out.reshape(len(values) >> (bit + 1), 2, 1 << bit, *shape[1:])
            out = jnp.where((index >> bit) % 2 == 1, out[:, ::-1], out)
        return out.reshape(shape)

    start(0)
    if fast:
        tp_exchange(0)
        tp_exchange(2)
    start(1)
    advance(0)
    if pieces == 2:
        weights[1] = step(weights[1])
        start(2)
        advance(1)
        arrive(0)
        advance(2)
        start(3)
        arrive(1)
        attention(1, 0)
        attention(1, 1)
        advance(3)
        arrive(2)
        attention(2, 0)
        row = jnp.concatenate([lasts[0] + lasts[1], lasts[2]], axis=1)
    else:
        start(2)
        advance(1)
        arrive(0)
        advance(2)
        arrive(1)
        attention(1, 0)
        row = lasts[0]
    row = step(row)
    in_group = [row] + [over_inst(row, m) for m in range(1, INNER)]
    in_group = ordered(in_group, w)
    over_all = [in_group] + [over_outer(in_group, b) for b in range(1, outer)]
    arrive(len(jobs) - 1)
    attention(len(jobs) - 1, 1)
    attended[0], *over_all[1:] = step(attended[0], *over_all[1:])
    handoff = from_xor_order(over_all, z).reshape(n_inst, heads * wide)
    return (attended[0], handoff)


def solution(mesh):
    return jax.shard_map(
        shards,
        mesh=mesh,
        in_specs=(
            P("inst", "tp"),
            P("inst", "tp"),
            P("inst", "tp"),
            P("inst", "tp"),
            P("inst", "tp"),
            P("inst", "tp"),
            P("inst"),
        ),
        out_specs=(P("inst", "tp"), P(None, "tp")),
        check_vma=False,
    )
```

```python
import jax
import jax.numpy as jnp
from jax import lax
from jax.experimental import pallas as pl
from jax.experimental.pallas import tpu as pltpu
from jax.sharding import PartitionSpec as P

HEAD_SIZE = 128
QUERY_PER_GROUP = 4
VMEM_LIMIT = 32 * 1024 * 1024
COST = 1 << 10
INNER = 4


def dot(a, b):
    return jnp.dot(a, b, preferred_element_type=jnp.float32)


def first_kernel(low_ref, high_ref, w_ref, send_ref):
    t = jnp.concatenate([low_ref[...], high_ref[...]], axis=0)
    send_ref[...] = dot(t, w_ref[...]).astype(send_ref.dtype)


def later_kernel(low_ref, high_ref, w_ref, came_ref, send_ref, keep_ref):
    t = jnp.concatenate([low_ref[...], high_ref[...]], axis=0)
    out = dot(t, w_ref[...]) + came_ref[...].astype(jnp.float32)
    n = keep_ref.shape[0]
    keep_ref[...] = out[:n]
    send_ref[...] = out[n:].astype(send_ref.dtype)


def half_product(low, high, h, weight, came=None, tile=512):
    half, features, columns = low.shape[0] // 2, low.shape[1], weight.shape[1]
    tile = min(tile, columns)
    column = lambda i: (0, i)
    rows = pl.BlockSpec((half, features), lambda i: (h, 0))
    both = pl.BlockSpec((2 * half, tile), column)
    one = pl.BlockSpec((half, tile), column)
    shape = lambda n, dtype: jax.ShapeDtypeStruct((n, columns), dtype)
    first = came is None
    cost = 2 * features * columns * 2 if first else COST
    return pl.pallas_call(
        first_kernel if first else later_kernel,
        grid=(columns // tile,),
        in_specs=[rows, rows, pl.BlockSpec((features, tile), column)] + ([] if first else [both]),
        out_specs=both if first else [one, one],
        out_shape=shape(2 * half, jnp.bfloat16)
        if first
        else [shape(half, jnp.bfloat16), shape(half, jnp.float32)],
        compiler_params=pltpu.CompilerParams(vmem_limit_bytes=VMEM_LIMIT),
        cost_estimate=pl.CostEstimate(flops=0, bytes_accessed=cost, transcendentals=0),
        name="half_product",
    )(low, high, weight, *([] if first else [came]))


def order_kernel(index_ref, *refs):
    out_ref = refs[-1]
    for m, ref in enumerate(refs[:-1]):
        out_ref[index_ref[0] ^ m] = ref[...]


def ordered(values, index):
    return pl.pallas_call(
        order_kernel,
        in_specs=[pl.BlockSpec(memory_space=pltpu.SMEM)]
        + [pl.BlockSpec(memory_space=pltpu.VMEM)] * len(values),
        out_specs=pl.BlockSpec(memory_space=pltpu.VMEM),
        out_shape=jax.ShapeDtypeStruct((len(values), *values[0].shape), values[0].dtype),
        cost_estimate=pl.CostEstimate(flops=0, bytes_accessed=COST, transcendentals=0),
        name="order",
    )(index[None].astype(jnp.int32), *values)


def attention_kernel(
    place_ref, qm_ref, qc_ref, kc_ref, vc_ref, km_ref, kt_ref, vm_ref, vt_ref, *rest
):
    o_ref, last_ref = rest[-2:]
    length, here, first = place_ref[0], place_ref[1], place_ref[2]
    rows, block = qm_ref.shape[0], km_ref.shape[0]
    half = block // 2
    total = lambda mine, came: (mine + came.astype(jnp.float32)).astype(jnp.bfloat16)
    factor = 1.4426950408889634 / HEAD_SIZE**0.5
    row = lax.broadcasted_iota(jnp.int32, (rows, 1), 0) + here * half
    col = lax.broadcasted_iota(jnp.int32, (rows, block), 1)
    col = jnp.where(col < half, col + first * half, col - first * half)
    allowed = (col <= row) & (col < length)
    contract = (((1,), (1,)), ((), ()))
    at = row == length - 1
    keys = total(km_ref[...], kt_ref[...])
    values = total(vm_ref[...], vt_ref[...])
    stack = 2
    allowed = jnp.concatenate([allowed] * stack, axis=0)
    for member in range(0, QUERY_PER_GROUP, stack):
        each = [
            slice((member + i) * HEAD_SIZE, (member + i + 1) * HEAD_SIZE) for i in range(stack)
        ]
        q = [qm_ref[:, cols] + qc_ref[:, cols].astype(jnp.float32) for cols in each]
        q = (jnp.concatenate(q, axis=0) * factor).astype(jnp.bfloat16)
        s1 = lax.dot_general(q, kc_ref[...], contract, preferred_element_type=jnp.float32)
        s2 = lax.dot_general(q, keys, contract, preferred_element_type=jnp.float32)
        s2 = jnp.where(allowed, s2, -jnp.inf)
        top = jnp.maximum(jnp.max(s1, axis=1, keepdims=True), jnp.max(s2, axis=1, keepdims=True))
        p1 = jnp.exp2(s1 - top)
        p2 = jnp.exp2(s2 - top)
        norm = jnp.sum(p1, axis=1, keepdims=True) + jnp.sum(p2, axis=1, keepdims=True)
        both = dot(p1.astype(jnp.bfloat16), vc_ref[...]) + dot(p2.astype(jnp.bfloat16), values)
        both = both / norm
        for i, cols in enumerate(each):
            out = both[i * rows : (i + 1) * rows]
            o_ref[:, cols] = out.astype(o_ref.dtype)
            last_ref[:, cols] = jnp.sum(jnp.where(at, out, 0.0), axis=0, keepdims=True).astype(
                last_ref.dtype
            )


def attend(place, q, which, k_cache, v_cache, kv, start, shape, buffer, limit):
    cols = q[0].shape[1]
    wide = QUERY_PER_GROUP * HEAD_SIZE
    cached, block = k_cache.shape[0], kv[0].shape[0]
    rows = block // 2
    heads = k_cache.shape[1] // HEAD_SIZE
    groups = cols // wide
    begin = start // wide
    column = lambda i, place: (0, begin + i)
    after = lambda i, place: (0, heads + begin + i)
    mine = lambda i, place: (which, i)
    buffers = [] if buffer is None else [buffer]
    return pl.pallas_call(
        attention_kernel,
        grid_spec=pltpu.PrefetchScalarGridSpec(
            num_scalar_prefetch=1,
            grid=(groups,),
            in_specs=[
                pl.BlockSpec((rows, wide), mine),
                pl.BlockSpec((rows, wide), mine),
                pl.BlockSpec((cached, HEAD_SIZE), column),
                pl.BlockSpec((cached, HEAD_SIZE), column),
                pl.BlockSpec((block, HEAD_SIZE), column),
                pl.BlockSpec((block, HEAD_SIZE), column),
                pl.BlockSpec((block, HEAD_SIZE), after),
                pl.BlockSpec((block, HEAD_SIZE), after),
            ]
            + [pl.BlockSpec(memory_space=pl.ANY)] * len(buffers),
            out_specs=[
                pl.BlockSpec((rows, wide), lambda i, place: (place[1], begin + i)),
                pl.BlockSpec((1, wide), lambda i, place: (0, i)),
            ],
        ),
        out_shape=[
            jax.ShapeDtypeStruct(shape, jnp.bfloat16),
            jax.ShapeDtypeStruct((1, cols), jnp.bfloat16),
        ],
        input_output_aliases={9: 0} if buffers else {},
        compiler_params=pltpu.CompilerParams(vmem_limit_bytes=limit),
        cost_estimate=pl.CostEstimate(flops=0, bytes_accessed=COST, transcendentals=0),
        name="attention",
    )(place, *q, k_cache, v_cache, *kv, *kv, *buffers)


def shards(tokens_in, w_query, w_key, w_value, stored_key_cache, stored_value_cache, prompt_len):
    n_inst, n_tp = lax.axis_size("inst"), lax.axis_size("tp")
    outer = n_inst // INNER
    me = lax.axis_index("inst")
    z, w = me // INNER, me % INNER
    x = lax.axis_index("tp")
    rows, local = tokens_in.shape
    half = rows // 2
    part = local // outer

    first = (prompt_len[0] - 1) // half

    def over_inst(value, bits):
        return lax.ppermute(value, "inst", [(i, i ^ bits) for i in range(n_inst)])

    def over_outer(value, bits):
        return over_inst(value, bits * INNER)

    def over_tp(value):
        return lax.ppermute(value, "tp", [(0, 1), (1, 0)])

    def swapped_if(flag, a, b, axis):
        return jnp.where(
            flag, jnp.concatenate([b, a], axis=axis), jnp.concatenate([a, b], axis=axis)
        )

    last_step = [None]

    def step(*values):
        if last_step[0] is not None:
            *values, _ = lax.optimization_barrier((*values, last_step[0]))
        last_step[0] = values[0]
        return values[0] if len(values) == 1 else values

    heads = w_key.shape[1] // HEAD_SIZE
    wide = QUERY_PER_GROUP * HEAD_SIZE
    pieces = 2 if heads % 2 == 0 else 1
    chunk = heads * wide // pieces
    fast = outer == 4 and n_tp == 2

    groups = [list(range(o * INNER, (o + 1) * INNER)) for o in range(outer)]

    def group_gather(value):
        return lax.all_gather(value, "inst", axis=0, tiled=True, axis_index_groups=groups)

    weights = {}

    weights["kv"] = group_gather(jnp.concatenate([w_key, w_value], axis=1))

    q_parts = [w_query[:, piece * chunk : (piece + 1) * chunk] for piece in range(pieces)]

    def gather_queries():
        for piece, value in enumerate(q_parts):
            weights[piece] = group_gather(value)

    tokens = {}
    if fast:

        def cut(source, j, p):
            column = (((z % 2) ^ j) * n_tp + p) * part
            return jnp.concatenate(
                [
                    lax.dynamic_slice(source, (h * half, column), (half, part))
                    for h in (first, 1 - first)
                ],
                axis=0,
            )

        swap = {1: over_tp(step(cut(tokens_in, 1, 1 - x)))}
        source = step(tokens_in)
        swap[0] = over_tp(step(cut(source, 0, 1 - x)))
        mine = z // 2 == x
        held, came = {}, {}
        swap[1], *q_parts = step(swap[1], *q_parts)
        own = cut(source, 1, x)
        send = {b: jnp.where(mine == (b < 2), own, swap[1]) for b in (1, 3)}
        send[1], send[3] = step(send[1], send[3])
        got = {b: over_outer(send[b], b) for b in (1, 3)}
        gather_queries()

        def tp_exchange(b):
            held[b] = step(got[b])
            came[b] = over_tp(held[b])

        tp_exchange(1)
        weights["kv"] = step(weights["kv"])
        tp_exchange(3)
        swap[0] = step(swap[0])
        own = cut(source, 0, x)
        send = {b: jnp.where(mine == (b < 2), own, swap[0]) for b in (2, 0)}
        send[2] = step(send[2])
        got[2], got[0] = over_outer(send[2], 2), send[0]

        def arrived(b):
            if b not in tokens:
                tokens[b] = (swapped_if(x == 1, held[b], step(came[b]), 1),)

    else:
        gather_queries()
        swapped = jnp.where(first == 1, jnp.roll(tokens_in, half, axis=0), tokens_in)
        own = swapped.reshape(rows, outer // n_tp, n_tp, part)
        parts = lax.all_to_all(own, "tp", 2, 1, tiled=True).reshape(rows, outer, part)
        come = jnp.stack(
            [
                over_outer(lax.dynamic_index_in_dim(parts, z ^ b, 1, keepdims=False), b)
                for b in range(outer)
            ]
        )
        both = lax.all_gather(come.reshape(-1, part), "tp", axis=1, tiled=True)
        both = both.reshape(outer, rows, -1)
        tokens.update({b: (both[b],) for b in range(outer)})

        def arrived(b):
            pass

    def rows_of(values, h):
        if h is None:
            return values
        return tuple(value[h * half : (h + 1) * half] for value in values)

    def times(values, weight):
        total, row = None, 0
        for value in values:
            one = dot(value, weight[row : row + value.shape[1]])
            total = one if total is None else total + one
            row += value.shape[1]
        return total

    def first_send(h, name):
        weight = weights[name] = step(weights[name])
        bits = range(1, outer, 2)
        if h is None:
            come = {}
            for b in bits:
                arrived(b)
                come[b] = over_outer(step(times(tokens[b], weight).astype(jnp.bfloat16)), 1)
            return come
        if fast:
            send = half_product(tokens[1][0], tokens[3][0], h, weight)
            return over_outer(step(send), 1)
        joined = [jnp.concatenate(same) for same in zip(*[rows_of(tokens[b], h) for b in bits])]
        come = over_outer(step(times(joined, weight).astype(jnp.bfloat16)), 1)
        return {b: (come, i) for i, b in enumerate(bits)}

    def later_sends(h, name, come):
        weight = weights[name]
        arrived(0)
        if fast and h is not None:
            send, keep = half_product(tokens[0][0], tokens[2][0], h, weight, step(come))
            send, keep = step(send, keep)
            return keep, over_outer(send, 2)
        if h is None:
            bits = list(come)
            come = dict(zip(bits, step(*[come[b] for b in bits])))
            arrived(2)
        else:
            whole = step(next(iter(come.values()))[0])
            come = {b: whole[i * half : (i + 1) * half] for b, (_, i) in come.items()}

        def total(b, arrival):
            return times(rows_of(tokens[b], h), weight) + arrival.astype(jnp.float32)

        if outer == 4:
            moved = over_outer(step(total(2, come[3]).astype(jnp.bfloat16)), 2)
            return total(0, step(come[1])), moved
        sums = {b: total(b, come[b + 1]) for b in range(0, outer, 2)}
        bit = 2
        while True:
            for b in sorted(sums):
                if b & bit:
                    moved = over_outer(step(sums.pop(b).astype(jnp.bfloat16)), bit)
                    if 2 * bit == outer:
                        return sums[0], moved
                    sums[b ^ bit] = sums[b ^ bit] + moved.astype(jnp.float32)
            bit *= 2

    jobs = [(None, "kv")] + ([(None, 0)] if pieces == 2 else [])
    jobs += [(0, pieces - 1), (1, pieces - 1)]
    opened, parts_of, lasts = {}, {}, []
    attended = [None]

    def start(n):
        opened[n] = first_send(*jobs[n])

    def advance(n):
        parts_of[n] = later_sends(*jobs[n], opened[n])

    def arrive(n):
        came_in, mine = step(parts_of[n][1], parts_of[n][0])
        parts_of[n] = (mine, came_in)

    def attention(n, h):
        own_half, piece = jobs[n]
        which = h if own_half is None else 0
        place = jnp.stack([prompt_len[0], h ^ first, first]).astype(jnp.int32)
        caches = (stored_key_cache, stored_value_cache)
        shape = (rows, heads * wide)
        limit = VMEM_LIMIT if n < len(jobs) - 1 else 56 * 1024 * 1024
        where = (piece * chunk, shape, attended[0], limit)
        attended[0], last = attend(place, parts_of[n], which, *caches, parts_of[0], *where)
        lasts.append(step(last))

    def from_xor_order(values, index):
        out = jnp.stack(values)
        shape = out.shape
        bits = len(values).bit_length() - 1
        for bit in range(bits):
            out = out.reshape(len(values) >> (bit + 1), 2, 1 << bit, *shape[1:])
            out = jnp.where((index >> bit) % 2 == 1, out[:, ::-1], out)
        return out.reshape(shape)

    start(0)
    if fast:
        tp_exchange(0)
        tp_exchange(2)
    start(1)
    advance(0)
    if pieces == 2:
        weights[1] = step(weights[1])
        start(2)
        advance(1)
        arrive(0)
        advance(2)
        start(3)
        arrive(1)
        attention(1, 0)
        attention(1, 1)
        advance(3)
        arrive(2)
        attention(2, 0)
        row = jnp.concatenate([lasts[0] + lasts[1], lasts[2]], axis=1)
    else:
        start(2)
        advance(1)
        arrive(0)
        advance(2)
        arrive(1)
        attention(1, 0)
        row = lasts[0]
    row = step(row)
    in_group = [row] + [over_inst(row, m) for m in range(1, INNER)]
    in_group = ordered(in_group, w)
    over_all = [in_group] + [over_outer(in_group, b) for b in range(1, outer)]
    arrive(len(jobs) - 1)
    attention(len(jobs) - 1, 1)
    attended[0], *over_all[1:] = step(attended[0], *over_all[1:])
    handoff = from_xor_order(over_all, z).reshape(n_inst, heads * wide)
    return (attended[0], handoff)


def solution(mesh):
    return jax.shard_map(
        shards,
        mesh=mesh,
        in_specs=(
            P("inst", "tp"),
            P("inst", "tp"),
            P("inst", "tp"),
            P("inst", "tp"),
            P("inst", "tp"),
            P("inst", "tp"),
            P("inst"),
        ),
        out_specs=(P("inst", "tp"), P(None, "tp")),
        check_vma=False,
    )
```

```python
import jax
import jax.numpy as jnp
from jax import lax
from jax.experimental import pallas as pl
from jax.experimental.pallas import tpu as pltpu
from jax.sharding import PartitionSpec as P

HEAD_SIZE = 128
QUERY_PER_GROUP = 4
VMEM_LIMIT = 32 * 1024 * 1024
COST = 1 << 10
INNER = 4


def dot(a, b):
    return jnp.dot(a, b, preferred_element_type=jnp.float32)


def first_kernel(low_ref, high_ref, w_ref, send_ref):
    t = jnp.concatenate([low_ref[...], high_ref[...]], axis=0)
    send_ref[...] = dot(t, w_ref[...]).astype(send_ref.dtype)


def later_kernel(low_ref, high_ref, w_ref, came_ref, send_ref, keep_ref):
    t = jnp.concatenate([low_ref[...], high_ref[...]], axis=0)
    out = dot(t, w_ref[...]) + came_ref[...].astype(jnp.float32)
    n = keep_ref.shape[0]
    keep_ref[...] = out[:n]
    send_ref[...] = out[n:].astype(send_ref.dtype)


def half_product(low, high, h, weight, came=None, tile=512):
    half, features, columns = low.shape[0] // 2, low.shape[1], weight.shape[1]
    tile = min(tile, columns)
    column = lambda i: (0, i)
    rows = pl.BlockSpec((half, features), lambda i: (h, 0))
    both = pl.BlockSpec((2 * half, tile), column)
    one = pl.BlockSpec((half, tile), column)
    shape = lambda n, dtype: jax.ShapeDtypeStruct((n, columns), dtype)
    first = came is None
    cost = 2 * features * columns * 2 if first else COST
    return pl.pallas_call(
        first_kernel if first else later_kernel,
        grid=(columns // tile,),
        in_specs=[rows, rows, pl.BlockSpec((features, tile), column)] + ([] if first else [both]),
        out_specs=both if first else [one, one],
        out_shape=shape(2 * half, jnp.bfloat16)
        if first
        else [shape(half, jnp.bfloat16), shape(half, jnp.float32)],
        compiler_params=pltpu.CompilerParams(vmem_limit_bytes=VMEM_LIMIT),
        cost_estimate=pl.CostEstimate(flops=0, bytes_accessed=cost, transcendentals=0),
        name="half_product",
    )(low, high, weight, *([] if first else [came]))


def order_kernel(index_ref, *refs):
    out_ref = refs[-1]
    for m, ref in enumerate(refs[:-1]):
        out_ref[index_ref[0] ^ m] = ref[...]


def ordered(values, index):
    return pl.pallas_call(
        order_kernel,
        in_specs=[pl.BlockSpec(memory_space=pltpu.SMEM)]
        + [pl.BlockSpec(memory_space=pltpu.VMEM)] * len(values),
        out_specs=pl.BlockSpec(memory_space=pltpu.VMEM),
        out_shape=jax.ShapeDtypeStruct((len(values), *values[0].shape), values[0].dtype),
        cost_estimate=pl.CostEstimate(flops=0, bytes_accessed=COST, transcendentals=0),
        name="order",
    )(index[None].astype(jnp.int32), *values)


def attention_kernel(
    place_ref, qm_ref, qc_ref, kc_ref, vc_ref, km_ref, kt_ref, vm_ref, vt_ref, *rest
):
    o_ref, last_ref = rest[-2:]
    length, here, first = place_ref[0], place_ref[1], place_ref[2]
    rows, block = qm_ref.shape[0], km_ref.shape[0]
    half = block // 2
    total = lambda mine, came: (mine + came.astype(jnp.float32)).astype(jnp.bfloat16)
    factor = 1.4426950408889634 / HEAD_SIZE**0.5
    row = lax.broadcasted_iota(jnp.int32, (rows, 1), 0) + here * half
    col = lax.broadcasted_iota(jnp.int32, (rows, block), 1)
    col = jnp.where(col < half, col + first * half, col - first * half)
    allowed = (col <= row) & (col < length)
    contract = (((1,), (1,)), ((), ()))
    at = row == length - 1
    keys = total(km_ref[...], kt_ref[...])
    values = total(vm_ref[...], vt_ref[...])
    stack = 2
    allowed = jnp.concatenate([allowed] * stack, axis=0)
    for member in range(0, QUERY_PER_GROUP, stack):
        each = [
            slice((member + i) * HEAD_SIZE, (member + i + 1) * HEAD_SIZE) for i in range(stack)
        ]
        q = [qm_ref[:, cols] + qc_ref[:, cols].astype(jnp.float32) for cols in each]
        q = (jnp.concatenate(q, axis=0) * factor).astype(jnp.bfloat16)
        s1 = lax.dot_general(q, kc_ref[...], contract, preferred_element_type=jnp.float32)
        s2 = lax.dot_general(q, keys, contract, preferred_element_type=jnp.float32)
        s2 = jnp.where(allowed, s2, -jnp.inf)
        top = jnp.maximum(jnp.max(s1, axis=1, keepdims=True), jnp.max(s2, axis=1, keepdims=True))
        p1 = jnp.exp2(s1 - top)
        p2 = jnp.exp2(s2 - top)
        norm = jnp.sum(p1, axis=1, keepdims=True) + jnp.sum(p2, axis=1, keepdims=True)
        both = dot(p1.astype(jnp.bfloat16), vc_ref[...]) + dot(p2.astype(jnp.bfloat16), values)
        both = both / norm
        for i, cols in enumerate(each):
            out = both[i * rows : (i + 1) * rows]
            o_ref[:, cols] = out.astype(o_ref.dtype)
            last_ref[:, cols] = jnp.sum(jnp.where(at, out, 0.0), axis=0, keepdims=True).astype(
                last_ref.dtype
            )


def attend(place, q, which, k_cache, v_cache, kv, start, shape, buffer, limit):
    cols = q[0].shape[1]
    wide = QUERY_PER_GROUP * HEAD_SIZE
    cached, block = k_cache.shape[0], kv[0].shape[0]
    rows = block // 2
    heads = k_cache.shape[1] // HEAD_SIZE
    groups = cols // wide
    begin = start // wide
    column = lambda i, place: (0, begin + i)
    after = lambda i, place: (0, heads + begin + i)
    mine = lambda i, place: (which, i)
    buffers = [] if buffer is None else [buffer]
    return pl.pallas_call(
        attention_kernel,
        grid_spec=pltpu.PrefetchScalarGridSpec(
            num_scalar_prefetch=1,
            grid=(groups,),
            in_specs=[
                pl.BlockSpec((rows, wide), mine),
                pl.BlockSpec((rows, wide), mine),
                pl.BlockSpec((cached, HEAD_SIZE), column),
                pl.BlockSpec((cached, HEAD_SIZE), column),
                pl.BlockSpec((block, HEAD_SIZE), column),
                pl.BlockSpec((block, HEAD_SIZE), column),
                pl.BlockSpec((block, HEAD_SIZE), after),
                pl.BlockSpec((block, HEAD_SIZE), after),
            ]
            + [pl.BlockSpec(memory_space=pl.ANY)] * len(buffers),
            out_specs=[
                pl.BlockSpec((rows, wide), lambda i, place: (place[1], begin + i)),
                pl.BlockSpec((1, wide), lambda i, place: (0, i)),
            ],
        ),
        out_shape=[
            jax.ShapeDtypeStruct(shape, jnp.bfloat16),
            jax.ShapeDtypeStruct((1, cols), jnp.bfloat16),
        ],
        input_output_aliases={9: 0} if buffers else {},
        compiler_params=pltpu.CompilerParams(vmem_limit_bytes=limit),
        cost_estimate=pl.CostEstimate(flops=0, bytes_accessed=COST, transcendentals=0),
        name="attention",
    )(place, *q, k_cache, v_cache, *kv, *kv, *buffers)


def shards(tokens_in, w_query, w_key, w_value, stored_key_cache, stored_value_cache, prompt_len):
    n_inst, n_tp = lax.axis_size("inst"), lax.axis_size("tp")
    outer = n_inst // INNER
    me = lax.axis_index("inst")
    z, w = me // INNER, me % INNER
    x = lax.axis_index("tp")
    rows, local = tokens_in.shape
    half = rows // 2
    part = local // outer

    first = (prompt_len[0] - 1) // half

    def over_inst(value, bits):
        return lax.ppermute(value, "inst", [(i, i ^ bits) for i in range(n_inst)])

    def over_outer(value, bits):
        return over_inst(value, bits * INNER)

    def over_tp(value):
        return lax.ppermute(value, "tp", [(0, 1), (1, 0)])

    def swapped_if(flag, a, b, axis):
        return jnp.where(
            flag, jnp.concatenate([b, a], axis=axis), jnp.concatenate([a, b], axis=axis)
        )

    last_step = [None]

    def step(*values):
        if last_step[0] is not None:
            *values, _ = lax.optimization_barrier((*values, last_step[0]))
        last_step[0] = values[0]
        return values[0] if len(values) == 1 else values

    heads = w_key.shape[1] // HEAD_SIZE
    wide = QUERY_PER_GROUP * HEAD_SIZE
    pieces = 2 if heads % 2 == 0 else 1
    chunk = heads * wide // pieces
    fast = outer == 4 and n_tp == 2

    groups = [list(range(o * INNER, (o + 1) * INNER)) for o in range(outer)]

    def group_gather(value):
        return lax.all_gather(value, "inst", axis=0, tiled=True, axis_index_groups=groups)

    weights = {}

    weights["kv"] = group_gather(jnp.concatenate([w_key, w_value], axis=1))

    q_parts = [w_query[:, piece * chunk : (piece + 1) * chunk] for piece in range(pieces)]

    def gather_queries():
        for piece, value in enumerate(q_parts):
            weights[piece] = group_gather(value)

    tokens = {}
    between = []
    if fast:

        def cut(source, j, p):
            column = (((z % 2) ^ j) * n_tp + p) * part
            return jnp.concatenate(
                [
                    lax.dynamic_slice(source, (h * half, column), (half, part))
                    for h in (first, 1 - first)
                ],
                axis=0,
            )

        swap = {1: over_tp(step(cut(tokens_in, 1, 1 - x)))}
        source = step(tokens_in)
        swap[0] = over_tp(step(cut(source, 0, 1 - x)))
        mine = z // 2 == x
        held, came = {}, {}
        swap[1], *q_parts = step(swap[1], *q_parts)
        own = cut(source, 1, x)
        send = {b: jnp.where(mine == (b < 2), own, swap[1]) for b in (1, 3)}
        send[1], send[3] = step(send[1], send[3])
        got = {b: over_outer(send[b], b) for b in (1, 3)}
        gather_queries()

        def tp_exchange(b):
            held[b] = step(got[b])
            came[b] = over_tp(held[b])

        tp_exchange(1)
        swap[0] = step(swap[0])
        weights["kv"] = step(weights["kv"])
        tp_exchange(3)

        def even_sends():
            own = cut(source, 0, x)
            got[2] = over_outer(step(jnp.where(mine, step(swap[0]), own)), 2)
            got[0] = jnp.where(mine, own, swap[0])

        between.append(even_sends)

        def arrived(b):
            if b not in tokens:
                tokens[b] = (swapped_if(x == 1, held[b], step(came[b]), 1),)

    else:
        gather_queries()
        swapped = jnp.where(first == 1, jnp.roll(tokens_in, half, axis=0), tokens_in)
        own = swapped.reshape(rows, outer // n_tp, n_tp, part)
        parts = lax.all_to_all(own, "tp", 2, 1, tiled=True).reshape(rows, outer, part)
        come = jnp.stack(
            [
                over_outer(lax.dynamic_index_in_dim(parts, z ^ b, 1, keepdims=False), b)
                for b in range(outer)
            ]
        )
        both = lax.all_gather(come.reshape(-1, part), "tp", axis=1, tiled=True)
        both = both.reshape(outer, rows, -1)
        tokens.update({b: (both[b],) for b in range(outer)})

        def arrived(b):
            pass

    def rows_of(values, h):
        if h is None:
            return values
        return tuple(value[h * half : (h + 1) * half] for value in values)

    def times(values, weight):
        total, row = None, 0
        for value in values:
            one = dot(value, weight[row : row + value.shape[1]])
            total = one if total is None else total + one
            row += value.shape[1]
        return total

    def first_send(h, name):
        weight = weights[name] = step(weights[name])
        bits = range(1, outer, 2)
        if h is None:
            come = {}
            for b in bits:
                arrived(b)
                come[b] = over_outer(step(times(tokens[b], weight).astype(jnp.bfloat16)), 1)
                if between:
                    between.pop()()
            return come
        if fast:
            send = half_product(tokens[1][0], tokens[3][0], h, weight)
            return over_outer(step(send), 1)
        joined = [jnp.concatenate(same) for same in zip(*[rows_of(tokens[b], h) for b in bits])]
        come = over_outer(step(times(joined, weight).astype(jnp.bfloat16)), 1)
        return {b: (come, i) for i, b in enumerate(bits)}

    def later_sends(h, name, come):
        weight = weights[name]
        arrived(0)
        if fast and h is not None:
            send, keep = half_product(tokens[0][0], tokens[2][0], h, weight, step(come))
            send, keep = step(send, keep)
            return keep, over_outer(send, 2)
        if h is None:
            bits = list(come)
            come = dict(zip(bits, step(*[come[b] for b in bits])))
            arrived(2)
        else:
            whole = step(next(iter(come.values()))[0])
            come = {b: whole[i * half : (i + 1) * half] for b, (_, i) in come.items()}

        def total(b, arrival):
            return times(rows_of(tokens[b], h), weight) + arrival.astype(jnp.float32)

        if outer == 4:
            moved = over_outer(step(total(2, come[3]).astype(jnp.bfloat16)), 2)
            return total(0, step(come[1])), moved
        sums = {b: total(b, come[b + 1]) for b in range(0, outer, 2)}
        bit = 2
        while True:
            for b in sorted(sums):
                if b & bit:
                    moved = over_outer(step(sums.pop(b).astype(jnp.bfloat16)), bit)
                    if 2 * bit == outer:
                        return sums[0], moved
                    sums[b ^ bit] = sums[b ^ bit] + moved.astype(jnp.float32)
            bit *= 2

    jobs = [(None, "kv")] + ([(None, 0)] if pieces == 2 else [])
    jobs += [(0, pieces - 1), (1, pieces - 1)]
    opened, parts_of, lasts = {}, {}, []
    attended = [None]

    def start(n):
        opened[n] = first_send(*jobs[n])

    def advance(n):
        parts_of[n] = later_sends(*jobs[n], opened[n])

    def arrive(n):
        came_in, mine = step(parts_of[n][1], parts_of[n][0])
        parts_of[n] = (mine, came_in)

    def attention(n, h):
        own_half, piece = jobs[n]
        which = h if own_half is None else 0
        place = jnp.stack([prompt_len[0], h ^ first, first]).astype(jnp.int32)
        caches = (stored_key_cache, stored_value_cache)
        shape = (rows, heads * wide)
        limit = VMEM_LIMIT if n < len(jobs) - 1 else 56 * 1024 * 1024
        where = (piece * chunk, shape, attended[0], limit)
        attended[0], last = attend(place, parts_of[n], which, *caches, parts_of[0], *where)
        lasts.append(step(last))

    def from_xor_order(values, index):
        out = jnp.stack(values)
        shape = out.shape
        bits = len(values).bit_length() - 1
        for bit in range(bits):
            out = out.reshape(len(values) >> (bit + 1), 2, 1 << bit, *shape[1:])
            out = jnp.where((index >> bit) % 2 == 1, out[:, ::-1], out)
        return out.reshape(shape)

    start(0)
    if fast:
        tp_exchange(0)
        tp_exchange(2)
    start(1)
    advance(0)
    if pieces == 2:
        weights[1] = step(weights[1])
        start(2)
        advance(1)
        arrive(0)
        advance(2)
        start(3)
        arrive(1)
        attention(1, 0)
        attention(1, 1)
        advance(3)
        arrive(2)
        attention(2, 0)
        row = jnp.concatenate([lasts[0] + lasts[1], lasts[2]], axis=1)
    else:
        start(2)
        advance(1)
        arrive(0)
        advance(2)
        arrive(1)
        attention(1, 0)
        row = lasts[0]
    row = step(row)
    in_group = [row] + [over_inst(row, m) for m in range(1, INNER)]
    in_group = ordered(in_group, w)
    over_all = [in_group] + [over_outer(in_group, b) for b in range(1, outer)]
    arrive(len(jobs) - 1)
    attention(len(jobs) - 1, 1)
    attended[0], *over_all[1:] = step(attended[0], *over_all[1:])
    handoff = from_xor_order(over_all, z).reshape(n_inst, heads * wide)
    return (attended[0], handoff)


def solution(mesh):
    return jax.shard_map(
        shards,
        mesh=mesh,
        in_specs=(
            P("inst", "tp"),
            P("inst", "tp"),
            P("inst", "tp"),
            P("inst", "tp"),
            P("inst", "tp"),
            P("inst", "tp"),
            P("inst"),
        ),
        out_specs=(P("inst", "tp"), P(None, "tp")),
        check_vma=False,
    )
```
